32 devices in a mesh: dp: 4 (over z), head: 4 (over y, x), rep: 2 (over core).
Axes of the slice: x: 2, y: 2, z: 4, core: 2. Of those that a mesh axis runs over, the one named last changes fastest.
Arguments:
- embeddings: bfloat16 [2048, 8, 1152], P(('dp', 'head', 'rep')), may hold values from -6 to 6
- coverage: int32 [2048, 2], P(('dp', 'head', 'rep')), may hold values from 0 to 15, all different within a row; in each aligned block of 64 rows (0 to 63, 64 to 127, ...) at most 16 rows name the same one
- labels: int32 [2048, 2, 8], P(('dp', 'head', 'rep')), may hold values 0 or 1
- w_in: bfloat16 [16, 1152, 768], P(('dp', 'head')), may hold values from -0.1875 to 0.1875
- bias_in: bfloat16 [16, 768], P(('dp', 'head')), may hold values from -3 to 3
- w_out: bfloat16 [16, 768], P(('dp', 'head')), may hold values from -0.21875 to 0.21875
- first_w: float32 [16, 1152, 768], P(('dp', 'head'), 'rep'), may hold values from -0.5 to 0.5
- second_w: float32 [16, 1152, 768], P(('dp', 'head'), 'rep'), may hold values from 0.0001 to 0.001
- first_vec: float32 [16, 2, 768], P(('dp', 'head')), may hold values from -0.5 to 0.5
- second_vec: float32 [16, 2, 768], P(('dp', 'head')), may hold values from 0.0001 to 0.01
Outputs:
- new_w_in: bfloat16 [16, 1152, 768], P(('dp', 'head'))
- new_vec: bfloat16 [16, 2, 768], P(('dp', 'head'))
- new_first_w: float32 [16, 1152, 768], P(('dp', 'head'), 'rep')
- new_second_w: float32 [16, 1152, 768], P(('dp', 'head'), 'rep')
- new_first_vec: float32 [16, 2, 768], P(('dp', 'head'))
- new_second_vec: float32 [16, 2, 768], P(('dp', 'head'))
The draws below stay inside these ranges and needn't reach their ends.
Inputs may be any that keep to these rules, and one draw needn't show every extreme that they name: `coverage`: each block names 2 different heads. Among the 64 blocks of one device (aligned blocks of rows, in order) no head is named more than 16 times, a bound that some block reaches; every head is named by some block.
All inputs are finite; a program needn't handle non-finite values. No bound on the sum of `labels` on one device may be relied on, other than what follows from the above.
Results may differ from the reference program's by a relative error of at most 0.00155.
Values may be sent and summed in bfloat16 or wider, within the bound.
No kernel may reach another device: no remote copies, remote signals or barrier semaphores. Data moves between devices by JAX's collectives and lax.ppermute only.
A program may use at most 128 MiB of HBM per device.

```python
import math
import jax
import jax.numpy as jnp
import numpy as np
from jax import lax

D = 1152
HID = 768
ROWS_BLK = 8
TOP = 2
BLK_DEV = 64
HEADS = 16
MOST = 16
BLOCKS = 2048
N_DP = 4
N_HEAD = 4
N_REP = 2


def set_ends(array, stream_key, low, largest):
    longest = array.shape.index(max(array.shape))
    spots = []
    for shift in (0, 1):
        where = [jax.random.randint(jax.random.fold_in(stream_key, axis), (), 0, length) for axis, length in enumerate(array.shape)]
        where[longest] = (where[longest] + shift) % array.shape[longest]
        spots.append(tuple(where))
    return array.at[spots[0]].set(low).at[spots[1]].set(largest)


def steps_of(own_key, dims, shards, least, largest):
    loudness, own = 1.0, jax.random.fold_in(own_key, 6)
    for axis_at, shards_of in shards:
        heights = jnp.exp(jax.random.uniform(jax.random.fold_in(own, axis_at), (shards_of,), jnp.float32, least / len(shards), largest / len(shards)))
        loudness = loudness * jnp.repeat(heights, dims[axis_at] // shards_of).reshape([-1 if axis == axis_at else 1 for axis in range(len(dims))])
    return loudness


def shared_out(rng, own, number, rows, number_of, top, most, slope):
    order = jax.random.permutation(rng, number_of)
    heavy_load, common = portions_of(number_of, rows * top, most, slope, True), portions_of(number_of, rows * top, most, slope, False)
    places = jnp.arange(number_of)

    def named(sizes, turn):
        used = int((sizes > 0).sum())
        fixed = max(1, used // 4)
        shifted = fixed + (places - fixed + turn * (used - fixed)) % max(1, number_of - fixed)
        return jnp.zeros((number_of,), jnp.int32).at[order[jnp.where(places < fixed, places, shifted)]].set(jnp.asarray(sizes, jnp.int32))

    sizes = jnp.where(number % 4 == 0, named(heavy_load, number // 4), named(common, number - number // 4 - 1))
    mixed = jax.random.permutation(jax.random.fold_in(own, 3), number_of)
    donor, receiver = mixed[0:number_of // 2 * 2:2], mixed[1:number_of // 2 * 2:2]
    room = jnp.minimum(sizes[donor] - 1, most - sizes[receiver]) // 2
    room = jnp.where((donor == order[0]) | (receiver == order[0]) | (sizes[receiver] == 0), 0, jnp.maximum(room, 0))
    shifted = jax.random.randint(jax.random.fold_in(own, 4), (number_of // 2,), 0, 1 << 20) % (room + 1)
    sizes = sizes.at[donor].add(-shifted).at[receiver].add(shifted)
    members = jnp.searchsorted(jnp.cumsum(sizes), jnp.arange(rows * top), side="right").astype(jnp.int32)
    listing = members.reshape(top, rows).T
    listing = listing[jax.random.permutation(jax.random.fold_in(own, 1), rows)]
    turn = jax.random.randint(jax.random.fold_in(own, 2), (rows, 1), 0, top)
    return jnp.take_along_axis(listing, (jnp.arange(top)[None, :] + turn) % top, axis=1)


def portions_of(number_of, total, reach, skew, full):
    weights = [(1 << 20) // math.isqrt(standing ** skew) + 1 for standing in range(1, number_of + 1)]
    largest = reach if full else min(reach, max(-(-total // number_of), total * weights[0] // sum(weights)))
    least = 1 if total - largest >= number_of - 1 else 0
    given, rest = [largest] + [least] * (number_of - 1), total - largest - least * (number_of - 1)
    while rest > 0:
        movable = [i for i in range(1, number_of) if given[i] < largest] or [i for i in range(1, number_of) if given[i] < reach]
        whole, budget = sum([weights[i] for i in movable]), rest
        for i in movable:
            extra = min(reach - given[i], max(1, budget * weights[i] // whole), rest)
            given[i] = given[i] + extra
            rest = rest - extra
    return np.array(given)


def scatter_about(key, shape, spread, bound, split=(), kind=jnp.bfloat16):
    values = spread * jax.random.normal(key, shape, jnp.float32)
    if split:
        values = values * steps_of(key, shape, split, -0.22, 0.18)
    return jnp.clip(values, -bound, bound).astype(kind)


def setup_inputs(seed: int = 0) -> dict:
    key_of = jax.random.split(jax.random.key(seed), 11)
    embeddings = scatter_about(key_of[0], (BLOCKS, ROWS_BLK, D), 1.0, 6.0, ((0, 32),))
    coverage_keys = jax.random.split(jax.random.fold_in(key_of[1], 1), BLOCKS // BLK_DEV)
    coverage_turns = jax.random.permutation(jax.random.fold_in(key_of[1], 3), BLOCKS // BLK_DEV)
    coverage = jax.vmap(lambda own, number: shared_out(jax.random.fold_in(key_of[1], 2), own, number, BLK_DEV, HEADS, TOP, MOST, 2))(coverage_keys, coverage_turns).reshape((BLOCKS, TOP))
    labels = set_ends((jax.random.randint(key_of[2], (BLOCKS, TOP, ROWS_BLK), 0, 2) < 1).astype(jnp.int32), jax.random.fold_in(key_of[2], 1), 0, 1)
    w_in = scatter_about(key_of[3], (HEADS, D, HID), D ** -0.5, 0.1875, ((0, 16),))
    bias_in = scatter_about(key_of[4], (HEADS, HID), 0.5, 3.0, ((0, 16),))
    w_out = scatter_about(key_of[5], (HEADS, HID), HID ** -0.5, 0.21875, ((0, 16),))
    first_w = scatter_about(key_of[6], (HEADS, D, HID), 0.1, 0.5, ((0, 16), (1, 2)), jnp.float32)
    second_w = jnp.clip(jnp.exp(math.log(0.001) - 2.3025852 * jax.random.uniform(key_of[7], (HEADS, D, HID), jnp.float32) ** steps_of(key_of[7], (HEADS, D, HID), ((0, 16), (1, 2)), -0.2, 0.2)), 0.0001, 0.001)
    first_vec = scatter_about(key_of[8], (HEADS, 2, HID), 0.1, 0.5, ((0, 16),), jnp.float32)
    second_vec = jnp.clip(jnp.exp(math.log(0.01) - 4.6051702 * jax.random.uniform(key_of[9], (HEADS, 2, HID), jnp.float32) ** steps_of(key_of[9], (HEADS, 2, HID), ((0, 16),), -0.2, 0.2)), 0.0001, 0.01)
    return {"embeddings": embeddings, "coverage": coverage, "labels": labels, "w_in": w_in, "bias_in": bias_in, "w_out": w_out, "first_w": first_w, "second_w": second_w, "first_vec": first_vec, "second_vec": second_vec}


beta_one = 0.9
beta_two = 0.999
learn_rate = 0.001
epsilon = 1e-08

def reference(embeddings, coverage, labels, w_in, bias_in, w_out, first_w, second_w, first_vec, second_vec):
    entry_bound = N_DP * N_HEAD * N_REP * MOST
    heads_flat = coverage.reshape(-1)
    targets_all = labels.reshape(-1, ROWS_BLK)

    def one_head(head_id):
        entry_order = jnp.argsort((heads_flat != head_id).astype(jnp.int32), stable=True)[:entry_bound].astype(jnp.int32)
        usable = heads_flat[entry_order] == head_id
        block_ids = (entry_order // TOP).astype(jnp.int32)
        row_data = embeddings[block_ids].reshape(entry_bound * ROWS_BLK, D)
        target = targets_all[entry_order].reshape(-1).astype(jnp.float32)
        row_keep = jnp.repeat(usable, ROWS_BLK)
        out_weight = w_out[head_id].astype(jnp.float32)
        pre_act = jnp.dot(row_data, w_in[head_id], preferred_element_type=jnp.float32) + bias_in[head_id].astype(jnp.float32)
        sig_pre = jax.nn.sigmoid(pre_act)
        hidden = pre_act * sig_pre
        logits = lax.optimization_barrier(jnp.sum(hidden * out_weight[None, :], axis=1))
        residual = jnp.where(row_keep, jax.nn.sigmoid(logits) - target, jnp.zeros_like(logits))
        grad_pre = residual[:, None] * out_weight[None, :] * sig_pre * (1.0 + pre_act * (1.0 - sig_pre))
        grad_low = grad_pre.astype(jnp.bfloat16)
        grad_w = lax.dot_general(row_data, grad_low, (((0,), (0,)), ((), ())), preferred_element_type=jnp.float32)
        grad_vec = jnp.stack([lax.optimization_barrier(jnp.sum(grad_pre, axis=0)), lax.optimization_barrier(jnp.sum(residual[:, None] * hidden, axis=0))])
        return (grad_w, grad_vec)
    grad_w, grad_vec = lax.map(one_head, jnp.arange(HEADS, dtype=jnp.int32))
    new_first_w = beta_one * first_w + (1.0 - beta_one) * grad_w
    new_second_w = beta_two * second_w + (1.0 - beta_two) * grad_w * grad_w
    new_w_in = (w_in.astype(jnp.float32) - learn_rate * new_first_w / (jnp.sqrt(new_second_w) + epsilon)).astype(jnp.bfloat16)
    vector = jnp.stack([bias_in, w_out], axis=1).astype(jnp.float32)
    new_first_vec = beta_one * first_vec + (1.0 - beta_one) * grad_vec
    new_second_vec = beta_two * second_vec + (1.0 - beta_two) * grad_vec * grad_vec
    new_vec = (vector - learn_rate * new_first_vec / (jnp.sqrt(new_second_vec) + epsilon)).astype(jnp.bfloat16)
    return (new_w_in, new_vec, new_first_w, new_second_w, new_first_vec, new_second_vec)
```

```python
import jax
import jax.numpy as jnp
from jax import lax
from jax.sharding import PartitionSpec as P

beta_one = 0.9
beta_two = 0.999
learn_rate = 0.001
epsilon = 1e-08
swap = [(0, 1), (1, 0)]


def per_device(
    embeddings, coverage, labels, w_in, bias_in, w_out, first_w, second_w, first_vec, second_vec
):
    dp_count = lax.axis_size("dp")
    head_count = lax.axis_size("head")
    owners = dp_count * head_count
    block_count, rows_block, feature = embeddings.shape
    per_block = coverage.shape[1]
    slot_count = 2 * block_count * per_block // owners
    entries = block_count * per_block
    heads_flat = coverage.reshape(entries)
    onehot = (heads_flat[:, None] == jnp.arange(owners, dtype=jnp.int32)[None, :]).astype(jnp.int32)
    slot_rank = jnp.sum((jnp.cumsum(onehot, axis=0) - 1) * onehot, axis=1)
    target_slot = heads_flat * slot_count + slot_rank
    picker = jnp.arange(owners * slot_count, dtype=jnp.int32)[:, None] == target_slot[None, :]
    block_pick = jnp.sum(
        picker.reshape(owners * slot_count, block_count, per_block).astype(jnp.int32), axis=2
    ).astype(jnp.bfloat16)
    send_rows = jnp.dot(
        block_pick,
        embeddings.reshape(block_count, rows_block * feature),
        preferred_element_type=jnp.float32,
    ).astype(jnp.bfloat16)
    label_marks = (labels.reshape(entries, rows_block) + 1).astype(jnp.float32)
    send_marks = jnp.dot(
        picker.astype(jnp.float32), label_marks, precision=lax.Precision.HIGHEST
    ).astype(jnp.bfloat16)
    direct_rows = send_rows.reshape(owners, slot_count, rows_block, feature)
    direct_marks = send_marks.reshape(owners, slot_count, rows_block)
    got_rows, got_marks = (
        lax.all_to_all(direct_rows, ("dp", "head"), split_axis=0, concat_axis=0, tiled=True),
        lax.all_to_all(direct_marks, ("dp", "head"), split_axis=0, concat_axis=0, tiled=True),
    )
    row_data = got_rows.reshape(-1, feature)
    marks_all = got_marks.reshape(-1).astype(jnp.float32)
    usable = marks_all > 0.5
    target = marks_all - 1.0
    out_weight = w_out[0].astype(jnp.float32)
    pre_act = (
        jnp.dot(row_data, w_in[0], preferred_element_type=jnp.float32)
        + bias_in[0].astype(jnp.float32)[None, :]
    )
    sig_pre = jax.nn.sigmoid(pre_act)
    hidden = pre_act * sig_pre
    logits = jnp.sum(hidden * out_weight[None, :], axis=1)
    residual = jnp.where(usable, jax.nn.sigmoid(logits) - target, jnp.zeros_like(logits))
    grad_pre = residual[:, None] * out_weight[None, :] * sig_pre * (1.0 + pre_act * (1.0 - sig_pre))
    grad_low = grad_pre.astype(jnp.bfloat16)
    vec_part = jnp.stack([jnp.sum(grad_pre, axis=0), jnp.sum(residual[:, None] * hidden, axis=0)])
    half_rows = feature // lax.axis_size("rep")
    rep_at = lax.axis_index("rep")
    first_row = rep_at * half_rows
    grad_part = lax.dot_general(
        row_data, grad_low, (((0,), (0,)), ((), ())), preferred_element_type=jnp.float32
    ).reshape(2, half_rows, -1)
    kept = jnp.where(rep_at == 0, grad_part[0], grad_part[1])
    given = jnp.where(rep_at == 0, grad_part[1], grad_part[0])
    grad_w = kept + lax.ppermute(given, "rep", swap)
    grad_vec = vec_part + lax.ppermute(vec_part, "rep", swap)
    new_first_w = beta_one * first_w[0] + (1.0 - beta_one) * grad_w
    new_second_w = beta_two * second_w[0] + (1.0 - beta_two) * grad_w * grad_w
    old_rows = lax.dynamic_slice_in_dim(w_in[0], first_row, half_rows, 0).astype(jnp.float32)
    new_half = (old_rows - learn_rate * new_first_w / (jnp.sqrt(new_second_w) + epsilon)).astype(
        jnp.bfloat16
    )
    other_half = lax.ppermute(new_half, "rep", swap)
    new_w_in = jnp.where(
        rep_at == 0,
        jnp.concatenate([new_half, other_half]),
        jnp.concatenate([other_half, new_half]),
    )
    vector = jnp.stack([bias_in[0], w_out[0]]).astype(jnp.float32)
    new_first_vec = beta_one * first_vec[0] + (1.0 - beta_one) * grad_vec
    new_second_vec = beta_two * second_vec[0] + (1.0 - beta_two) * grad_vec * grad_vec
    new_vec = (vector - learn_rate * new_first_vec / (jnp.sqrt(new_second_vec) + epsilon)).astype(
        jnp.bfloat16
    )
    return (
        new_w_in[None],
        new_vec[None],
        new_first_w[None],
        new_second_w[None],
        new_first_vec[None],
        new_second_vec[None],
    )


def solution(mesh):
    placed = (
        P(("dp", "head", "rep"), None, None),
        P(("dp", "head", "rep"), None),
        P(("dp", "head", "rep"), None, None),
        P(("dp", "head"), None, None),
        P(("dp", "head"), None),
        P(("dp", "head"), None),
        P(("dp", "head"), "rep", None),
        P(("dp", "head"), "rep", None),
        P(("dp", "head"), None, None),
        P(("dp", "head"), None, None),
    )
    return jax.shard_map(
        per_device,
        mesh=mesh,
        in_specs=placed,
        out_specs=(
            P(("dp", "head"), None, None),
            P(("dp", "head"), None, None),
            P(("dp", "head"), "rep", None),
            P(("dp", "head"), "rep", None),
            P(("dp", "head"), None, None),
            P(("dp", "head"), None, None),
        ),
        check_vma=False,
    )
```

```python
import functools

import jax
import jax.numpy as jnp
from jax import lax
from jax.experimental import pallas as pl
from jax.experimental.pallas import tpu as pltpu
from jax.sharding import PartitionSpec as P

beta_one = 0.9
beta_two = 0.999
learn_rate = 0.001
epsilon = 1e-08
swap = [(0, 1), (1, 0)]
MIB = 1024 * 1024
ANY = pl.BlockSpec(memory_space=pl.ANY)
VMEM = pl.BlockSpec(memory_space=pltpu.VMEM)
SMEM = pl.BlockSpec(memory_space=pltpu.SMEM)
f32 = jnp.float32
bf16 = jnp.bfloat16


def params(mib):
    return pltpu.CompilerParams(vmem_limit_bytes=mib * MIB)


def sds(shape, dtype):
    return jax.ShapeDtypeStruct(shape, dtype)


def half_sigmoid(x):
    return 0.5 * jnp.tanh(0.5 * x) + 0.5


def marks_kernel(owners, unit, cov_ref, lab_ref, out_ref):
    per_block, blocks = cov_ref.shape
    rows_block = lab_ref.shape[1]
    rows = blocks * rows_block
    cov = cov_ref[...]
    heads_at = lax.broadcasted_iota(jnp.int32, (owners, blocks), 0)
    named = (cov[0:1] == heads_at).astype(f32)
    for t in range(1, per_block):
        named = named + (cov[t : t + 1] == heads_at).astype(f32)
    block_of = lax.broadcasted_iota(jnp.int32, (blocks, rows), 1) // rows_block
    block_at = lax.broadcasted_iota(jnp.int32, (blocks, rows), 0)
    same = (block_of == block_at).astype(bf16)
    before = (block_at < block_of).astype(bf16)
    rank = jnp.dot(named.astype(bf16), before, preferred_element_type=f32)
    cov_rows = jnp.dot(cov.astype(f32).astype(bf16), same, preferred_element_type=f32)
    row_in = lax.broadcasted_iota(jnp.int32, (rows_block, rows), 1) % rows_block
    row_at = lax.broadcasted_iota(jnp.int32, (rows_block, rows), 0)
    head_rows = lax.broadcasted_iota(jnp.int32, (owners, rows), 0).astype(f32)
    for t in range(per_block):
        mine = cov_rows[t : t + 1]
        own_rank = jnp.sum(jnp.where(mine == head_rows, rank, 0.0), axis=0, keepdims=True)
        out_ref[t : t + 1, :] = (
            mine * unit + own_rank * rows_block + row_in[0:1].astype(f32)
        )
        spread = jnp.dot(lab_ref[t].astype(f32).astype(bf16), same, preferred_element_type=f32)
        out_ref[per_block + t : per_block + t + 1, :] = 1.0 + jnp.sum(
            jnp.where(row_in == row_at, spread, 0.0), axis=0, keepdims=True
        )


def make_marks(coverage, labels, owners, unit):
    blocks, per_block = coverage.shape
    rows = blocks * labels.shape[2]
    return pl.pallas_call(
        functools.partial(marks_kernel, owners, unit),
        out_shape=sds((2 * per_block, rows), f32),
        in_specs=[VMEM, VMEM],
        out_specs=VMEM,
        compiler_params=params(8),
        name="marks",
    )(coverage.T, labels.transpose(1, 2, 0))


def pick_rows(marks, shard, first_code, unit, per_block):
    rows = marks.shape[1]
    slot = lax.broadcasted_iota(jnp.int32, (unit, rows), 0).astype(f32) + first_code
    chosen = marks[0:1] == slot
    for t in range(1, per_block):
        chosen = chosen | (marks[t : t + 1] == slot)
    return jnp.dot(
        jnp.where(chosen, 1.0, 0.0).astype(bf16), shard, preferred_element_type=f32
    ).astype(bf16)


def pick_kernel(plan, unit, per_block, n_shards, n_marks, at_ref, *refs):
    shards, refs = refs[:n_shards], refs[n_shards:]
    marks, refs = refs[:n_marks], refs[n_marks:]
    n_heads = len(plan[0][2])
    n_out = len(plan) * n_heads
    outs, (held, sems) = refs[:-2], refs[-2:]
    loads = []
    for i in range(n_shards):
        load = pltpu.make_async_copy(shards[i], held.at[i], sems.at[i])
        load.start()
        loads.append(load)
    done = set()
    for shard_at, mark_at, places in plan:
        if shard_at not in done:
            loads[shard_at].wait()
            done.add(shard_at)
        for slot, (out_at, row_at) in enumerate(places):
            first_code = at_ref[mark_at * n_heads + slot].astype(f32)
            outs[out_at][row_at : row_at + unit, :] = pick_rows(
                marks[mark_at][...], held[shard_at], first_code, unit, per_block
            )


def pick_either_kernel(unit, per_block, n_heads, at_ref, left_ref, right_ref, marks_ref, *refs):
    outs, (held, sem) = refs[:-2], refs[-2:]
    use_left = at_ref[n_heads] > 0

    @pl.when(use_left)
    def _():
        load = pltpu.make_async_copy(left_ref, held, sem)
        load.start()
        load.wait()

    @pl.when(jnp.logical_not(use_left))
    def _():
        load = pltpu.make_async_copy(right_ref, held, sem)
        load.start()
        load.wait()

    for slot in range(n_heads):
        outs[slot][...] = pick_rows(
            marks_ref[...], held[...], at_ref[slot].astype(f32), unit, per_block
        )


def learn_kernel(
    unit, per_block, n_units, n_parts, last, with_total, half_rows,
    at_ref, *refs
):
    parts, refs = refs[:n_parts], refs[n_parts:]
    marks_ref, w_ref, bias_ref, out_ref, refs = refs[0], refs[1], refs[2], refs[3], refs[4:]
    if with_total:
        total_ref, vec_ref, refs = refs[0], refs[1], refs[2:]
    if last:
        kept_ref, given_ref, refs = refs[0], refs[1], refs[2:]
    else:
        new_total_ref, new_vec_ref, refs = refs[0], refs[1], refs[2:]
    rows_ref, low_ref, target_ref, sems = refs
    rows_all, feature = rows_ref.shape
    loads = []
    at = 0
    for i in range(n_parts):
        size = parts[i].shape[0]
        load = pltpu.make_async_copy(parts[i], rows_ref.at[pl.ds(at, size)], sems.at[i])
        load.start()
        loads.append(load)
        at += size
    first_code = at_ref[0].astype(f32)
    for u in range(n_units):
        source = at_ref[1 + u]
        real = at_ref[1 + n_units + u].astype(f32)
        marks = marks_ref[source]
        slot = lax.broadcasted_iota(jnp.int32, (unit, marks.shape[1]), 0).astype(f32) + first_code
        found = jnp.zeros(slot.shape, f32)
        for t in range(per_block):
            found = found + jnp.where(
                marks[t : t + 1] == slot, marks[per_block + t : per_block + t + 1], 0.0
            )
        target_ref[u * unit : (u + 1) * unit, :] = jnp.sum(found, axis=1, keepdims=True) * real
    for load in loads:
        load.wait()
    bias = bias_ref[...].astype(f32)
    out_weight = out_ref[...].astype(f32)
    step = 2 * unit
    hid = w_ref.shape[1]

    def forward(i, carry):
        span = pl.ds(pl.multiple_of(i * step, step), step)
        pre = jnp.dot(rows_ref[span, :], w_ref[...], preferred_element_type=f32) + bias
        gate = half_sigmoid(pre)
        hidden = pre * gate
        logit = jnp.sum(hidden * out_weight, axis=1, keepdims=True)
        mark = target_ref[span, :]
        residual = jnp.where(mark > 0.5, half_sigmoid(logit) - (mark - 1.0), 0.0)
        grad_pre = residual * out_weight * gate * (1.0 + pre * (1.0 - gate))
        low_ref[span, :] = grad_pre.astype(bf16)
        return (
            carry[0] + jnp.sum(grad_pre, axis=0, keepdims=True),
            carry[1] + jnp.sum(residual * hidden, axis=0, keepdims=True),
        )

    if with_total:
        start = (vec_ref[0:1, :], vec_ref[1:2, :])
    else:
        start = (jnp.zeros((1, hid), f32), jnp.zeros((1, hid), f32))
    grad_bias, grad_out = lax.fori_loop(0, rows_all // step, forward, start)

    def product(first, size):
        piece = lax.dot_general(
            rows_ref[:, first : first + size],
            low_ref[...],
            (((0,), (0,)), ((), ())),
            preferred_element_type=f32,
        )
        if with_total:
            piece = piece + total_ref[first : first + size, :]
        return piece

    tile = 128 * max(n for n in range(1, 5) if feature % (128 * n) == 0)
    if not last:
        for first in range(0, feature, tile):
            new_total_ref[first : first + tile, :] = product(first, tile)
        new_vec_ref[0:1, :] = grad_bias
        new_vec_ref[1:2, :] = grad_out
        return
    rep = at_ref[1 + 2 * n_units]
    given_ref[half_rows : half_rows + 8, :] = jnp.zeros((8, hid), f32)
    kept_ref[half_rows : half_rows + 8, :] = jnp.zeros((8, hid), f32)
    for ref in (given_ref, kept_ref):
        ref[half_rows : half_rows + 1, :] = grad_bias
        ref[half_rows + 1 : half_rows + 2, :] = grad_out
    for first in range(0, feature, tile):
        piece = product(first, tile)
        cut = min(max(half_rows - first, 0), tile)

        @pl.when(rep == 0)
        def _():
            if cut > 0:
                kept_ref[first : first + cut, :] = piece[:cut]
            if cut < tile:
                given_ref[first + cut - half_rows : first + tile - half_rows, :] = piece[cut:]

        @pl.when(rep != 0)
        def _():
            if cut > 0:
                given_ref[first : first + cut, :] = piece[:cut]
            if cut < tile:
                kept_ref[first + cut - half_rows : first + tile - half_rows, :] = piece[cut:]


def learn(unit, per_block, n_units, parts, at, marks, w, bias, out, total, last):
    feature, hid = w.shape
    rows_all = sum(p.shape[0] for p in parts)
    half = feature // 2
    if last:
        outs = (sds((half + 8, hid), f32), sds((half + 8, hid), f32))
    else:
        outs = (sds((feature, hid), f32), sds((2, hid), f32))
    extra = () if total is None else total
    kernel = functools.partial(
        learn_kernel, unit, per_block, n_units, len(parts), last, total is not None, half
    )
    return pl.pallas_call(
        kernel,
        out_shape=outs,
        in_specs=[SMEM] + [ANY] * len(parts) + [VMEM] * (4 + len(extra)),
        out_specs=(VMEM, VMEM),
        scratch_shapes=[
            pltpu.VMEM((rows_all, feature), bf16),
            pltpu.VMEM((rows_all, hid), bf16),
            pltpu.VMEM((rows_all, 1), f32),
            pltpu.SemaphoreType.DMA((len(parts),)),
        ],
        compiler_params=params(32),
        cost_estimate=pl.CostEstimate(
            flops=4 * rows_all * feature * hid,
            bytes_accessed=4 * rows_all * feature + 10 * feature * hid,
            transcendentals=rows_all * hid,
        ),
        name="learn",
    )(at, *parts, marks, w, bias, out, *extra)


def adam(old, grad, first, second):
    new_first = beta_one * first + (1.0 - beta_one) * grad
    new_second = beta_two * second + (1.0 - beta_two) * grad * grad
    new = old - learn_rate * new_first / (jnp.sqrt(new_second) + epsilon)
    return new.astype(bf16), new_first, new_second


def step_kernel(
    at_ref, kept, got, kept_vec, got_vec, w, first_w, second_w, vec_old, first_vec, second_vec,
    new_half, new_full, new_vec, new_first_w, new_second_w, new_first_vec, new_second_vec,
):
    new, new_first, new_second = adam(
        w[...].astype(f32), kept[...] + got[...], first_w[0], second_w[0]
    )
    new_half[...] = new
    new_full[0] = new
    new_first_w[0] = new_first
    new_second_w[0] = new_second

    @pl.when(pl.program_id(0) == 0)
    def _():
        grad = kept_vec[0:2, :] + got_vec[0:2, :]
        fresh, fresh_first, fresh_second = adam(
            vec_old[...].astype(f32), grad, first_vec[0], second_vec[0]
        )
        new_vec[0] = fresh
        new_first_vec[0] = fresh_first
        new_second_vec[0] = fresh_second


def take_step(rep, kept, got, w_in, vec_old, first_w, second_w, first_vec, second_vec):
    feature, hid = w_in.shape
    half = feature // 2
    tiles = max(n for n in range(1, 5) if half % (16 * n) == 0)
    tile = half // tiles
    here = pl.BlockSpec((tile, hid), lambda i, at: (i, 0))
    there = pl.BlockSpec((tile, hid), lambda i, at: (at[0] * tiles + i, 0))
    tail = pl.BlockSpec((8, hid), lambda i, at: (half // 8, 0))
    moment = pl.BlockSpec((1, tile, hid), lambda i, at: (0, i, 0))
    pair = pl.BlockSpec((2, hid), lambda i, at: (0, 0))
    pairs = pl.BlockSpec((1, 2, hid), lambda i, at: (0, 0, 0))
    full = pl.BlockSpec((1, tile, hid), lambda i, at: (0, at[0] * tiles + i, 0))
    return pl.pallas_call(
        step_kernel,
        grid_spec=pltpu.PrefetchScalarGridSpec(
            num_scalar_prefetch=1,
            grid=(tiles,),
            in_specs=[here, here, tail, tail, there, moment, moment, pair, pairs, pairs],
            out_specs=[here, full, pairs, moment, moment, pairs, pairs],
        ),
        out_shape=(
            sds((half, hid), bf16),
            sds((1, feature, hid), bf16),
            sds((1, 2, hid), bf16),
            sds((1, half, hid), f32),
            sds((1, half, hid), f32),
            sds((1, 2, hid), f32),
            sds((1, 2, hid), f32),
        ),
        compiler_params=params(24),
        name="step",
    )(rep, kept, got, kept, got, w_in, first_w, second_w, vec_old, first_vec, second_vec)


def join_kernel(at_ref, other_ref, full_ref, out_ref, sem):
    half = other_ref.shape[0]
    start = pl.multiple_of((1 - at_ref[0]) * half, half)
    load = pltpu.make_async_copy(other_ref, out_ref.at[0, pl.ds(start, half)], sem)
    load.start()
    load.wait()


def join(rep, other, full):
    return pl.pallas_call(
        join_kernel,
        out_shape=sds(full.shape, full.dtype),
        in_specs=[SMEM, ANY, ANY],
        out_specs=ANY,
        scratch_shapes=[pltpu.SemaphoreType.DMA(())],
        input_output_aliases={2: 0},
        compiler_params=params(8),
        name="join",
    )(rep, other, full)


def gathered(
    embeddings, coverage, labels, w_in, bias_in, w_out, first_w, second_w, first_vec, second_vec
):
    planes = lax.axis_size("dp")
    heads = lax.axis_size("head")
    owners = planes * heads
    z = lax.axis_index("dp")
    q = lax.axis_index("head")
    rep = lax.axis_index("rep").reshape(1)
    blocks, rows_block, feature = embeddings.shape
    per_block = coverage.shape[1]
    slots = 2 * blocks * per_block // owners
    unit = slots * rows_block
    rows = blocks * rows_block
    hid = w_in.shape[2]
    i32 = jnp.int32

    def right_pairs(hop):
        return [(i, i + 1) for i in range(hop - 1, planes - 1)]

    def left_pairs(hop):
        return [(i + 1, i) for i in range(planes - hop)]

    head_pairs = [[(i, i ^ k) for i in range(heads)] for k in range(heads)]

    def pair_up(k, ends):
        wanted = (0, planes - 1) if ends else range(planes)
        return [(p * heads + i, p * heads + (i ^ k)) for p in wanted for i in range(heads)]

    def exchange(units, ends=False):
        return [units[0]] + [
            lax.ppermute(units[k], ("dp", "head"), pair_up(k, ends)) for k in range(1, heads)
        ]

    def codes(plane):
        return [(plane * heads + (q ^ k)) * unit for k in range(heads)]

    own = embeddings.reshape(rows, feature)
    marks_own = make_marks(coverage, labels, owners, unit)

    hops_right, hops_left = [own], [own]
    for hop in range(1, planes - 1):
        hops_right.append(lax.ppermute(hops_right[-1], "dp", right_pairs(hop)))
        hops_left.append(lax.ppermute(hops_left[-1], "dp", left_pairs(hop)))

    marks_z = [marks_own] + [
        lax.ppermute(marks_own, "dp", [(i, (i + s) % planes) for i in range(planes)])
        for s in range(1, planes)
    ]
    marks_plane = jnp.stack(marks_z)
    marks_all = jnp.stack(
        [marks_plane]
        + [lax.ppermute(marks_plane, "head", head_pairs[k]) for k in range(1, heads)]
    ).reshape(heads * planes, 2 * per_block, rows)

    def pick(shards, marks, plan, scalars, out_rows):
        kernel = functools.partial(
            pick_kernel, plan, unit, per_block, len(shards), len(marks)
        )
        return pl.pallas_call(
            kernel,
            out_shape=[sds((r, feature), bf16) for r in out_rows],
            in_specs=[SMEM] + [ANY] * len(shards) + [VMEM] * len(marks),
            out_specs=[VMEM] * len(out_rows),
            scratch_shapes=[
                pltpu.VMEM((len(shards), rows, feature), bf16),
                pltpu.SemaphoreType.DMA((len(shards),)),
            ],
            compiler_params=params(32),
            cost_estimate=pl.CostEstimate(
                flops=2 * sum(out_rows) * rows * feature,
                bytes_accessed=2 * feature * (sum(out_rows) + rows * len(shards)),
                transcendentals=0,
            ),
            name="pick",
        )(jnp.stack(scalars).astype(i32), *shards, *marks)

    far = planes - 1 - z
    plan = [
        (0, 1, [(heads + k, 0) for k in range(heads)]),
        (0, 0, [(k, 0) for k in range(heads)]),
    ]
    picked = pick(
        [own], [marks_own, marks_own], plan, codes(z) + codes(far), [unit] * (2 * heads)
    )
    far_units = exchange(picked[heads:], ends=True)
    own_units = exchange(picked[:heads])
    far_sent = jnp.concatenate(far_units)
    far_got = lax.ppermute(far_sent, "dp", [(0, planes - 1), (planes - 1, 0)])

    one = jnp.ones((), i32)
    groups = [(own_units, [(k, jnp.zeros((), i32), one) for k in range(heads)])]
    for hop in range(1, planes - 1):
        from_left = (z >= hop).astype(i32)
        from_right = (z + hop < planes).astype(i32)
        if 2 * hop < planes:
            plan = [
                (0, 0, [(k, 0) for k in range(heads)]),
                (1, 1, [(k, unit) for k in range(heads)]),
            ]
            absent = -2 * unit * jnp.ones((), i32)
            scalars = [jnp.where(from_left > 0, c, absent) for c in codes(z)]
            scalars += [jnp.where(from_right > 0, c, absent) for c in codes(z)]
            got = exchange(
                pick(
                    [hops_right[hop], hops_left[hop]],
                    [marks_z[hop], marks_z[planes - hop]],
                    plan,
                    scalars,
                    [2 * unit] * heads,
                )
            )
            sources = []
            for k in range(heads):
                sources.append((k, jnp.full((), hop, i32), from_left))
                sources.append((k, jnp.full((), planes - hop, i32), from_right))
        else:
            use_left = from_right
            back = jnp.where(use_left > 0, planes - hop, hop).astype(i32)
            marks_hop = jnp.where(use_left > 0, marks_z[planes - hop], marks_z[hop])
            scalars = jnp.stack(codes(z) + [use_left]).astype(i32)
            got = exchange(
                pl.pallas_call(
                    functools.partial(pick_either_kernel, unit, per_block, heads),
                    out_shape=[sds((unit, feature), bf16)] * heads,
                    in_specs=[SMEM, ANY, ANY, VMEM],
                    out_specs=[VMEM] * heads,
                    scratch_shapes=[
                        pltpu.VMEM((rows, feature), bf16),
                        pltpu.SemaphoreType.DMA(()),
                    ],
                    compiler_params=params(32),
                    cost_estimate=pl.CostEstimate(
                        flops=2 * heads * unit * rows * feature,
                        bytes_accessed=2 * feature * (heads * unit + rows),
                        transcendentals=0,
                    ),
                    name="pick",
                )(scalars, hops_left[hop], hops_right[hop], marks_hop)
            )
            sources = [(k, back, from_left | from_right) for k in range(heads)]
        groups.append((got, sources))
    at_end = ((z == 0) | (z == planes - 1)).astype(i32)
    far_back = jnp.where(z == 0, 1, planes - 1).astype(i32)
    groups.append(([far_got], [(k, far_back, at_end) for k in range(heads)]))

    total = None
    my_code = (z * heads + q) * unit
    for at, (parts, sources) in enumerate(groups):
        scalars = [my_code]
        scalars += [k * planes + back for k, back, _ in sources]
        scalars += [real for _, _, real in sources]
        scalars += [rep[0]]
        total = learn(
            unit, per_block, len(sources), parts, jnp.stack(scalars).astype(i32), marks_all,
            w_in[0], bias_in, w_out, total, at == len(groups) - 1,
        )
    kept, given = total
    got = lax.ppermute(given, "rep", swap)
    vec_old = jnp.concatenate([bias_in, w_out])
    new_half, new_full, new_vec, nfw, nsw, nfv, nsv = take_step(
        rep, kept, got, w_in[0], vec_old, first_w, second_w, first_vec, second_vec
    )
    new_w_in = join(rep, lax.ppermute(new_half, "rep", swap), new_full)
    return new_w_in, new_vec, nfw, nsw, nfv, nsv


def routed(
    embeddings, coverage, labels, w_in, bias_in, w_out, first_w, second_w, first_vec, second_vec
):
    dp_count = lax.axis_size("dp")
    head_count = lax.axis_size("head")
    owners = dp_count * head_count
    block_count, rows_block, feature = embeddings.shape
    per_block = coverage.shape[1]
    slot_count = 2 * block_count * per_block // owners
    entries = block_count * per_block
    heads_flat = coverage.reshape(entries)
    onehot = (heads_flat[:, None] == jnp.arange(owners, dtype=jnp.int32)[None, :]).astype(jnp.int32)
    slot_rank = jnp.sum((jnp.cumsum(onehot, axis=0) - 1) * onehot, axis=1)
    target_slot = heads_flat * slot_count + slot_rank
    picker = jnp.arange(owners * slot_count, dtype=jnp.int32)[:, None] == target_slot[None, :]
    block_pick = jnp.sum(
        picker.reshape(owners * slot_count, block_count, per_block).astype(jnp.int32), axis=2
    ).astype(jnp.bfloat16)
    send_rows = jnp.dot(
        block_pick,
        embeddings.reshape(block_count, rows_block * feature),
        preferred_element_type=jnp.float32,
    ).astype(jnp.bfloat16)
    label_marks = (labels.reshape(entries, rows_block) + 1).astype(jnp.float32)
    send_marks = jnp.dot(
        picker.astype(jnp.float32), label_marks, precision=lax.Precision.HIGHEST
    ).astype(jnp.bfloat16)
    direct_rows = send_rows.reshape(owners, slot_count, rows_block, feature)
    direct_marks = send_marks.reshape(owners, slot_count, rows_block)
    got_rows, got_marks = (
        lax.all_to_all(direct_rows, ("dp", "head"), split_axis=0, concat_axis=0, tiled=True),
        lax.all_to_all(direct_marks, ("dp", "head"), split_axis=0, concat_axis=0, tiled=True),
    )
    row_data = got_rows.reshape(-1, feature)
    marks_all = got_marks.reshape(-1).astype(jnp.float32)
    usable = marks_all > 0.5
    target = marks_all - 1.0
    out_weight = w_out[0].astype(jnp.float32)
    pre_act = (
        jnp.dot(row_data, w_in[0], preferred_element_type=jnp.float32)
        + bias_in[0].astype(jnp.float32)[None, :]
    )
    sig_pre = jax.nn.sigmoid(pre_act)
    hidden = pre_act * sig_pre
    logits = jnp.sum(hidden * out_weight[None, :], axis=1)
    residual = jnp.where(usable, jax.nn.sigmoid(logits) - target, jnp.zeros_like(logits))
    grad_pre = residual[:, None] * out_weight[None, :] * sig_pre * (1.0 + pre_act * (1.0 - sig_pre))
    grad_low = grad_pre.astype(jnp.bfloat16)
    vec_part = jnp.stack([jnp.sum(grad_pre, axis=0), jnp.sum(residual[:, None] * hidden, axis=0)])
    half_rows = feature // lax.axis_size("rep")
    rep_at = lax.axis_index("rep")
    first_row = rep_at * half_rows
    grad_part = lax.dot_general(
        row_data, grad_low, (((0,), (0,)), ((), ())), preferred_element_type=jnp.float32
    ).reshape(2, half_rows, -1)
    kept = jnp.where(rep_at == 0, grad_part[0], grad_part[1])
    given = jnp.where(rep_at == 0, grad_part[1], grad_part[0])
    grad_w = kept + lax.ppermute(given, "rep", swap)
    grad_vec = vec_part + lax.ppermute(vec_part, "rep", swap)
    new_first_w = beta_one * first_w[0] + (1.0 - beta_one) * grad_w
    new_second_w = beta_two * second_w[0] + (1.0 - beta_two) * grad_w * grad_w
    old_rows = lax.dynamic_slice_in_dim(w_in[0], first_row, half_rows, 0).astype(jnp.float32)
    new_half = (old_rows - learn_rate * new_first_w / (jnp.sqrt(new_second_w) + epsilon)).astype(
        jnp.bfloat16
    )
    other_half = lax.ppermute(new_half, "rep", swap)
    new_w_in = jnp.where(
        rep_at == 0,
        jnp.concatenate([new_half, other_half]),
        jnp.concatenate([other_half, new_half]),
    )
    vector = jnp.stack([bias_in[0], w_out[0]]).astype(jnp.float32)
    new_first_vec = beta_one * first_vec[0] + (1.0 - beta_one) * grad_vec
    new_second_vec = beta_two * second_vec[0] + (1.0 - beta_two) * grad_vec * grad_vec
    new_vec = (vector - learn_rate * new_first_vec / (jnp.sqrt(new_second_vec) + epsilon)).astype(
        jnp.bfloat16
    )
    return (
        new_w_in[None],
        new_vec[None],
        new_first_w[None],
        new_second_w[None],
        new_first_vec[None],
        new_second_vec[None],
    )


def solution(mesh):
    placed = (
        P(("dp", "head", "rep"), None, None),
        P(("dp", "head", "rep"), None),
        P(("dp", "head", "rep"), None, None),
        P(("dp", "head"), None, None),
        P(("dp", "head"), None),
        P(("dp", "head"), None),
        P(("dp", "head"), "rep", None),
        P(("dp", "head"), "rep", None),
        P(("dp", "head"), None, None),
        P(("dp", "head"), None, None),
    )
    planes, heads, reps = mesh.shape["dp"], mesh.shape["head"], mesh.shape["rep"]
    short = 2 < planes <= heads and heads & (heads - 1) == 0 and reps == 2
    return jax.shard_map(
        gathered if short else routed,
        mesh=mesh,
        in_specs=placed,
        out_specs=(
            P(("dp", "head"), None, None),
            P(("dp", "head"), None, None),
            P(("dp", "head"), "rep", None),
            P(("dp", "head"), "rep", None),
            P(("dp", "head"), None, None),
            P(("dp", "head"), None, None),
        ),
        check_vma=False,
    )
```

```python
import functools

import jax
import jax.numpy as jnp
from jax import lax
from jax.experimental import pallas as pl
from jax.experimental.pallas import tpu as pltpu
from jax.sharding import PartitionSpec as P

beta_one = 0.9
beta_two = 0.999
learn_rate = 0.001
epsilon = 1e-08
swap = [(0, 1), (1, 0)]
PB, PC, LA, LB, LC, LF = (0, 10, 0, 40, 20, 0)
bf16 = jnp.bfloat16
MIB = 1024 * 1024
ANY = pl.BlockSpec(memory_space=pl.ANY)
VMEM = pl.BlockSpec(memory_space=pltpu.VMEM)
HBM = pl.BlockSpec(memory_space=pltpu.HBM)
SMEM = pl.BlockSpec(memory_space=pltpu.SMEM)
f32 = jnp.float32


def spent(us):
    return pl.CostEstimate(flops=int(us * 1150000000) + 1, bytes_accessed=1, transcendentals=0)


def params(mib):
    return pltpu.CompilerParams(vmem_limit_bytes=mib * MIB)


def sds(shape, dtype):
    return jax.ShapeDtypeStruct(shape, dtype)


def half_sigmoid(x):
    return 0.5 * jnp.tanh(0.5 * x) + 0.5


def shard_kernel(owners, cov_ref, lab_ref, own_ref, out_ref, mark_ref, sems):
    per_block, blocks = cov_ref.shape
    rows_block = lab_ref.shape[1]
    rows = blocks * rows_block
    load = pltpu.make_async_copy(own_ref, out_ref.at[pl.ds(0, rows)], sems.at[0])
    load.start()
    cov = cov_ref[...]
    heads_at = lax.broadcasted_iota(jnp.int32, (owners, blocks), 0)
    named = (cov[0:1] == heads_at).astype(f32)
    for t in range(1, per_block):
        named = named + (cov[t : t + 1] == heads_at).astype(f32)
    block_of = lax.broadcasted_iota(jnp.int32, (blocks, rows), 1) // rows_block
    block_at = lax.broadcasted_iota(jnp.int32, (blocks, rows), 0)
    same = (block_of == block_at).astype(bf16)
    before = (block_at < block_of).astype(bf16)
    rank = jnp.dot(named.astype(bf16), before, preferred_element_type=f32)
    cov_rows = jnp.dot(cov.astype(f32).astype(bf16), same, preferred_element_type=f32)
    row_in = lax.broadcasted_iota(jnp.int32, (rows_block, rows), 1) % rows_block
    row_at = lax.broadcasted_iota(jnp.int32, (rows_block, rows), 0)
    head_rows = lax.broadcasted_iota(jnp.int32, (owners, rows), 0).astype(f32)
    at_mark = lax.broadcasted_iota(jnp.int32, (16, rows), 0)
    mark_rows = jnp.zeros((16, rows), f32)
    for t in range(per_block):
        mine = cov_rows[t : t + 1]
        own_rank = jnp.sum(jnp.where(mine == head_rows, rank, 0.0), axis=0, keepdims=True)
        place = own_rank * rows_block + row_in[0:1].astype(f32)
        spread = jnp.dot(lab_ref[t].astype(f32).astype(bf16), same, preferred_element_type=f32)
        label = 1.0 + jnp.sum(jnp.where(row_in == row_at, spread, 0.0), axis=0, keepdims=True)
        mark_rows = jnp.where(at_mark == t, mine, mark_rows)
        mark_rows = jnp.where(at_mark == per_block + t, place, mark_rows)
        mark_rows = jnp.where(at_mark == 2 * per_block + t, label, mark_rows)
    mark_ref[...] = jnp.zeros(mark_ref.shape, bf16)
    mark_ref[:, 0:rows] = mark_rows.astype(bf16)
    store = pltpu.make_async_copy(mark_ref, out_ref.at[pl.ds(rows, 16)], sems.at[1])
    store.start()
    load.wait()
    store.wait()


def make_shard(own, coverage, labels, owners):
    rows, feature = own.shape
    return pl.pallas_call(
        functools.partial(shard_kernel, owners),
        out_shape=sds((rows + 16, feature), bf16),
        in_specs=[VMEM, VMEM, HBM],
        out_specs=HBM,
        scratch_shapes=[pltpu.VMEM((16, feature), bf16), pltpu.SemaphoreType.DMA((2,))],
        compiler_params=params(8),
        name="shard",
    )(coverage.T, labels.transpose(1, 2, 0), own)


def pick_rows(marks, shard, heads, unit, per_block):
    rows = marks.shape[1]
    slot = lax.broadcasted_iota(jnp.int32, (unit, rows), 0).astype(f32)
    at_head = lax.broadcasted_iota(jnp.int32, (8, rows), 0)
    chosen = []
    labels = jnp.zeros((8, rows), f32)
    for k, head in enumerate(heads):
        place = jnp.full((1, rows), -1.0, f32)
        label = jnp.zeros((1, rows), f32)
        for t in range(per_block):
            mine = marks[t : t + 1] == head
            place = jnp.where(mine, marks[per_block + t : per_block + t + 1], place)
            label = jnp.where(mine, marks[2 * per_block + t : 2 * per_block + t + 1], label)
        chosen.append(jnp.where(place == slot, 1.0, 0.0).astype(bf16))
        labels = jnp.where(at_head == k, label, labels)
    chosen = jnp.concatenate(chosen, axis=0)
    picked = jnp.dot(chosen, shard, preferred_element_type=f32).astype(bf16)
    mark = lax.dot_general(
        labels.astype(bf16), chosen, (((1,), (1,)), ((), ())), preferred_element_type=f32
    )
    return picked, mark


def pick_kernel(unit, per_block, plan, n_shards, n_heads, at_ref, *refs):
    shards, refs = refs[:n_shards], refs[n_shards:]
    outs, refs = refs[:n_heads], refs[n_heads:]
    held, ready, in_sems, out_sems = refs
    units = len(plan)
    rows = held.shape[1] - 16

    for g, (yes, no) in enumerate(plan):
        if yes == no:
            pltpu.make_async_copy(shards[yes], held.at[g], in_sems.at[g]).start()
        else:
            flag = at_ref[units * n_heads + g] > 0

            @pl.when(flag)
            def _():
                pltpu.make_async_copy(shards[yes], held.at[g], in_sems.at[g]).start()

            @pl.when(jnp.logical_not(flag))
            def _():
                pltpu.make_async_copy(shards[no], held.at[g], in_sems.at[g]).start()

    at_mark = lax.broadcasted_iota(jnp.int32, (16, unit), 0)
    mark_rows = [jnp.zeros((16, unit), f32)] * n_heads
    for g, (yes, _) in enumerate(plan):
        pltpu.make_async_copy(shards[yes], held.at[g], in_sems.at[g]).wait()
        marks = held[g, rows:, 0:rows].astype(f32)
        wanted = [at_ref[g * n_heads + k].astype(f32) for k in range(n_heads)]
        picked, mark = pick_rows(marks, held[g, 0:rows], wanted, unit, per_block)
        for k in range(n_heads):
            ready[k, g * unit : (g + 1) * unit, :] = picked[k * unit : (k + 1) * unit]
            own_mark = mark[k : k + 1, k * unit : (k + 1) * unit]
            mark_rows[k] = jnp.where(at_mark == g, own_mark, mark_rows[k])
    for k in range(n_heads):
        ready[k, units * unit :, :] = jnp.zeros((16, ready.shape[2]), bf16)
        ready[k, units * unit :, 0:unit] = mark_rows[k].astype(bf16)
        pltpu.make_async_copy(ready.at[k], outs[k], out_sems.at[k]).start()
    for k in range(n_heads):
        pltpu.make_async_copy(ready.at[k], outs[k], out_sems.at[k]).wait()


def pick(unit, per_block, shards, plan, heads_at, flags, cost):
    rows, feature = shards[0].shape
    units = len(plan)
    n_heads = len(heads_at) // units
    size = units * unit + 16
    return pl.pallas_call(
        functools.partial(pick_kernel, unit, per_block, plan, len(shards), n_heads),
        out_shape=[sds((size, feature), bf16)] * n_heads,
        in_specs=[SMEM] + [HBM] * len(shards),
        out_specs=[HBM] * n_heads,
        scratch_shapes=[
            pltpu.VMEM((units, rows, feature), bf16),
            pltpu.VMEM((n_heads, size, feature), bf16),
            pltpu.SemaphoreType.DMA((units,)),
            pltpu.SemaphoreType.DMA((n_heads,)),
        ],
        compiler_params=params(16),
        cost_estimate=spent(cost),
        name="pick",
    )(jnp.stack(heads_at + flags).astype(jnp.int32), *shards)


def pack_kernel(unit, n, *refs):
    parts, out_ref, mark_ref, all_ref, sems = refs[:n], *refs[n:]
    loads = []
    for k in range(n):
        loads.append(
            pltpu.make_async_copy(
                parts[k].at[pl.ds(0, unit)], out_ref.at[pl.ds(k * unit, unit)], sems.at[0, k]
            )
        )
        loads.append(
            pltpu.make_async_copy(
                parts[k].at[pl.ds(unit, 16)], mark_ref.at[k], sems.at[1, k]
            )
        )
    for load in loads:
        load.start()
    for load in loads:
        load.wait()
    at_mark = lax.broadcasted_iota(jnp.int32, (16, unit), 0)
    mark_rows = jnp.zeros((16, unit), f32)
    for k in range(n):
        marks = mark_ref[k, :, 0:unit].astype(f32)
        mark_rows = jnp.where(at_mark == k, marks[0:1], mark_rows)
    all_ref[...] = jnp.zeros(all_ref.shape, bf16)
    all_ref[:, 0:unit] = mark_rows.astype(bf16)
    store = pltpu.make_async_copy(all_ref, out_ref.at[pl.ds(n * unit, 16)], sems.at[0, n])
    store.start()
    store.wait()


def pack(unit, parts):
    feature = parts[0].shape[1]
    n = len(parts)
    return pl.pallas_call(
        functools.partial(pack_kernel, unit, n),
        out_shape=sds((n * unit + 16, feature), bf16),
        in_specs=[HBM] * n,
        out_specs=HBM,
        scratch_shapes=[
            pltpu.VMEM((n, 16, feature), bf16),
            pltpu.VMEM((16, feature), bf16),
            pltpu.SemaphoreType.DMA((2, n + 1)),
        ],
        compiler_params=params(8),
        name="pack",
    )(*parts)


def learn_kernel(unit, spots, n_parts, last, with_total, half_rows, at_ref, *refs):
    parts, refs = refs[:n_parts], refs[n_parts:]
    w_ref, bias_ref, out_ref, refs = refs[0], refs[1], refs[2], refs[3:]
    if with_total:
        total_ref, vec_ref, refs = refs[0], refs[1], refs[2:]
    if last:
        kept_ref, given_ref, refs = refs[0], refs[1], refs[2:]
    else:
        new_total_ref, new_vec_ref, refs = refs[0], refs[1], refs[2:]
    rows_ref, low_ref, mark_ref, target_ref, sems = refs
    rows_all, feature = rows_ref.shape
    loads = []
    for i in range(n_parts):
        loads.append(
            pltpu.make_async_copy(
                parts[i].at[pl.ds(parts[i].shape[0] - 16, 16)], mark_ref.at[i], sems.at[0, i]
            )
        )
    for u, (part, at, _) in enumerate(spots):
        loads.append(
            pltpu.make_async_copy(
                parts[part].at[pl.ds(at, unit)],
                rows_ref.at[pl.ds(u * unit, unit)],
                sems.at[1, u],
            )
        )
    for load in loads:
        load.start()
    for load in loads:
        load.wait()
    eye = lax.broadcasted_iota(jnp.int32, (unit, unit), 0) == lax.broadcasted_iota(
        jnp.int32, (unit, unit), 1
    )
    for u, (part, _, mark_at) in enumerate(spots):
        marks = mark_ref[part, :, 0:unit].astype(f32)[mark_at : mark_at + 1]
        target_ref[u * unit : (u + 1) * unit, :] = jnp.sum(
            jnp.where(eye, marks, 0.0), axis=1, keepdims=True
        ) * at_ref[1].astype(f32)
    bias = bias_ref[...].astype(f32)
    out_weight = out_ref[...].astype(f32)
    step = 2 * unit
    hid = w_ref.shape[1]

    def forward(i, carry):
        span = pl.ds(pl.multiple_of(i * step, step), step)
        pre = jnp.dot(rows_ref[span, :], w_ref[...], preferred_element_type=f32) + bias
        gate = half_sigmoid(pre)
        hidden = pre * gate
        logit = jnp.sum(hidden * out_weight, axis=1, keepdims=True)
        mark = target_ref[span, :]
        residual = jnp.where(mark > 0.5, half_sigmoid(logit) - (mark - 1.0), 0.0)
        grad_pre = residual * out_weight * gate * (1.0 + pre * (1.0 - gate))
        low_ref[span, :] = grad_pre.astype(bf16)
        return (
            carry[0] + jnp.sum(grad_pre, axis=0, keepdims=True),
            carry[1] + jnp.sum(residual * hidden, axis=0, keepdims=True),
        )

    if with_total:
        start = (vec_ref[0:1, :], vec_ref[1:2, :])
    else:
        start = (jnp.zeros((1, hid), f32), jnp.zeros((1, hid), f32))
    grad_bias, grad_out = lax.fori_loop(0, rows_all // step, forward, start)

    def product(first, size):
        piece = lax.dot_general(
            rows_ref[:, first : first + size],
            low_ref[...],
            (((0,), (0,)), ((), ())),
            preferred_element_type=f32,
        )
        if with_total:
            piece = piece + total_ref[first : first + size, :]
        return piece

    tile = 128 * max(n for n in range(1, 5) if feature % (128 * n) == 0)
    if not last:
        for first in range(0, feature, tile):
            new_total_ref[first : first + tile, :] = product(first, tile)
        new_vec_ref[0:1, :] = grad_bias
        new_vec_ref[1:2, :] = grad_out
        return
    rep = at_ref[0]
    given_ref[half_rows : half_rows + 8, :] = jnp.zeros((8, hid), f32)
    kept_ref[half_rows : half_rows + 8, :] = jnp.zeros((8, hid), f32)
    for ref in (given_ref, kept_ref):
        ref[half_rows : half_rows + 1, :] = grad_bias
        ref[half_rows + 1 : half_rows + 2, :] = grad_out
    for first in range(0, feature, tile):
        piece = product(first, tile)
        cut = min(max(half_rows - first, 0), tile)

        @pl.when(rep == 0)
        def _():
            if cut > 0:
                kept_ref[first : first + cut, :] = piece[:cut]
            if cut < tile:
                given_ref[first + cut - half_rows : first + tile - half_rows, :] = piece[cut:]

        @pl.when(rep != 0)
        def _():
            if cut > 0:
                given_ref[first : first + cut, :] = piece[:cut]
            if cut < tile:
                kept_ref[first + cut - half_rows : first + tile - half_rows, :] = piece[cut:]


def learn(unit, spots, parts, at, w, bias, out, total, cost, last):
    feature, hid = w.shape
    rows_all = len(spots) * unit
    half = feature // 2
    if last:
        outs = (sds((half + 8, hid), f32), sds((half + 8, hid), f32))
    else:
        outs = (sds((feature, hid), f32), sds((2, hid), f32))
    extra = () if total is None else total
    kernel = functools.partial(
        learn_kernel, unit, spots, len(parts), last, total is not None, half
    )
    return pl.pallas_call(
        kernel,
        out_shape=outs,
        in_specs=[SMEM] + [HBM] * len(parts) + [VMEM] * (3 + len(extra)),
        out_specs=(VMEM, VMEM),
        scratch_shapes=[
            pltpu.VMEM((rows_all, feature), bf16),
            pltpu.VMEM((rows_all, hid), bf16),
            pltpu.VMEM((len(parts), 16, feature), bf16),
            pltpu.VMEM((rows_all, 1), f32),
            pltpu.SemaphoreType.DMA((2, max(len(parts), len(spots)))),
        ],
        compiler_params=params(24),
        cost_estimate=spent(cost),
        name="learn",
    )(at, *parts, w, bias, out, *extra)


def adam(old, grad, first, second):
    new_first = beta_one * first + (1.0 - beta_one) * grad
    new_second = beta_two * second + (1.0 - beta_two) * grad * grad
    new = old - learn_rate * new_first / (jnp.sqrt(new_second) + epsilon)
    return new.astype(bf16), new_first, new_second


def step_kernel(
    at_ref, kept, got, kept_vec, got_vec, w, first_w, second_w, vec_old, first_vec, second_vec,
    new_half, new_full, new_vec, new_first_w, new_second_w, new_first_vec, new_second_vec,
):
    new, new_first, new_second = adam(
        w[...].astype(f32), kept[...] + got[...], first_w[0], second_w[0]
    )
    new_half[...] = new
    new_full[0] = new
    new_first_w[0] = new_first
    new_second_w[0] = new_second

    @pl.when(pl.program_id(0) == 0)
    def _():
        grad = kept_vec[0:2, :] + got_vec[0:2, :]
        fresh, fresh_first, fresh_second = adam(
            vec_old[...].astype(f32), grad, first_vec[0], second_vec[0]
        )
        new_vec[0] = fresh
        new_first_vec[0] = fresh_first
        new_second_vec[0] = fresh_second


def take_step(rep, kept, got, w_in, vec_old, first_w, second_w, first_vec, second_vec):
    feature, hid = w_in.shape
    half = feature // 2
    tiles = max(n for n in range(1, 5) if half % (16 * n) == 0)
    tile = half // tiles
    here = pl.BlockSpec((tile, hid), lambda i, at: (i, 0))
    there = pl.BlockSpec((tile, hid), lambda i, at: (at[0] * tiles + i, 0))
    tail = pl.BlockSpec((8, hid), lambda i, at: (half // 8, 0))
    moment = pl.BlockSpec((1, tile, hid), lambda i, at: (0, i, 0))
    pair = pl.BlockSpec((2, hid), lambda i, at: (0, 0))
    pairs = pl.BlockSpec((1, 2, hid), lambda i, at: (0, 0, 0))
    full = pl.BlockSpec((1, tile, hid), lambda i, at: (0, at[0] * tiles + i, 0))
    return pl.pallas_call(
        step_kernel,
        grid_spec=pltpu.PrefetchScalarGridSpec(
            num_scalar_prefetch=1,
            grid=(tiles,),
            in_specs=[here, here, tail, tail, there, moment, moment, pair, pairs, pairs],
            out_specs=[here, full, pairs, moment, moment, pairs, pairs],
        ),
        out_shape=(
            sds((half, hid), bf16),
            sds((1, feature, hid), bf16),
            sds((1, 2, hid), bf16),
            sds((1, half, hid), f32),
            sds((1, half, hid), f32),
            sds((1, 2, hid), f32),
            sds((1, 2, hid), f32),
        ),
        compiler_params=params(16),
        name="step",
    )(rep, kept, got, kept, got, w_in, first_w, second_w, vec_old, first_vec, second_vec)


def join_kernel(at_ref, other_ref, full_ref, out_ref, sem):
    half = other_ref.shape[0]
    start = pl.multiple_of((1 - at_ref[0]) * half, half)
    load = pltpu.make_async_copy(other_ref, out_ref.at[0, pl.ds(start, half)], sem)
    load.start()
    load.wait()


def join(rep, other, full):
    return pl.pallas_call(
        join_kernel,
        out_shape=sds(full.shape, full.dtype),
        in_specs=[SMEM, ANY, ANY],
        out_specs=ANY,
        scratch_shapes=[pltpu.SemaphoreType.DMA(())],
        input_output_aliases={2: 0},
        compiler_params=params(8),
        name="join",
    )(rep, other, full)


def gathered(
    embeddings, coverage, labels, w_in, bias_in, w_out, first_w, second_w, first_vec, second_vec
):
    planes = lax.axis_size("dp")
    heads = lax.axis_size("head")
    owners = planes * heads
    z = lax.axis_index("dp")
    q = lax.axis_index("head")
    rep = lax.axis_index("rep").reshape(1)
    blocks, rows_block, feature = embeddings.shape
    per_block = coverage.shape[1]
    slots = 2 * blocks * per_block // owners
    unit = slots * rows_block
    rows = blocks * rows_block
    def right_pairs(hop):
        return [(i, i + 1) for i in range(hop - 1, planes - 1)]

    def left_pairs(hop):
        return [(i + 1, i) for i in range(planes - hop)]

    def exchange(units):
        return [units[0]] + [
            lax.ppermute(units[k], "head", [(i, i ^ k) for i in range(heads)])
            for k in range(1, heads)
        ]

    def plane_heads(plane, real=None):
        found = [plane * heads + (q ^ k) for k in range(heads)]
        return found if real is None else [jnp.where(real, h, -1) for h in found]

    own = make_shard(embeddings.reshape(rows, feature), coverage, labels, owners)
    right = lax.ppermute(own, "dp", right_pairs(1))
    left = lax.ppermute(own, "dp", left_pairs(1))
    always = jnp.ones((), jnp.bool_)
    at_end = (z == 0) | (z == planes - 1)

    def add(total, parts, spots, real, cost, last=False):
        scalars = jnp.stack([rep[0], real]).astype(jnp.int32)
        return learn(unit, spots, parts, scalars, w_in[0], bias_in, w_out, total, cost, last)

    first_heads = plane_heads(jnp.where(at_end, planes - 1 - z, z))
    first_units = exchange(pick(unit, per_block, [own], [(0, 0)], first_heads, [always], 0))
    far_sent = pack(unit, first_units)
    one = jnp.ones((), jnp.int32)
    first_spots = [(k, 0, 0) for k in range(heads)]
    middle = 1 - at_end.astype(jnp.int32)
    rest = []
    for hop in range(1, planes - 1):
        from_left = z >= hop
        from_right = z + hop < planes
        if hop + 1 < planes - 1:
            right, left, far_sent = lax.optimization_barrier((right, left, far_sent))
            next_right = lax.ppermute(right, "dp", right_pairs(hop + 1))
            next_left = lax.ppermute(left, "dp", left_pairs(hop + 1))
        else:
            next_right, next_left = None, None
        if hop == planes - 2 and hop > 1:
            far_sent, right, left, *total = lax.optimization_barrier(
                (far_sent, right, left, *total)
            )
            far_got = lax.ppermute(far_sent, "dp", [(0, planes - 1), (planes - 1, 0)])
        if 2 * hop < planes:
            fill = hop == 1
            messages = pick(
                unit,
                per_block,
                [right, left, own],
                [(0, 2), (1, 2)],
                plane_heads(z, from_left | fill) + plane_heads(z, from_right | fill),
                [from_left, from_right],
                PB,
            )
            units = 2
        else:
            messages = pick(
                unit,
                per_block,
                [left, right],
                [(0, 1)],
                plane_heads(z, from_left | from_right),
                [from_right],
                PC,
            )
            units = 1
        where = [(k, g * unit, g) for k in range(heads) for g in range(units)]
        if hop == 1:
            first_units = lax.optimization_barrier((*first_units, *messages))[:heads]
            total = add(None, first_units, first_spots, middle, LA)
        else:
            messages = lax.optimization_barrier((*messages, *rest[-1][0]))[:heads]
        rest.append((exchange(messages), where))
        right, left = next_right, next_left
    rest.append(([far_got], [(0, k * unit, k) for k in range(heads)]))

    for at, (parts, spots) in enumerate(rest):
        cost = (LB, LC, LF)[min(at, 2)]
        total = add(total, parts, spots, one, cost, at == len(rest) - 1)
    kept, given = total
    got = lax.ppermute(given, "rep", swap)
    vec_old = jnp.concatenate([bias_in, w_out])
    new_half, new_full, new_vec, nfw, nsw, nfv, nsv = take_step(
        rep, kept, got, w_in[0], vec_old, first_w, second_w, first_vec, second_vec
    )
    new_w_in = join(rep, lax.ppermute(new_half, "rep", swap), new_full)
    return new_w_in, new_vec, nfw, nsw, nfv, nsv


def routed(
    embeddings, coverage, labels, w_in, bias_in, w_out, first_w, second_w, first_vec, second_vec
):
    dp_count = lax.axis_size("dp")
    head_count = lax.axis_size("head")
    owners = dp_count * head_count
    block_count, rows_block, feature = embeddings.shape
    per_block = coverage.shape[1]
    slot_count = 2 * block_count * per_block // owners
    entries = block_count * per_block
    heads_flat = coverage.reshape(entries)
    onehot = (heads_flat[:, None] == jnp.arange(owners, dtype=jnp.int32)[None, :]).astype(jnp.int32)
    slot_rank = jnp.sum((jnp.cumsum(onehot, axis=0) - 1) * onehot, axis=1)
    target_slot = heads_flat * slot_count + slot_rank
    picker = jnp.arange(owners * slot_count, dtype=jnp.int32)[:, None] == target_slot[None, :]
    block_pick = jnp.sum(
        picker.reshape(owners * slot_count, block_count, per_block).astype(jnp.int32), axis=2
    ).astype(jnp.bfloat16)
    send_rows = jnp.dot(
        block_pick,
        embeddings.reshape(block_count, rows_block * feature),
        preferred_element_type=jnp.float32,
    ).astype(jnp.bfloat16)
    label_marks = (labels.reshape(entries, rows_block) + 1).astype(jnp.float32)
    send_marks = jnp.dot(
        picker.astype(jnp.float32), label_marks, precision=lax.Precision.HIGHEST
    ).astype(jnp.bfloat16)
    direct_rows = send_rows.reshape(owners, slot_count, rows_block, feature)
    direct_marks = send_marks.reshape(owners, slot_count, rows_block)
    got_rows, got_marks = (
        lax.all_to_all(direct_rows, ("dp", "head"), split_axis=0, concat_axis=0, tiled=True),
        lax.all_to_all(direct_marks, ("dp", "head"), split_axis=0, concat_axis=0, tiled=True),
    )
    row_data = got_rows.reshape(-1, feature)
    marks_all = got_marks.reshape(-1).astype(jnp.float32)
    usable = marks_all > 0.5
    target = marks_all - 1.0
    out_weight = w_out[0].astype(jnp.float32)
    pre_act = (
        jnp.dot(row_data, w_in[0], preferred_element_type=jnp.float32)
        + bias_in[0].astype(jnp.float32)[None, :]
    )
    sig_pre = jax.nn.sigmoid(pre_act)
    hidden = pre_act * sig_pre
    logits = jnp.sum(hidden * out_weight[None, :], axis=1)
    residual = jnp.where(usable, jax.nn.sigmoid(logits) - target, jnp.zeros_like(logits))
    grad_pre = residual[:, None] * out_weight[None, :] * sig_pre * (1.0 + pre_act * (1.0 - sig_pre))
    grad_low = grad_pre.astype(jnp.bfloat16)
    vec_part = jnp.stack([jnp.sum(grad_pre, axis=0), jnp.sum(residual[:, None] * hidden, axis=0)])
    half_rows = feature // lax.axis_size("rep")
    rep_at = lax.axis_index("rep")
    first_row = rep_at * half_rows
    grad_part = lax.dot_general(
        row_data, grad_low, (((0,), (0,)), ((), ())), preferred_element_type=jnp.float32
    ).reshape(2, half_rows, -1)
    kept = jnp.where(rep_at == 0, grad_part[0], grad_part[1])
    given = jnp.where(rep_at == 0, grad_part[1], grad_part[0])
    grad_w = kept + lax.ppermute(given, "rep", swap)
    grad_vec = vec_part + lax.ppermute(vec_part, "rep", swap)
    new_first_w = beta_one * first_w[0] + (1.0 - beta_one) * grad_w
    new_second_w = beta_two * second_w[0] + (1.0 - beta_two) * grad_w * grad_w
    old_rows = lax.dynamic_slice_in_dim(w_in[0], first_row, half_rows, 0).astype(jnp.float32)
    new_half = (old_rows - learn_rate * new_first_w / (jnp.sqrt(new_second_w) + epsilon)).astype(
        jnp.bfloat16
    )
    other_half = lax.ppermute(new_half, "rep", swap)
    new_w_in = jnp.where(
        rep_at == 0,
        jnp.concatenate([new_half, other_half]),
        jnp.concatenate([other_half, new_half]),
    )
    vector = jnp.stack([bias_in[0], w_out[0]]).astype(jnp.float32)
    new_first_vec = beta_one * first_vec[0] + (1.0 - beta_one) * grad_vec
    new_second_vec = beta_two * second_vec[0] + (1.0 - beta_two) * grad_vec * grad_vec
    new_vec = (vector - learn_rate * new_first_vec / (jnp.sqrt(new_second_vec) + epsilon)).astype(
        jnp.bfloat16
    )
    return (
        new_w_in[None],
        new_vec[None],
        new_first_w[None],
        new_second_w[None],
        new_first_vec[None],
        new_second_vec[None],
    )


def solution(mesh):
    placed = (
        P(("dp", "head", "rep"), None, None),
        P(("dp", "head", "rep"), None),
        P(("dp", "head", "rep"), None, None),
        P(("dp", "head"), None, None),
        P(("dp", "head"), None),
        P(("dp", "head"), None),
        P(("dp", "head"), "rep", None),
        P(("dp", "head"), "rep", None),
        P(("dp", "head"), None, None),
        P(("dp", "head"), None, None),
    )
    planes, heads, reps = mesh.shape["dp"], mesh.shape["head"], mesh.shape["rep"]
    short = 2 < planes <= heads and heads & (heads - 1) == 0 and reps == 2
    return jax.shard_map(
        gathered if short else routed,
        mesh=mesh,
        in_specs=placed,
        out_specs=(
            P(("dp", "head"), None, None),
            P(("dp", "head"), None, None),
            P(("dp", "head"), "rep", None),
            P(("dp", "head"), "rep", None),
            P(("dp", "head"), None, None),
            P(("dp", "head"), None, None),
        ),
        check_vma=False,
    )
```

```python
import functools

import jax
import jax.numpy as jnp
from jax import lax
from jax.experimental import pallas as pl
from jax.experimental.pallas import tpu as pltpu
from jax.sharding import PartitionSpec as P

beta_one = 0.9
beta_two = 0.999
learn_rate = 0.001
epsilon = 1e-08
swap = [(0, 1), (1, 0)]
PB, PC, LA, LB, LC, LF = (0, 10, 0, 40, 20, 0)
bf16 = jnp.bfloat16
MIB = 1024 * 1024
ROOM = 60
ANY = pl.BlockSpec(memory_space=pl.ANY)
VMEM = pl.BlockSpec(memory_space=pltpu.VMEM)
HBM = pl.BlockSpec(memory_space=pltpu.HBM)
SMEM = pl.BlockSpec(memory_space=pltpu.SMEM)
f32 = jnp.float32


def spent(us):
    return pl.CostEstimate(flops=int(us * 1150000000) + 1, bytes_accessed=1, transcendentals=0)


def params(mib):
    return pltpu.CompilerParams(vmem_limit_bytes=mib * MIB)


def sds(shape, dtype):
    return jax.ShapeDtypeStruct(shape, dtype)


def half_sigmoid(x):
    return 0.5 * jnp.tanh(0.5 * x) + 0.5


def shard_kernel(owners, cov_hbm, lab_hbm, own_ref, out_ref, cov_ref, lab_ref, held_ref, sems):
    per_block, blocks = cov_ref.shape
    rows_block = lab_ref.shape[1]
    rows = blocks * rows_block
    load_cov = pltpu.make_async_copy(cov_hbm, cov_ref, sems.at[0])
    load_lab = pltpu.make_async_copy(lab_hbm, lab_ref, sems.at[1])
    half = rows // 2
    loads = []
    stores = []
    for i in range(2):
        part = pl.ds(i * half, half)
        loads.append(pltpu.make_async_copy(own_ref.at[part], held_ref.at[part], sems.at[2 + i]))
        stores.append(pltpu.make_async_copy(held_ref.at[part], out_ref.at[part], sems.at[4 + i]))
    load_cov.start()
    load_lab.start()
    for load in loads:
        load.start()
    for load, store in zip(loads, stores):
        load.wait()
        store.start()
    load_cov.wait()
    load_lab.wait()
    cov = cov_ref[...]
    heads_at = lax.broadcasted_iota(jnp.int32, (owners, blocks), 0)
    named = (cov[0:1] == heads_at).astype(f32)
    for t in range(1, per_block):
        named = named + (cov[t : t + 1] == heads_at).astype(f32)
    block_of = lax.broadcasted_iota(jnp.int32, (blocks, rows), 1) // rows_block
    block_at = lax.broadcasted_iota(jnp.int32, (blocks, rows), 0)
    same = (block_of == block_at).astype(bf16)
    before = (block_at < block_of).astype(bf16)
    rank = jnp.dot(named.astype(bf16), before, preferred_element_type=f32)
    cov_rows = jnp.dot(cov.astype(f32).astype(bf16), same, preferred_element_type=f32)
    row_in = lax.broadcasted_iota(jnp.int32, (rows_block, rows), 1) % rows_block
    row_at = lax.broadcasted_iota(jnp.int32, (rows_block, rows), 0)
    head_rows = lax.broadcasted_iota(jnp.int32, (owners, rows), 0).astype(f32)
    at_mark = lax.broadcasted_iota(jnp.int32, (16, rows), 0)
    mark_rows = jnp.zeros((16, rows), f32)
    for t in range(per_block):
        mine = cov_rows[t : t + 1]
        own_rank = jnp.sum(jnp.where(mine == head_rows, rank, 0.0), axis=0, keepdims=True)
        place = own_rank * rows_block + row_in[0:1].astype(f32)
        spread = jnp.dot(lab_ref[t].astype(f32).astype(bf16), same, preferred_element_type=f32)
        label = 1.0 + jnp.sum(jnp.where(row_in == row_at, spread, 0.0), axis=0, keepdims=True)
        mark_rows = jnp.where(at_mark == t, mine, mark_rows)
        mark_rows = jnp.where(at_mark == per_block + t, place, mark_rows)
        mark_rows = jnp.where(at_mark == 2 * per_block + t, label, mark_rows)
    held_ref[rows:, :] = jnp.zeros((16, held_ref.shape[1]), bf16)
    held_ref[rows:, 0:rows] = mark_rows.astype(bf16)
    last = pl.ds(rows, 16)
    stores.append(pltpu.make_async_copy(held_ref.at[last], out_ref.at[last], sems.at[6]))
    stores[-1].start()
    for store in stores:
        store.wait()


def make_shard(own, coverage, labels, owners):
    rows, feature = own.shape
    return pl.pallas_call(
        functools.partial(shard_kernel, owners),
        out_shape=sds((rows + 16, feature), bf16),
        in_specs=[HBM, HBM, HBM],
        out_specs=HBM,
        scratch_shapes=[
            pltpu.VMEM((coverage.shape[1], coverage.shape[0]), jnp.int32),
            pltpu.VMEM((labels.shape[1], labels.shape[2], labels.shape[0]), jnp.int32),
            pltpu.VMEM((rows + 16, feature), bf16),
            pltpu.SemaphoreType.DMA((7,)),
        ],
        compiler_params=params(ROOM),
        name="shard",
    )(coverage.T, labels.transpose(1, 2, 0), own)


def pick_rows(marks, shard, heads, unit, per_block):
    rows = marks.shape[1]
    slot = lax.broadcasted_iota(jnp.int32, (unit, rows), 0).astype(f32)
    at_head = lax.broadcasted_iota(jnp.int32, (8, rows), 0)
    chosen = []
    labels = jnp.zeros((8, rows), f32)
    for k, head in enumerate(heads):
        place = jnp.full((1, rows), -1.0, f32)
        label = jnp.zeros((1, rows), f32)
        for t in range(per_block):
            mine = marks[t : t + 1] == head
            place = jnp.where(mine, marks[per_block + t : per_block + t + 1], place)
            label = jnp.where(mine, marks[2 * per_block + t : 2 * per_block + t + 1], label)
        chosen.append(jnp.where(place == slot, 1.0, 0.0).astype(bf16))
        labels = jnp.where(at_head == k, label, labels)
    chosen = jnp.concatenate(chosen, axis=0)
    picked = jnp.dot(chosen, shard, preferred_element_type=f32).astype(bf16)
    mark = lax.dot_general(
        labels.astype(bf16), chosen, (((1,), (1,)), ((), ())), preferred_element_type=f32
    )
    return picked, mark


def pick_kernel(unit, per_block, plan, n_shards, n_heads, at_ref, *refs):
    shards, refs = refs[:n_shards], refs[n_shards:]
    outs, refs = refs[:n_heads], refs[n_heads:]
    held, ready, in_sems, out_sems = refs
    units = len(plan)
    rows = held.shape[1] - 16

    for g, (yes, no) in enumerate(plan):
        if yes == no:
            pltpu.make_async_copy(shards[yes], held.at[g], in_sems.at[g]).start()
        else:
            flag = at_ref[units * n_heads + g] > 0

            @pl.when(flag)
            def _():
                pltpu.make_async_copy(shards[yes], held.at[g], in_sems.at[g]).start()

            @pl.when(jnp.logical_not(flag))
            def _():
                pltpu.make_async_copy(shards[no], held.at[g], in_sems.at[g]).start()

    at_mark = lax.broadcasted_iota(jnp.int32, (16, unit), 0)
    mark_rows = [jnp.zeros((16, unit), f32)] * n_heads
    for g, (yes, _) in enumerate(plan):
        pltpu.make_async_copy(shards[yes], held.at[g], in_sems.at[g]).wait()
        marks = held[g, rows:, 0:rows].astype(f32)
        wanted = [at_ref[g * n_heads + k].astype(f32) for k in range(n_heads)]
        picked, mark = pick_rows(marks, held[g, 0:rows], wanted, unit, per_block)
        for k in range(n_heads):
            ready[k, g * unit : (g + 1) * unit, :] = picked[k * unit : (k + 1) * unit]
            own_mark = mark[k : k + 1, k * unit : (k + 1) * unit]
            mark_rows[k] = jnp.where(at_mark == g, own_mark, mark_rows[k])
    for k in range(n_heads):
        ready[k, units * unit :, :] = jnp.zeros((16, ready.shape[2]), bf16)
        ready[k, units * unit :, 0:unit] = mark_rows[k].astype(bf16)
        pltpu.make_async_copy(ready.at[k], outs[k], out_sems.at[k]).start()
    for k in range(n_heads):
        pltpu.make_async_copy(ready.at[k], outs[k], out_sems.at[k]).wait()


def pick(unit, per_block, shards, plan, heads_at, flags, cost):
    rows, feature = shards[0].shape
    units = len(plan)
    n_heads = len(heads_at) // units
    size = units * unit + 16
    return pl.pallas_call(
        functools.partial(pick_kernel, unit, per_block, plan, len(shards), n_heads),
        out_shape=[sds((size, feature), bf16)] * n_heads,
        in_specs=[SMEM] + [HBM] * len(shards),
        out_specs=[HBM] * n_heads,
        scratch_shapes=[
            pltpu.VMEM((units, rows, feature), bf16),
            pltpu.VMEM((n_heads, size, feature), bf16),
            pltpu.SemaphoreType.DMA((units,)),
            pltpu.SemaphoreType.DMA((n_heads,)),
        ],
        compiler_params=params(16),
        cost_estimate=spent(cost),
        name="pick",
    )(jnp.stack(heads_at + flags).astype(jnp.int32), *shards)


def pack_kernel(unit, n, *refs):
    parts, out_ref, mark_ref, all_ref, sems = refs[:n], *refs[n:]
    loads = []
    for k in range(n):
        loads.append(
            pltpu.make_async_copy(
                parts[k].at[pl.ds(0, unit)], out_ref.at[pl.ds(k * unit, unit)], sems.at[0, k]
            )
        )
        loads.append(
            pltpu.make_async_copy(
                parts[k].at[pl.ds(unit, 16)], mark_ref.at[k], sems.at[1, k]
            )
        )
    for load in loads:
        load.start()
    for load in loads:
        load.wait()
    at_mark = lax.broadcasted_iota(jnp.int32, (16, unit), 0)
    mark_rows = jnp.zeros((16, unit), f32)
    for k in range(n):
        marks = mark_ref[k, :, 0:unit].astype(f32)
        mark_rows = jnp.where(at_mark == k, marks[0:1], mark_rows)
    all_ref[...] = jnp.zeros(all_ref.shape, bf16)
    all_ref[:, 0:unit] = mark_rows.astype(bf16)
    store = pltpu.make_async_copy(all_ref, out_ref.at[pl.ds(n * unit, 16)], sems.at[0, n])
    store.start()
    store.wait()


def pack(unit, parts):
    feature = parts[0].shape[1]
    n = len(parts)
    return pl.pallas_call(
        functools.partial(pack_kernel, unit, n),
        out_shape=sds((n * unit + 16, feature), bf16),
        in_specs=[HBM] * n,
        out_specs=HBM,
        scratch_shapes=[
            pltpu.VMEM((n, 16, feature), bf16),
            pltpu.VMEM((16, feature), bf16),
            pltpu.SemaphoreType.DMA((2, n + 1)),
        ],
        compiler_params=params(8),
        name="pack",
    )(*parts)


def learn_kernel(unit, spots, n_parts, last, with_total, half_rows, at_ref, *refs):
    parts, refs = refs[:n_parts], refs[n_parts:]
    w_ref, bias_ref, out_ref, refs = refs[0], refs[1], refs[2], refs[3:]
    if with_total:
        total_ref, vec_ref, refs = refs[0], refs[1], refs[2:]
    if last:
        given_ref, new_vec_ref, low_ref, refs = refs[0], refs[1], refs[2], refs[3:]
        rows_ref, wide_ref, mark_ref, target_ref, sems = refs
    else:
        new_total_ref, new_vec_ref, refs = refs[0], refs[1], refs[2:]
        rows_ref, low_ref, mark_ref, target_ref, sems = refs
    low_cut = half_rows // 128 * 128
    rows_all, feature = rows_ref.shape
    loads = []
    for i in range(n_parts):
        loads.append(
            pltpu.make_async_copy(
                parts[i].at[pl.ds(parts[i].shape[0] - 16, 16)], mark_ref.at[i], sems.at[0, i]
            )
        )
    for u, (part, at, _) in enumerate(spots):
        loads.append(
            pltpu.make_async_copy(
                parts[part].at[pl.ds(at, unit)],
                rows_ref.at[pl.ds(u * unit, unit)],
                sems.at[1, u],
            )
        )
    for load in loads:
        load.start()
    for load in loads:
        load.wait()
    eye = lax.broadcasted_iota(jnp.int32, (unit, unit), 0) == lax.broadcasted_iota(
        jnp.int32, (unit, unit), 1
    )
    for u, (part, _, mark_at) in enumerate(spots):
        marks = mark_ref[part, :, 0:unit].astype(f32)[mark_at : mark_at + 1]
        target_ref[u * unit : (u + 1) * unit, :] = jnp.sum(
            jnp.where(eye, marks, 0.0), axis=1, keepdims=True
        ) * at_ref[1].astype(f32)
    bias = bias_ref[...].astype(f32)
    out_weight = out_ref[...].astype(f32)
    step = 2 * unit
    hid = w_ref.shape[1]

    def forward(i, carry):
        span = pl.ds(pl.multiple_of(i * step, step), step)
        pre = jnp.dot(rows_ref[span, :], w_ref[...], preferred_element_type=f32) + bias
        gate = half_sigmoid(pre)
        hidden = pre * gate
        logit = jnp.sum(hidden * out_weight, axis=1, keepdims=True)
        mark = target_ref[span, :]
        residual = jnp.where(mark > 0.5, half_sigmoid(logit) - (mark - 1.0), 0.0)
        grad_pre = residual * out_weight * gate * (1.0 + pre * (1.0 - gate))
        low_ref[span, :] = grad_pre.astype(bf16)
        return (
            carry[0] + jnp.sum(grad_pre, axis=0, keepdims=True),
            carry[1] + jnp.sum(residual * hidden, axis=0, keepdims=True),
        )

    if with_total:
        start = (vec_ref[0:1, :], vec_ref[1:2, :])
    else:
        start = (jnp.zeros((1, hid), f32), jnp.zeros((1, hid), f32))
    grad_bias, grad_out = lax.fori_loop(0, rows_all // step, forward, start)

    def product(first, size):
        piece = lax.dot_general(
            rows_ref[:, first : first + size],
            low_ref[...],
            (((0,), (0,)), ((), ())),
            preferred_element_type=f32,
        )
        if with_total:
            piece = piece + total_ref[first : first + size, :]
        return piece

    tile = 128 * max(n for n in range(1, 5) if feature % (128 * n) == 0)
    if not last:
        for first in range(0, feature, tile):
            new_total_ref[first : first + tile, :] = product(first, tile)
        new_vec_ref[0:1, :] = grad_bias
        new_vec_ref[1:2, :] = grad_out
        return
    first = pl.multiple_of((1 - at_ref[0]) * low_cut, 128)
    skip = pl.multiple_of((1 - at_ref[0]) * (half_rows - low_cut), 8)
    wide_ref[...] = lax.dot_general(
        rows_ref[:, pl.ds(first, feature - low_cut)],
        low_ref[...],
        (((0,), (0,)), ((), ())),
        preferred_element_type=f32,
    )
    other = pl.multiple_of((1 - at_ref[0]) * half_rows, 8)
    given_ref[0:half_rows, :] = (
        wide_ref[pl.ds(skip, half_rows), :] + total_ref[pl.ds(other, half_rows), :]
    )
    given_ref[half_rows : half_rows + 8, :] = jnp.zeros((8, hid), f32)
    given_ref[half_rows : half_rows + 1, :] = grad_bias
    given_ref[half_rows + 1 : half_rows + 2, :] = grad_out
    new_vec_ref[0:1, :] = grad_bias
    new_vec_ref[1:2, :] = grad_out


def keep_kernel(half_rows, low_cut, unit, spots, n_parts, at_ref, *refs):
    parts, (low_ref, total_ref, out_ref, rows_ref, wide_ref, sems) = refs[:n_parts], refs[n_parts:]
    feature = rows_ref.shape[1]
    loads = []
    for u, (part, at, _) in enumerate(spots):
        loads.append(
            pltpu.make_async_copy(
                parts[part].at[pl.ds(at, unit)], rows_ref.at[pl.ds(u * unit, unit)], sems.at[u]
            )
        )
    for load in loads:
        load.start()
    for load in loads:
        load.wait()
    first = pl.multiple_of(at_ref[0] * low_cut, 128)
    skip = pl.multiple_of(at_ref[0] * (half_rows - low_cut), 8)
    wide_ref[...] = lax.dot_general(
        rows_ref[:, pl.ds(first, feature - low_cut)],
        low_ref[...],
        (((0,), (0,)), ((), ())),
        preferred_element_type=f32,
    )
    own = pl.multiple_of(at_ref[0] * half_rows, 8)
    out_ref[...] = wide_ref[pl.ds(skip, half_rows), :] + total_ref[pl.ds(own, half_rows), :]


def keep(unit, spots, parts, at, low, total):
    feature, hid = total.shape
    half = feature // 2
    low_cut = half // 128 * 128
    return pl.pallas_call(
        functools.partial(keep_kernel, half, low_cut, unit, spots, len(parts)),
        out_shape=sds((half, hid), f32),
        in_specs=[SMEM] + [HBM] * len(parts) + [VMEM, VMEM],
        out_specs=VMEM,
        scratch_shapes=[
            pltpu.VMEM((low.shape[0], feature), bf16),
            pltpu.VMEM((feature - low_cut, hid), f32),
            pltpu.SemaphoreType.DMA((len(spots),)),
        ],
        compiler_params=params(16),
        cost_estimate=spent(2),
        name="keep",
    )(at, *parts, low, total)


def learn(unit, spots, parts, at, w, bias, out, total, cost, last):
    feature, hid = w.shape
    rows_all = len(spots) * unit
    half = feature // 2
    if last:
        outs = (sds((half + 8, hid), f32), sds((2, hid), f32), sds((rows_all, hid), bf16))
        work = pltpu.VMEM((feature - half // 128 * 128, hid), f32)
    else:
        outs = (sds((feature, hid), f32), sds((2, hid), f32))
        work = pltpu.VMEM((rows_all, hid), bf16)
    extra = () if total is None else total
    kernel = functools.partial(
        learn_kernel, unit, spots, len(parts), last, total is not None, half
    )
    return pl.pallas_call(
        kernel,
        out_shape=outs,
        in_specs=[SMEM] + [HBM] * len(parts) + [VMEM] * (3 + len(extra)),
        out_specs=(VMEM,) * len(outs),
        scratch_shapes=[
            pltpu.VMEM((rows_all, feature), bf16),
            work,
            pltpu.VMEM((len(parts), 16, feature), bf16),
            pltpu.VMEM((rows_all, 1), f32),
            pltpu.SemaphoreType.DMA((2, max(len(parts), len(spots)))),
        ],
        compiler_params=params(24),
        cost_estimate=spent(cost),
        name="learn",
    )(at, *parts, w, bias, out, *extra)


def adam(old, grad, first, second):
    new_first = beta_one * first + (1.0 - beta_one) * grad
    new_second = beta_two * second + (1.0 - beta_two) * grad * grad
    new = old - learn_rate * new_first / (jnp.sqrt(new_second) + epsilon)
    return new.astype(bf16), new_first, new_second


def step_kernel(
    at_ref, kept, got, kept_vec, got_vec, w, first_w, second_w, vec_old, first_vec, second_vec,
    new_half, new_full, new_vec, new_first_w, new_second_w, new_first_vec, new_second_vec,
):
    new, new_first, new_second = adam(
        w[...].astype(f32), kept[...] + got[...], first_w[0], second_w[0]
    )
    new_half[...] = new
    new_full[0] = new
    new_first_w[0] = new_first
    new_second_w[0] = new_second

    @pl.when(pl.program_id(0) == 0)
    def _():
        grad = kept_vec[...] + got_vec[0:2, :]
        fresh, fresh_first, fresh_second = adam(
            vec_old[...].astype(f32), grad, first_vec[0], second_vec[0]
        )
        new_vec[0] = fresh
        new_first_vec[0] = fresh_first
        new_second_vec[0] = fresh_second


def take_step(rep, kept, kept_vec, got, w_in, vec_old, first_w, second_w, first_vec, second_vec):
    feature, hid = w_in.shape
    half = feature // 2
    tiles = max(n for n in range(1, 5) if half % (16 * n) == 0)
    tile = half // tiles
    here = pl.BlockSpec((tile, hid), lambda i, at: (i, 0))
    there = pl.BlockSpec((tile, hid), lambda i, at: (at[0] * tiles + i, 0))
    tail = pl.BlockSpec((8, hid), lambda i, at: (half // 8, 0))
    moment = pl.BlockSpec((1, tile, hid), lambda i, at: (0, i, 0))
    pair = pl.BlockSpec((2, hid), lambda i, at: (0, 0))
    pairs = pl.BlockSpec((1, 2, hid), lambda i, at: (0, 0, 0))
    full = pl.BlockSpec((1, tile, hid), lambda i, at: (0, at[0] * tiles + i, 0))
    return pl.pallas_call(
        step_kernel,
        grid_spec=pltpu.PrefetchScalarGridSpec(
            num_scalar_prefetch=1,
            grid=(tiles,),
            in_specs=[here, here, pair, tail, there, moment, moment, pair, pairs, pairs],
            out_specs=[here, full, pairs, moment, moment, pairs, pairs],
        ),
        out_shape=(
            sds((half, hid), bf16),
            sds((1, feature, hid), bf16),
            sds((1, 2, hid), bf16),
            sds((1, half, hid), f32),
            sds((1, half, hid), f32),
            sds((1, 2, hid), f32),
            sds((1, 2, hid), f32),
        ),
        compiler_params=params(16),
        name="step",
    )(rep, kept, got, kept_vec, got, w_in, first_w, second_w, vec_old, first_vec, second_vec)


def join_kernel(at_ref, other_ref, full_ref, out_ref, sem):
    half = other_ref.shape[0]
    start = pl.multiple_of((1 - at_ref[0]) * half, half)
    load = pltpu.make_async_copy(other_ref, out_ref.at[0, pl.ds(start, half)], sem)
    load.start()
    load.wait()


def join(rep, other, full):
    return pl.pallas_call(
        join_kernel,
        out_shape=sds(full.shape, full.dtype),
        in_specs=[SMEM, ANY, ANY],
        out_specs=ANY,
        scratch_shapes=[pltpu.SemaphoreType.DMA(())],
        input_output_aliases={2: 0},
        compiler_params=params(8),
        name="join",
    )(rep, other, full)


def gathered(
    embeddings, coverage, labels, w_in, bias_in, w_out, first_w, second_w, first_vec, second_vec
):
    planes = lax.axis_size("dp")
    heads = lax.axis_size("head")
    owners = planes * heads
    z = lax.axis_index("dp")
    q = lax.axis_index("head")
    rep = lax.axis_index("rep").reshape(1)
    blocks, rows_block, feature = embeddings.shape
    per_block = coverage.shape[1]
    slots = 2 * blocks * per_block // owners
    unit = slots * rows_block
    rows = blocks * rows_block
    def right_pairs(hop):
        return [(i, i + 1) for i in range(hop - 1, planes - 1)]

    def left_pairs(hop):
        return [(i + 1, i) for i in range(planes - hop)]

    def exchange(units):
        return [units[0]] + [
            lax.ppermute(units[k], "head", [(i, i ^ k) for i in range(heads)])
            for k in range(1, heads)
        ]

    def plane_heads(plane, real=None):
        found = [plane * heads + (q ^ k) for k in range(heads)]
        return found if real is None else [jnp.where(real, h, -1) for h in found]

    own = make_shard(embeddings.reshape(rows, feature), coverage, labels, owners)
    right = lax.ppermute(own, "dp", right_pairs(1))
    left = lax.ppermute(own, "dp", left_pairs(1))
    always = jnp.ones((), jnp.bool_)
    at_end = (z == 0) | (z == planes - 1)

    def add(total, parts, spots, real, cost, last=False):
        scalars = jnp.stack([rep[0], real]).astype(jnp.int32)
        return learn(unit, spots, parts, scalars, w_in[0], bias_in, w_out, total, cost, last)

    first_heads = plane_heads(jnp.where(at_end, planes - 1 - z, z))
    first_units = exchange(pick(unit, per_block, [own], [(0, 0)], first_heads, [always], 0))
    far_sent = pack(unit, first_units)
    one = jnp.ones((), jnp.int32)
    first_spots = [(k, 0, 0) for k in range(heads)]
    middle = 1 - at_end.astype(jnp.int32)
    rest = []
    for hop in range(1, planes - 1):
        from_left = z >= hop
        from_right = z + hop < planes
        if hop + 1 < planes - 1:
            right, left, far_sent = lax.optimization_barrier((right, left, far_sent))
            next_right = lax.ppermute(right, "dp", right_pairs(hop + 1))
            next_left = lax.ppermute(left, "dp", left_pairs(hop + 1))
        else:
            next_right, next_left = None, None
        if hop == planes - 2 and hop > 1:
            far_sent, right, left, grad, vec = lax.optimization_barrier(
                (far_sent, right, left, *total)
            )
            total = (grad, vec)
            ends = [(0, planes - 1), (planes - 1, 0)]
            far_got = lax.ppermute(far_sent, "dp", ends)
        if 2 * hop < planes:
            fill = hop == 1
            messages = pick(
                unit,
                per_block,
                [right, left, own],
                [(0, 2), (1, 2)],
                plane_heads(z, from_left | fill) + plane_heads(z, from_right | fill),
                [from_left, from_right],
                PB,
            )
            units = 2
        else:
            messages = pick(
                unit,
                per_block,
                [left, right],
                [(0, 1)],
                plane_heads(z, from_left | from_right),
                [from_right],
                PC,
            )
            units = 1
        where = [(k, g * unit, g) for k in range(heads) for g in range(units)]
        if hop == 1:
            first_units = lax.optimization_barrier((*first_units, *messages))[:heads]
            total = add(None, first_units, first_spots, middle, LA)
        else:
            messages = lax.optimization_barrier((*messages, *rest[-1][0]))[:heads]
        rest.append((exchange(messages), where))
        right, left = next_right, next_left
    rest.append(([far_got], [(0, k * unit, k) for k in range(heads)]))

    for at, (parts, spots) in enumerate(rest):
        cost = (LB, LC, LF)[min(at, 2)]
        last = at == len(rest) - 1
        done, total = total, add(total, parts, spots, one, cost, last)
    given, kept_vec, low = total
    got = lax.ppermute(given, "rep", swap)
    kept = keep(unit, spots, parts, rep, low, done[0])
    vec_old = jnp.concatenate([bias_in, w_out])
    new_half, new_full, new_vec, nfw, nsw, nfv, nsv = take_step(
        rep, kept, kept_vec, got, w_in[0], vec_old, first_w, second_w, first_vec, second_vec
    )
    new_w_in = join(rep, lax.ppermute(new_half, "rep", swap), new_full)
    return new_w_in, new_vec, nfw, nsw, nfv, nsv


def routed(
    embeddings, coverage, labels, w_in, bias_in, w_out, first_w, second_w, first_vec, second_vec
):
    dp_count = lax.axis_size("dp")
    head_count = lax.axis_size("head")
    owners = dp_count * head_count
    block_count, rows_block, feature = embeddings.shape
    per_block = coverage.shape[1]
    slot_count = 2 * block_count * per_block // owners
    entries = block_count * per_block
    heads_flat = coverage.reshape(entries)
    onehot = (heads_flat[:, None] == jnp.arange(owners, dtype=jnp.int32)[None, :]).astype(jnp.int32)
    slot_rank = jnp.sum((jnp.cumsum(onehot, axis=0) - 1) * onehot, axis=1)
    target_slot = heads_flat * slot_count + slot_rank
    picker = jnp.arange(owners * slot_count, dtype=jnp.int32)[:, None] == target_slot[None, :]
    block_pick = jnp.sum(
        picker.reshape(owners * slot_count, block_count, per_block).astype(jnp.int32), axis=2
    ).astype(jnp.bfloat16)
    send_rows = jnp.dot(
        block_pick,
        embeddings.reshape(block_count, rows_block * feature),
        preferred_element_type=jnp.float32,
    ).astype(jnp.bfloat16)
    label_marks = (labels.reshape(entries, rows_block) + 1).astype(jnp.float32)
    send_marks = jnp.dot(
        picker.astype(jnp.float32), label_marks, precision=lax.Precision.HIGHEST
    ).astype(jnp.bfloat16)
    direct_rows = send_rows.reshape(owners, slot_count, rows_block, feature)
    direct_marks = send_marks.reshape(owners, slot_count, rows_block)
    got_rows, got_marks = (
        lax.all_to_all(direct_rows, ("dp", "head"), split_axis=0, concat_axis=0, tiled=True),
        lax.all_to_all(direct_marks, ("dp", "head"), split_axis=0, concat_axis=0, tiled=True),
    )
    row_data = got_rows.reshape(-1, feature)
    marks_all = got_marks.reshape(-1).astype(jnp.float32)
    usable = marks_all > 0.5
    target = marks_all - 1.0
    out_weight = w_out[0].astype(jnp.float32)
    pre_act = (
        jnp.dot(row_data, w_in[0], preferred_element_type=jnp.float32)
        + bias_in[0].astype(jnp.float32)[None, :]
    )
    sig_pre = jax.nn.sigmoid(pre_act)
    hidden = pre_act * sig_pre
    logits = jnp.sum(hidden * out_weight[None, :], axis=1)
    residual = jnp.where(usable, jax.nn.sigmoid(logits) - target, jnp.zeros_like(logits))
    grad_pre = residual[:, None] * out_weight[None, :] * sig_pre * (1.0 + pre_act * (1.0 - sig_pre))
    grad_low = grad_pre.astype(jnp.bfloat16)
    vec_part = jnp.stack([jnp.sum(grad_pre, axis=0), jnp.sum(residual[:, None] * hidden, axis=0)])
    half_rows = feature // lax.axis_size("rep")
    rep_at = lax.axis_index("rep")
    first_row = rep_at * half_rows
    grad_part = lax.dot_general(
        row_data, grad_low, (((0,), (0,)), ((), ())), preferred_element_type=jnp.float32
    ).reshape(2, half_rows, -1)
    kept = jnp.where(rep_at == 0, grad_part[0], grad_part[1])
    given = jnp.where(rep_at == 0, grad_part[1], grad_part[0])
    grad_w = kept + lax.ppermute(given, "rep", swap)
    grad_vec = vec_part + lax.ppermute(vec_part, "rep", swap)
    new_first_w = beta_one * first_w[0] + (1.0 - beta_one) * grad_w
    new_second_w = beta_two * second_w[0] + (1.0 - beta_two) * grad_w * grad_w
    old_rows = lax.dynamic_slice_in_dim(w_in[0], first_row, half_rows, 0).astype(jnp.float32)
    new_half = (old_rows - learn_rate * new_first_w / (jnp.sqrt(new_second_w) + epsilon)).astype(
        jnp.bfloat16
    )
    other_half = lax.ppermute(new_half, "rep", swap)
    new_w_in = jnp.where(
        rep_at == 0,
        jnp.concatenate([new_half, other_half]),
        jnp.concatenate([other_half, new_half]),
    )
    vector = jnp.stack([bias_in[0], w_out[0]]).astype(jnp.float32)
    new_first_vec = beta_one * first_vec[0] + (1.0 - beta_one) * grad_vec
    new_second_vec = beta_two * second_vec[0] + (1.0 - beta_two) * grad_vec * grad_vec
    new_vec = (vector - learn_rate * new_first_vec / (jnp.sqrt(new_second_vec) + epsilon)).astype(
        jnp.bfloat16
    )
    return (
        new_w_in[None],
        new_vec[None],
        new_first_w[None],
        new_second_w[None],
        new_first_vec[None],
        new_second_vec[None],
    )


def solution(mesh):
    placed = (
        P(("dp", "head", "rep"), None, None),
        P(("dp", "head", "rep"), None),
        P(("dp", "head", "rep"), None, None),
        P(("dp", "head"), None, None),
        P(("dp", "head"), None),
        P(("dp", "head"), None),
        P(("dp", "head"), "rep", None),
        P(("dp", "head"), "rep", None),
        P(("dp", "head"), None, None),
        P(("dp", "head"), None, None),
    )
    planes, heads, reps = mesh.shape["dp"], mesh.shape["head"], mesh.shape["rep"]
    short = 3 < planes <= heads and heads & (heads - 1) == 0 and reps == 2
    return jax.shard_map(
        gathered if short else routed,
        mesh=mesh,
        in_specs=placed,
        out_specs=(
            P(("dp", "head"), None, None),
            P(("dp", "head"), None, None),
            P(("dp", "head"), "rep", None),
            P(("dp", "head"), "rep", None),
            P(("dp", "head"), None, None),
            P(("dp", "head"), None, None),
        ),
        check_vma=False,
    )
```

```python
import functools

import jax
import jax.numpy as jnp
from jax import lax
from jax.experimental import pallas as pl
from jax.experimental.pallas import tpu as pltpu
from jax.sharding import PartitionSpec as P

beta_one = 0.9
beta_two = 0.999
learn_rate = 0.001
epsilon = 1e-08
swap = [(0, 1), (1, 0)]
PB, PC, LA, LB, LC, LF = (0, 10, 0, 40, 20, 0)
bf16 = jnp.bfloat16
MIB = 1024 * 1024
ROOM = 60
ANY = pl.BlockSpec(memory_space=pl.ANY)
VMEM = pl.BlockSpec(memory_space=pltpu.VMEM)
HBM = pl.BlockSpec(memory_space=pltpu.HBM)
SMEM = pl.BlockSpec(memory_space=pltpu.SMEM)
f32 = jnp.float32


def spent(us):
    return pl.CostEstimate(flops=int(us * 1150000000) + 1, bytes_accessed=1, transcendentals=0)


def params(mib):
    return pltpu.CompilerParams(vmem_limit_bytes=mib * MIB)


def sds(shape, dtype):
    return jax.ShapeDtypeStruct(shape, dtype)


def half_sigmoid(x):
    return 0.5 * jnp.tanh(0.5 * x) + 0.5


def shard_kernel(owners, cov_hbm, lab_hbm, own_ref, out_ref, cov_ref, lab_ref, held_ref, sems):
    per_block, blocks = cov_ref.shape
    rows_block = lab_ref.shape[1]
    rows = blocks * rows_block
    load_cov = pltpu.make_async_copy(cov_hbm, cov_ref, sems.at[0])
    load_lab = pltpu.make_async_copy(lab_hbm, lab_ref, sems.at[1])
    half = rows // 2
    loads = []
    stores = []
    for i in range(2):
        part = pl.ds(i * half, half)
        loads.append(pltpu.make_async_copy(own_ref.at[part], held_ref.at[part], sems.at[2 + i]))
        stores.append(pltpu.make_async_copy(held_ref.at[part], out_ref.at[part], sems.at[4 + i]))
    load_cov.start()
    load_lab.start()
    for load in loads:
        load.start()
    for load, store in zip(loads, stores):
        load.wait()
        store.start()
    load_cov.wait()
    load_lab.wait()
    cov = cov_ref[...]
    heads_at = lax.broadcasted_iota(jnp.int32, (owners, blocks), 0)
    named = (cov[0:1] == heads_at).astype(f32)
    for t in range(1, per_block):
        named = named + (cov[t : t + 1] == heads_at).astype(f32)
    block_of = lax.broadcasted_iota(jnp.int32, (blocks, rows), 1) // rows_block
    block_at = lax.broadcasted_iota(jnp.int32, (blocks, rows), 0)
    same = (block_of == block_at).astype(bf16)
    before = (block_at < block_of).astype(bf16)
    rank = jnp.dot(named.astype(bf16), before, preferred_element_type=f32)
    cov_rows = jnp.dot(cov.astype(f32).astype(bf16), same, preferred_element_type=f32)
    row_in = lax.broadcasted_iota(jnp.int32, (rows_block, rows), 1) % rows_block
    row_at = lax.broadcasted_iota(jnp.int32, (rows_block, rows), 0)
    head_rows = lax.broadcasted_iota(jnp.int32, (owners, rows), 0).astype(f32)
    at_mark = lax.broadcasted_iota(jnp.int32, (16, rows), 0)
    mark_rows = jnp.zeros((16, rows), f32)
    for t in range(per_block):
        mine = cov_rows[t : t + 1]
        own_rank = jnp.sum(jnp.where(mine == head_rows, rank, 0.0), axis=0, keepdims=True)
        place = own_rank * rows_block + row_in[0:1].astype(f32)
        spread = jnp.dot(lab_ref[t].astype(f32).astype(bf16), same, preferred_element_type=f32)
        label = 1.0 + jnp.sum(jnp.where(row_in == row_at, spread, 0.0), axis=0, keepdims=True)
        mark_rows = jnp.where(at_mark == t, mine, mark_rows)
        mark_rows = jnp.where(at_mark == per_block + t, place, mark_rows)
        mark_rows = jnp.where(at_mark == 2 * per_block + t, label, mark_rows)
    held_ref[rows:, :] = jnp.zeros((16, held_ref.shape[1]), bf16)
    held_ref[rows:, 0:rows] = mark_rows.astype(bf16)
    last = pl.ds(rows, 16)
    stores.append(pltpu.make_async_copy(held_ref.at[last], out_ref.at[last], sems.at[6]))
    stores[-1].start()
    for store in stores:
        store.wait()


def make_shard(own, coverage, labels, owners):
    rows, feature = own.shape
    return pl.pallas_call(
        functools.partial(shard_kernel, owners),
        out_shape=sds((rows + 16, feature), bf16),
        in_specs=[HBM, HBM, HBM],
        out_specs=HBM,
        scratch_shapes=[
            pltpu.VMEM((coverage.shape[1], coverage.shape[0]), jnp.int32),
            pltpu.VMEM((labels.shape[1], labels.shape[2], labels.shape[0]), jnp.int32),
            pltpu.VMEM((rows + 16, feature), bf16),
            pltpu.SemaphoreType.DMA((7,)),
        ],
        compiler_params=params(ROOM),
        name="shard",
    )(coverage.T, labels.transpose(1, 2, 0), own)


def pick_rows(marks, shard, heads, unit, per_block):
    rows = marks.shape[1]
    slot = lax.broadcasted_iota(jnp.int32, (unit, rows), 0).astype(f32)
    at_head = lax.broadcasted_iota(jnp.int32, (8, rows), 0)
    chosen = []
    labels = jnp.zeros((8, rows), f32)
    for k, head in enumerate(heads):
        place = jnp.full((1, rows), -1.0, f32)
        label = jnp.zeros((1, rows), f32)
        for t in range(per_block):
            mine = marks[t : t + 1] == head
            place = jnp.where(mine, marks[per_block + t : per_block + t + 1], place)
            label = jnp.where(mine, marks[2 * per_block + t : 2 * per_block + t + 1], label)
        chosen.append(jnp.where(place == slot, 1.0, 0.0).astype(bf16))
        labels = jnp.where(at_head == k, label, labels)
    chosen = jnp.concatenate(chosen, axis=0)
    picked = jnp.dot(chosen, shard, preferred_element_type=f32).astype(bf16)
    mark = lax.dot_general(
        labels.astype(bf16), chosen, (((1,), (1,)), ((), ())), preferred_element_type=f32
    )
    return picked, mark


def pick_kernel(unit, per_block, plan, n_shards, n_heads, at_ref, *refs):
    shards, refs = refs[:n_shards], refs[n_shards:]
    outs, refs = refs[:n_heads], refs[n_heads:]
    held, ready, in_sems, out_sems = refs
    units = len(plan)
    rows = held.shape[1] - 16

    for g, (yes, no) in enumerate(plan):
        if yes == no:
            pltpu.make_async_copy(shards[yes], held.at[g], in_sems.at[g]).start()
        else:
            flag = at_ref[units * n_heads + g] > 0

            @pl.when(flag)
            def _():
                pltpu.make_async_copy(shards[yes], held.at[g], in_sems.at[g]).start()

            @pl.when(jnp.logical_not(flag))
            def _():
                pltpu.make_async_copy(shards[no], held.at[g], in_sems.at[g]).start()

    at_mark = lax.broadcasted_iota(jnp.int32, (16, unit), 0)
    mark_rows = [jnp.zeros((16, unit), f32)] * n_heads
    for g, (yes, _) in enumerate(plan):
        pltpu.make_async_copy(shards[yes], held.at[g], in_sems.at[g]).wait()
        marks = held[g, rows:, 0:rows].astype(f32)
        wanted = [at_ref[g * n_heads + k].astype(f32) for k in range(n_heads)]
        picked, mark = pick_rows(marks, held[g, 0:rows], wanted, unit, per_block)
        for k in range(n_heads):
            ready[k, g * unit : (g + 1) * unit, :] = picked[k * unit : (k + 1) * unit]
            own_mark = mark[k : k + 1, k * unit : (k + 1) * unit]
            mark_rows[k] = jnp.where(at_mark == g, own_mark, mark_rows[k])
    for k in range(n_heads):
        ready[k, units * unit :, :] = jnp.zeros((16, ready.shape[2]), bf16)
        ready[k, units * unit :, 0:unit] = mark_rows[k].astype(bf16)
        pltpu.make_async_copy(ready.at[k], outs[k], out_sems.at[k]).start()
    for k in range(n_heads):
        pltpu.make_async_copy(ready.at[k], outs[k], out_sems.at[k]).wait()


def pick(unit, per_block, shards, plan, heads_at, flags, cost):
    rows, feature = shards[0].shape
    units = len(plan)
    n_heads = len(heads_at) // units
    size = units * unit + 16
    return pl.pallas_call(
        functools.partial(pick_kernel, unit, per_block, plan, len(shards), n_heads),
        out_shape=[sds((size, feature), bf16)] * n_heads,
        in_specs=[SMEM] + [HBM] * len(shards),
        out_specs=[HBM] * n_heads,
        scratch_shapes=[
            pltpu.VMEM((units, rows, feature), bf16),
            pltpu.VMEM((n_heads, size, feature), bf16),
            pltpu.SemaphoreType.DMA((units,)),
            pltpu.SemaphoreType.DMA((n_heads,)),
        ],
        compiler_params=params(16),
        cost_estimate=spent(cost),
        name="pick",
    )(jnp.stack(heads_at + flags).astype(jnp.int32), *shards)


def pack_kernel(unit, n, *refs):
    parts, out_ref, mark_ref, all_ref, sems = refs[:n], *refs[n:]
    loads = []
    for k in range(n):
        loads.append(
            pltpu.make_async_copy(
                parts[k].at[pl.ds(0, unit)], out_ref.at[pl.ds(k * unit, unit)], sems.at[0, k]
            )
        )
        loads.append(
            pltpu.make_async_copy(
                parts[k].at[pl.ds(unit, 16)], mark_ref.at[k], sems.at[1, k]
            )
        )
    for load in loads:
        load.start()
    for load in loads:
        load.wait()
    at_mark = lax.broadcasted_iota(jnp.int32, (16, unit), 0)
    mark_rows = jnp.zeros((16, unit), f32)
    for k in range(n):
        marks = mark_ref[k, :, 0:unit].astype(f32)
        mark_rows = jnp.where(at_mark == k, marks[0:1], mark_rows)
    all_ref[...] = jnp.zeros(all_ref.shape, bf16)
    all_ref[:, 0:unit] = mark_rows.astype(bf16)
    store = pltpu.make_async_copy(all_ref, out_ref.at[pl.ds(n * unit, 16)], sems.at[0, n])
    store.start()
    store.wait()


def pack(unit, parts):
    feature = parts[0].shape[1]
    n = len(parts)
    return pl.pallas_call(
        functools.partial(pack_kernel, unit, n),
        out_shape=sds((n * unit + 16, feature), bf16),
        in_specs=[HBM] * n,
        out_specs=HBM,
        scratch_shapes=[
            pltpu.VMEM((n, 16, feature), bf16),
            pltpu.VMEM((16, feature), bf16),
            pltpu.SemaphoreType.DMA((2, n + 1)),
        ],
        compiler_params=params(8),
        name="pack",
    )(*parts)


def learn_kernel(unit, spots, n_parts, last, with_total, half_rows, at_ref, *refs):
    parts, refs = refs[:n_parts], refs[n_parts:]
    w_ref, bias_ref, out_ref, refs = refs[0], refs[1], refs[2], refs[3:]
    if with_total:
        total_ref, vec_ref, refs = refs[0], refs[1], refs[2:]
    if last:
        given_ref, new_vec_ref, low_ref, refs = refs[0], refs[1], refs[2], refs[3:]
        rows_ref, wide_ref, mark_ref, target_ref, sems = refs
    else:
        new_total_ref, new_vec_ref, refs = refs[0], refs[1], refs[2:]
        rows_ref, low_ref, mark_ref, target_ref, sems = refs
    low_cut = half_rows // 128 * 128
    rows_all, feature = rows_ref.shape
    loads = []
    for i in range(n_parts):
        loads.append(
            pltpu.make_async_copy(
                parts[i].at[pl.ds(parts[i].shape[0] - 16, 16)], mark_ref.at[i], sems.at[0, i]
            )
        )
    for u, (part, at, _) in enumerate(spots):
        loads.append(
            pltpu.make_async_copy(
                parts[part].at[pl.ds(at, unit)],
                rows_ref.at[pl.ds(u * unit, unit)],
                sems.at[1, u],
            )
        )
    for load in loads:
        load.start()
    for load in loads:
        load.wait()
    eye = lax.broadcasted_iota(jnp.int32, (unit, unit), 0) == lax.broadcasted_iota(
        jnp.int32, (unit, unit), 1
    )
    for u, (part, _, mark_at) in enumerate(spots):
        marks = mark_ref[part, :, 0:unit].astype(f32)[mark_at : mark_at + 1]
        target_ref[u * unit : (u + 1) * unit, :] = jnp.sum(
            jnp.where(eye, marks, 0.0), axis=1, keepdims=True
        ) * at_ref[1].astype(f32)
    bias = bias_ref[...].astype(f32)
    out_weight = out_ref[...].astype(f32)
    step = 2 * unit
    hid = w_ref.shape[1]

    def forward(i, carry):
        span = pl.ds(pl.multiple_of(i * step, step), step)
        pre = jnp.dot(rows_ref[span, :], w_ref[...], preferred_element_type=f32) + bias
        gate = half_sigmoid(pre)
        hidden = pre * gate
        logit = jnp.sum(hidden * out_weight, axis=1, keepdims=True)
        mark = target_ref[span, :]
        residual = jnp.where(mark > 0.5, half_sigmoid(logit) - (mark - 1.0), 0.0)
        grad_pre = residual * out_weight * gate * (1.0 + pre * (1.0 - gate))
        low_ref[span, :] = grad_pre.astype(bf16)
        return (
            carry[0] + jnp.sum(grad_pre, axis=0, keepdims=True),
            carry[1] + jnp.sum(residual * hidden, axis=0, keepdims=True),
        )

    if with_total:
        start = (vec_ref[0:1, :], vec_ref[1:2, :])
    else:
        start = (jnp.zeros((1, hid), f32), jnp.zeros((1, hid), f32))
    grad_bias, grad_out = lax.fori_loop(0, rows_all // step, forward, start)

    def product(first, size):
        piece = lax.dot_general(
            rows_ref[:, first : first + size],
            low_ref[...],
            (((0,), (0,)), ((), ())),
            preferred_element_type=f32,
        )
        if with_total:
            piece = piece + total_ref[first : first + size, :]
        return piece

    tile = 128 * max(n for n in range(1, 5) if feature % (128 * n) == 0)
    if not last:
        for first in range(0, feature, tile):
            new_total_ref[first : first + tile, :] = product(first, tile)
        new_vec_ref[0:1, :] = grad_bias
        new_vec_ref[1:2, :] = grad_out
        return
    first = pl.multiple_of((1 - at_ref[0]) * low_cut, 128)
    skip = pl.multiple_of((1 - at_ref[0]) * (half_rows - low_cut), 8)
    wide_ref[...] = lax.dot_general(
        rows_ref[:, pl.ds(first, feature - low_cut)],
        low_ref[...],
        (((0,), (0,)), ((), ())),
        preferred_element_type=f32,
    )
    other = pl.multiple_of((1 - at_ref[0]) * half_rows, 8)
    given_ref[0:half_rows, :] = (
        wide_ref[pl.ds(skip, half_rows), :] + total_ref[pl.ds(other, half_rows), :]
    )
    given_ref[half_rows : half_rows + 8, :] = jnp.zeros((8, hid), f32)
    given_ref[half_rows : half_rows + 1, :] = grad_bias
    given_ref[half_rows + 1 : half_rows + 2, :] = grad_out
    new_vec_ref[0:1, :] = grad_bias
    new_vec_ref[1:2, :] = grad_out


def keep_kernel(half_rows, low_cut, unit, spots, n_parts, at_ref, *refs):
    parts, (low_ref, total_ref, out_ref, rows_ref, wide_ref, sems) = refs[:n_parts], refs[n_parts:]
    feature = rows_ref.shape[1]
    loads = []
    for u, (part, at, _) in enumerate(spots):
        loads.append(
            pltpu.make_async_copy(
                parts[part].at[pl.ds(at, unit)], rows_ref.at[pl.ds(u * unit, unit)], sems.at[u]
            )
        )
    for load in loads:
        load.start()
    for load in loads:
        load.wait()
    first = pl.multiple_of(at_ref[0] * low_cut, 128)
    skip = pl.multiple_of(at_ref[0] * (half_rows - low_cut), 8)
    wide_ref[...] = lax.dot_general(
        rows_ref[:, pl.ds(first, feature - low_cut)],
        low_ref[...],
        (((0,), (0,)), ((), ())),
        preferred_element_type=f32,
    )
    own = pl.multiple_of(at_ref[0] * half_rows, 8)
    out_ref[...] = wide_ref[pl.ds(skip, half_rows), :] + total_ref[pl.ds(own, half_rows), :]


def keep(unit, spots, parts, at, low, total):
    feature, hid = total.shape
    half = feature // 2
    low_cut = half // 128 * 128
    return pl.pallas_call(
        functools.partial(keep_kernel, half, low_cut, unit, spots, len(parts)),
        out_shape=sds((half, hid), f32),
        in_specs=[SMEM] + [HBM] * len(parts) + [VMEM, VMEM],
        out_specs=VMEM,
        scratch_shapes=[
            pltpu.VMEM((low.shape[0], feature), bf16),
            pltpu.VMEM((feature - low_cut, hid), f32),
            pltpu.SemaphoreType.DMA((len(spots),)),
        ],
        compiler_params=params(16),
        cost_estimate=spent(2),
        name="keep",
    )(at, *parts, low, total)


def learn(unit, spots, parts, at, w, bias, out, total, cost, last):
    feature, hid = w.shape
    rows_all = len(spots) * unit
    half = feature // 2
    if last:
        outs = (sds((half + 8, hid), f32), sds((2, hid), f32), sds((rows_all, hid), bf16))
        work = pltpu.VMEM((feature - half // 128 * 128, hid), f32)
    else:
        outs = (sds((feature, hid), f32), sds((2, hid), f32))
        work = pltpu.VMEM((rows_all, hid), bf16)
    extra = () if total is None else total
    kernel = functools.partial(
        learn_kernel, unit, spots, len(parts), last, total is not None, half
    )
    return pl.pallas_call(
        kernel,
        out_shape=outs,
        in_specs=[SMEM] + [HBM] * len(parts) + [VMEM] * (3 + len(extra)),
        out_specs=(VMEM,) * len(outs),
        scratch_shapes=[
            pltpu.VMEM((rows_all, feature), bf16),
            work,
            pltpu.VMEM((len(parts), 16, feature), bf16),
            pltpu.VMEM((rows_all, 1), f32),
            pltpu.SemaphoreType.DMA((2, max(len(parts), len(spots)))),
        ],
        compiler_params=params(24),
        cost_estimate=spent(cost),
        name="learn",
    )(at, *parts, w, bias, out, *extra)


def adam(old, grad, first, second):
    new_first = beta_one * first + (1.0 - beta_one) * grad
    new_second = beta_two * second + (1.0 - beta_two) * grad * grad
    new = old - learn_rate * new_first / (jnp.sqrt(new_second) + epsilon)
    return new.astype(bf16), new_first, new_second


def step_kernel(
    at_ref, kept, got, kept_vec, got_vec, w, first_w, second_w, vec_old, first_vec, second_vec,
    new_half, new_full, new_vec, new_first_w, new_second_w, new_first_vec, new_second_vec,
):
    new, new_first, new_second = adam(
        w[...].astype(f32), kept[...] + got[...], first_w[0], second_w[0]
    )
    new_half[...] = new
    new_full[0] = new
    new_first_w[0] = new_first
    new_second_w[0] = new_second

    @pl.when(pl.program_id(0) == 0)
    def _():
        grad = kept_vec[...] + got_vec[0:2, :]
        fresh, fresh_first, fresh_second = adam(
            vec_old[...].astype(f32), grad, first_vec[0], second_vec[0]
        )
        new_vec[0] = fresh
        new_first_vec[0] = fresh_first
        new_second_vec[0] = fresh_second


def take_step(rep, kept, kept_vec, got, w_in, vec_old, first_w, second_w, first_vec, second_vec):
    feature, hid = w_in.shape
    half = feature // 2
    tiles = max(n for n in range(1, 5) if half % (16 * n) == 0)
    tile = half // tiles
    here = pl.BlockSpec((tile, hid), lambda i, at: (i, 0))
    there = pl.BlockSpec((tile, hid), lambda i, at: (at[0] * tiles + i, 0))
    tail = pl.BlockSpec((8, hid), lambda i, at: (half // 8, 0))
    moment = pl.BlockSpec((1, tile, hid), lambda i, at: (0, i, 0))
    pair = pl.BlockSpec((2, hid), lambda i, at: (0, 0))
    pairs = pl.BlockSpec((1, 2, hid), lambda i, at: (0, 0, 0))
    full = pl.BlockSpec((1, tile, hid), lambda i, at: (0, at[0] * tiles + i, 0))
    return pl.pallas_call(
        step_kernel,
        grid_spec=pltpu.PrefetchScalarGridSpec(
            num_scalar_prefetch=1,
            grid=(tiles,),
            in_specs=[here, here, pair, tail, there, moment, moment, pair, pairs, pairs],
            out_specs=[here, full, pairs, moment, moment, pairs, pairs],
        ),
        out_shape=(
            sds((half, hid), bf16),
            sds((1, feature, hid), bf16),
            sds((1, 2, hid), bf16),
            sds((1, half, hid), f32),
            sds((1, half, hid), f32),
            sds((1, 2, hid), f32),
            sds((1, 2, hid), f32),
        ),
        compiler_params=params(16),
        name="step",
    )(rep, kept, got, kept_vec, got, w_in, first_w, second_w, vec_old, first_vec, second_vec)


def join_kernel(at_ref, other_ref, full_ref, out_ref, sem):
    half = other_ref.shape[0]
    start = pl.multiple_of((1 - at_ref[0]) * half, half)
    load = pltpu.make_async_copy(other_ref, out_ref.at[0, pl.ds(start, half)], sem)
    load.start()
    load.wait()


def join(rep, other, full):
    return pl.pallas_call(
        join_kernel,
        out_shape=sds(full.shape, full.dtype),
        in_specs=[SMEM, ANY, ANY],
        out_specs=ANY,
        scratch_shapes=[pltpu.SemaphoreType.DMA(())],
        input_output_aliases={2: 0},
        compiler_params=params(8),
        name="join",
    )(rep, other, full)


def gathered(
    embeddings, coverage, labels, w_in, bias_in, w_out, first_w, second_w, first_vec, second_vec
):
    planes = lax.axis_size("dp")
    heads = lax.axis_size("head")
    owners = planes * heads
    z = lax.axis_index("dp")
    q = lax.axis_index("head")
    rep = lax.axis_index("rep").reshape(1)
    blocks, rows_block, feature = embeddings.shape
    per_block = coverage.shape[1]
    slots = 2 * blocks * per_block // owners
    unit = slots * rows_block
    rows = blocks * rows_block
    def right_pairs(hop):
        return [(i, i + 1) for i in range(hop - 1, planes - 1)]

    def left_pairs(hop):
        return [(i + 1, i) for i in range(planes - hop)]

    def exchange(units):
        return [units[0]] + [
            lax.ppermute(units[k], "head", [(i, i ^ k) for i in range(heads)])
            for k in range(1, heads)
        ]

    def plane_heads(plane, real=None):
        found = [plane * heads + (q ^ k) for k in range(heads)]
        return found if real is None else [jnp.where(real, h, -1) for h in found]

    own = make_shard(embeddings.reshape(rows, feature), coverage, labels, owners)
    left = lax.ppermute(own, "dp", left_pairs(1))
    right = lax.ppermute(own, "dp", right_pairs(1))
    always = jnp.ones((), jnp.bool_)
    at_end = (z == 0) | (z == planes - 1)

    def add(total, parts, spots, real, cost, last=False):
        scalars = jnp.stack([rep[0], real]).astype(jnp.int32)
        return learn(unit, spots, parts, scalars, w_in[0], bias_in, w_out, total, cost, last)

    first_heads = plane_heads(jnp.where(at_end, planes - 1 - z, z))
    first_units = exchange(pick(unit, per_block, [own], [(0, 0)], first_heads, [always], 0))
    far_sent = pack(unit, first_units)
    one = jnp.ones((), jnp.int32)
    first_spots = [(k, 0, 0) for k in range(heads)]
    middle = 1 - at_end.astype(jnp.int32)
    rest = []
    for hop in range(1, planes - 1):
        from_left = z >= hop
        from_right = z + hop < planes
        if hop + 1 < planes - 1:
            left, right, far_sent = lax.optimization_barrier((left, right, far_sent))
            next_left = lax.ppermute(left, "dp", left_pairs(hop + 1))
            next_right = lax.ppermute(right, "dp", right_pairs(hop + 1))
        else:
            next_right, next_left = None, None
        if hop == planes - 2 and hop > 1:
            far_sent, left, right, grad, vec = lax.optimization_barrier(
                (far_sent, left, right, *total)
            )
            total = (grad, vec)
            ends = [(0, planes - 1), (planes - 1, 0)]
            far_got = lax.ppermute(far_sent, "dp", ends)
        if 2 * hop < planes:
            fill = hop == 1
            messages = pick(
                unit,
                per_block,
                [left, right, own],
                [(1, 2), (0, 2)],
                plane_heads(z, from_left | fill) + plane_heads(z, from_right | fill),
                [from_left, from_right],
                PB,
            )
            units = 2
        else:
            messages = pick(
                unit,
                per_block,
                [left, right],
                [(0, 1)],
                plane_heads(z, from_left | from_right),
                [from_right],
                PC,
            )
            units = 1
        where = [(k, g * unit, g) for k in range(heads) for g in range(units)]
        if hop == 1:
            first_units = lax.optimization_barrier((*first_units, *messages))[:heads]
            total = add(None, first_units, first_spots, middle, LA)
        else:
            messages = lax.optimization_barrier((*messages, *rest[-1][0]))[:heads]
        rest.append((exchange(messages), where))
        right, left = next_right, next_left
    rest.append(([far_got], [(0, k * unit, k) for k in range(heads)]))

    for at, (parts, spots) in enumerate(rest):
        cost = (LB, LC, LF)[min(at, 2)]
        last = at == len(rest) - 1
        done, total = total, add(total, parts, spots, one, cost, last)
    given, kept_vec, low = total
    got = lax.ppermute(given, "rep", swap)
    kept = keep(unit, spots, parts, rep, low, done[0])
    vec_old = jnp.concatenate([bias_in, w_out])
    new_half, new_full, new_vec, nfw, nsw, nfv, nsv = take_step(
        rep, kept, kept_vec, got, w_in[0], vec_old, first_w, second_w, first_vec, second_vec
    )
    new_w_in = join(rep, lax.ppermute(new_half, "rep", swap), new_full)
    return new_w_in, new_vec, nfw, nsw, nfv, nsv


def routed(
    embeddings, coverage, labels, w_in, bias_in, w_out, first_w, second_w, first_vec, second_vec
):
    dp_count = lax.axis_size("dp")
    head_count = lax.axis_size("head")
    owners = dp_count * head_count
    block_count, rows_block, feature = embeddings.shape
    per_block = coverage.shape[1]
    slot_count = 2 * block_count * per_block // owners
    entries = block_count * per_block
    heads_flat = coverage.reshape(entries)
    onehot = (heads_flat[:, None] == jnp.arange(owners, dtype=jnp.int32)[None, :]).astype(jnp.int32)
    slot_rank = jnp.sum((jnp.cumsum(onehot, axis=0) - 1) * onehot, axis=1)
    target_slot = heads_flat * slot_count + slot_rank
    picker = jnp.arange(owners * slot_count, dtype=jnp.int32)[:, None] == target_slot[None, :]
    block_pick = jnp.sum(
        picker.reshape(owners * slot_count, block_count, per_block).astype(jnp.int32), axis=2
    ).astype(jnp.bfloat16)
    send_rows = jnp.dot(
        block_pick,
        embeddings.reshape(block_count, rows_block * feature),
        preferred_element_type=jnp.float32,
    ).astype(jnp.bfloat16)
    label_marks = (labels.reshape(entries, rows_block) + 1).astype(jnp.float32)
    send_marks = jnp.dot(
        picker.astype(jnp.float32), label_marks, precision=lax.Precision.HIGHEST
    ).astype(jnp.bfloat16)
    direct_rows = send_rows.reshape(owners, slot_count, rows_block, feature)
    direct_marks = send_marks.reshape(owners, slot_count, rows_block)
    got_rows, got_marks = (
        lax.all_to_all(direct_rows, ("dp", "head"), split_axis=0, concat_axis=0, tiled=True),
        lax.all_to_all(direct_marks, ("dp", "head"), split_axis=0, concat_axis=0, tiled=True),
    )
    row_data = got_rows.reshape(-1, feature)
    marks_all = got_marks.reshape(-1).astype(jnp.float32)
    usable = marks_all > 0.5
    target = marks_all - 1.0
    out_weight = w_out[0].astype(jnp.float32)
    pre_act = (
        jnp.dot(row_data, w_in[0], preferred_element_type=jnp.float32)
        + bias_in[0].astype(jnp.float32)[None, :]
    )
    sig_pre = jax.nn.sigmoid(pre_act)
    hidden = pre_act * sig_pre
    logits = jnp.sum(hidden * out_weight[None, :], axis=1)
    residual = jnp.where(usable, jax.nn.sigmoid(logits) - target, jnp.zeros_like(logits))
    grad_pre = residual[:, None] * out_weight[None, :] * sig_pre * (1.0 + pre_act * (1.0 - sig_pre))
    grad_low = grad_pre.astype(jnp.bfloat16)
    vec_part = jnp.stack([jnp.sum(grad_pre, axis=0), jnp.sum(residual[:, None] * hidden, axis=0)])
    half_rows = feature // lax.axis_size("rep")
    rep_at = lax.axis_index("rep")
    first_row = rep_at * half_rows
    grad_part = lax.dot_general(
        row_data, grad_low, (((0,), (0,)), ((), ())), preferred_element_type=jnp.float32
    ).reshape(2, half_rows, -1)
    kept = jnp.where(rep_at == 0, grad_part[0], grad_part[1])
    given = jnp.where(rep_at == 0, grad_part[1], grad_part[0])
    grad_w = kept + lax.ppermute(given, "rep", swap)
    grad_vec = vec_part + lax.ppermute(vec_part, "rep", swap)
    new_first_w = beta_one * first_w[0] + (1.0 - beta_one) * grad_w
    new_second_w = beta_two * second_w[0] + (1.0 - beta_two) * grad_w * grad_w
    old_rows = lax.dynamic_slice_in_dim(w_in[0], first_row, half_rows, 0).astype(jnp.float32)
    new_half = (old_rows - learn_rate * new_first_w / (jnp.sqrt(new_second_w) + epsilon)).astype(
        jnp.bfloat16
    )
    other_half = lax.ppermute(new_half, "rep", swap)
    new_w_in = jnp.where(
        rep_at == 0,
        jnp.concatenate([new_half, other_half]),
        jnp.concatenate([other_half, new_half]),
    )
    vector = jnp.stack([bias_in[0], w_out[0]]).astype(jnp.float32)
    new_first_vec = beta_one * first_vec[0] + (1.0 - beta_one) * grad_vec
    new_second_vec = beta_two * second_vec[0] + (1.0 - beta_two) * grad_vec * grad_vec
    new_vec = (vector - learn_rate * new_first_vec / (jnp.sqrt(new_second_vec) + epsilon)).astype(
        jnp.bfloat16
    )
    return (
        new_w_in[None],
        new_vec[None],
        new_first_w[None],
        new_second_w[None],
        new_first_vec[None],
        new_second_vec[None],
    )


def solution(mesh):
    placed = (
        P(("dp", "head", "rep"), None, None),
        P(("dp", "head", "rep"), None),
        P(("dp", "head", "rep"), None, None),
        P(("dp", "head"), None, None),
        P(("dp", "head"), None),
        P(("dp", "head"), None),
        P(("dp", "head"), "rep", None),
        P(("dp", "head"), "rep", None),
        P(("dp", "head"), None, None),
        P(("dp", "head"), None, None),
    )
    planes, heads, reps = mesh.shape["dp"], mesh.shape["head"], mesh.shape["rep"]
    short = 3 < planes <= heads and heads & (heads - 1) == 0 and reps == 2
    return jax.shard_map(
        gathered if short else routed,
        mesh=mesh,
        in_specs=placed,
        out_specs=(
            P(("dp", "head"), None, None),
            P(("dp", "head"), None, None),
            P(("dp", "head"), "rep", None),
            P(("dp", "head"), "rep", None),
            P(("dp", "head"), None, None),
            P(("dp", "head"), None, None),
        ),
        check_vma=False,
    )
```

```python
import functools

import jax
import jax.numpy as jnp
from jax import lax
from jax.experimental import pallas as pl
from jax.experimental.pallas import tpu as pltpu
from jax.sharding import PartitionSpec as P

beta_one = 0.9
beta_two = 0.999
learn_rate = 0.001
epsilon = 1e-08
swap = [(0, 1), (1, 0)]
PB, PC, LA, LB, LC, LF = (0, 10, 0, 40, 20, 0)
bf16 = jnp.bfloat16
MIB = 1024 * 1024
ROOM = 60
ANY = pl.BlockSpec(memory_space=pl.ANY)
VMEM = pl.BlockSpec(memory_space=pltpu.VMEM)
HBM = pl.BlockSpec(memory_space=pltpu.HBM)
SMEM = pl.BlockSpec(memory_space=pltpu.SMEM)
f32 = jnp.float32


def spent(us):
    return pl.CostEstimate(flops=int(us * 1150000000) + 1, bytes_accessed=1, transcendentals=0)


def params(mib):
    return pltpu.CompilerParams(vmem_limit_bytes=mib * MIB)


def sds(shape, dtype):
    return jax.ShapeDtypeStruct(shape, dtype)


def half_sigmoid(x):
    return 0.5 * jnp.tanh(0.5 * x) + 0.5


def shard_kernel(owners, cov_hbm, lab_hbm, own_ref, out_ref, cov_ref, lab_ref, held_ref, sems):
    per_block, blocks = cov_ref.shape
    rows_block = lab_ref.shape[1]
    rows = blocks * rows_block
    load_cov = pltpu.make_async_copy(cov_hbm, cov_ref, sems.at[0])
    load_lab = pltpu.make_async_copy(lab_hbm, lab_ref, sems.at[1])
    half = rows // 2
    loads = []
    stores = []
    for i in range(2):
        part = pl.ds(i * half, half)
        loads.append(pltpu.make_async_copy(own_ref.at[part], held_ref.at[part], sems.at[2 + i]))
        stores.append(pltpu.make_async_copy(held_ref.at[part], out_ref.at[part], sems.at[4 + i]))
    load_cov.start()
    load_lab.start()
    for load in loads:
        load.start()
    for load, store in zip(loads, stores):
        load.wait()
        store.start()
    load_cov.wait()
    load_lab.wait()
    cov = cov_ref[...]
    heads_at = lax.broadcasted_iota(jnp.int32, (owners, blocks), 0)
    named = (cov[0:1] == heads_at).astype(f32)
    for t in range(1, per_block):
        named = named + (cov[t : t + 1] == heads_at).astype(f32)
    block_of = lax.broadcasted_iota(jnp.int32, (blocks, rows), 1) // rows_block
    block_at = lax.broadcasted_iota(jnp.int32, (blocks, rows), 0)
    same = (block_of == block_at).astype(bf16)
    before = (block_at < block_of).astype(bf16)
    rank = jnp.dot(named.astype(bf16), before, preferred_element_type=f32)
    cov_rows = jnp.dot(cov.astype(f32).astype(bf16), same, preferred_element_type=f32)
    row_in = lax.broadcasted_iota(jnp.int32, (rows_block, rows), 1) % rows_block
    row_at = lax.broadcasted_iota(jnp.int32, (rows_block, rows), 0)
    head_rows = lax.broadcasted_iota(jnp.int32, (owners, rows), 0).astype(f32)
    at_mark = lax.broadcasted_iota(jnp.int32, (16, rows), 0)
    mark_rows = jnp.zeros((16, rows), f32)
    for t in range(per_block):
        mine = cov_rows[t : t + 1]
        own_rank = jnp.sum(jnp.where(mine == head_rows, rank, 0.0), axis=0, keepdims=True)
        place = own_rank * rows_block + row_in[0:1].astype(f32)
        spread = jnp.dot(lab_ref[t].astype(f32).astype(bf16), same, preferred_element_type=f32)
        label = 1.0 + jnp.sum(jnp.where(row_in == row_at, spread, 0.0), axis=0, keepdims=True)
        mark_rows = jnp.where(at_mark == t, mine, mark_rows)
        mark_rows = jnp.where(at_mark == per_block + t, place, mark_rows)
        mark_rows = jnp.where(at_mark == 2 * per_block + t, label, mark_rows)
    held_ref[rows:, :] = jnp.zeros((16, held_ref.shape[1]), bf16)
    held_ref[rows:, 0:rows] = mark_rows.astype(bf16)
    last = pl.ds(rows, 16)
    stores.append(pltpu.make_async_copy(held_ref.at[last], out_ref.at[last], sems.at[6]))
    stores[-1].start()
    for store in stores:
        store.wait()


def make_shard(own, coverage, labels, owners):
    rows, feature = own.shape
    return pl.pallas_call(
        functools.partial(shard_kernel, owners),
        out_shape=sds((rows + 16, feature), bf16),
        in_specs=[HBM, HBM, HBM],
        out_specs=HBM,
        scratch_shapes=[
            pltpu.VMEM((coverage.shape[1], coverage.shape[0]), jnp.int32),
            pltpu.VMEM((labels.shape[1], labels.shape[2], labels.shape[0]), jnp.int32),
            pltpu.VMEM((rows + 16, feature), bf16),
            pltpu.SemaphoreType.DMA((7,)),
        ],
        compiler_params=params(ROOM),
        name="shard",
    )(coverage.T, labels.transpose(1, 2, 0), own)


def pick_rows(marks, shard, heads, unit, per_block):
    rows = marks.shape[1]
    slot = lax.broadcasted_iota(jnp.int32, (unit, rows), 0).astype(f32)
    at_head = lax.broadcasted_iota(jnp.int32, (8, rows), 0)
    chosen = []
    labels = jnp.zeros((8, rows), f32)
    for k, head in enumerate(heads):
        place = jnp.full((1, rows), -1.0, f32)
        label = jnp.zeros((1, rows), f32)
        for t in range(per_block):
            mine = marks[t : t + 1] == head
            place = jnp.where(mine, marks[per_block + t : per_block + t + 1], place)
            label = jnp.where(mine, marks[2 * per_block + t : 2 * per_block + t + 1], label)
        chosen.append(jnp.where(place == slot, 1.0, 0.0).astype(bf16))
        labels = jnp.where(at_head == k, label, labels)
    chosen = jnp.concatenate(chosen, axis=0)
    picked = jnp.dot(chosen, shard, preferred_element_type=f32).astype(bf16)
    mark = lax.dot_general(
        labels.astype(bf16), chosen, (((1,), (1,)), ((), ())), preferred_element_type=f32
    )
    return picked, mark


def pick_kernel(unit, per_block, plan, n_shards, n_heads, at_ref, *refs):
    shards, refs = refs[:n_shards], refs[n_shards:]
    outs, refs = refs[:n_heads], refs[n_heads:]
    held, ready, in_sems, out_sems = refs
    units = len(plan)
    rows = held.shape[1] - 16

    for g, (yes, no) in enumerate(plan):
        if yes == no:
            pltpu.make_async_copy(shards[yes], held.at[g], in_sems.at[g]).start()
        else:
            flag = at_ref[units * n_heads + g] > 0

            @pl.when(flag)
            def _():
                pltpu.make_async_copy(shards[yes], held.at[g], in_sems.at[g]).start()

            @pl.when(jnp.logical_not(flag))
            def _():
                pltpu.make_async_copy(shards[no], held.at[g], in_sems.at[g]).start()

    at_mark = lax.broadcasted_iota(jnp.int32, (16, unit), 0)
    mark_rows = [jnp.zeros((16, unit), f32)] * n_heads
    for g, (yes, _) in enumerate(plan):
        pltpu.make_async_copy(shards[yes], held.at[g], in_sems.at[g]).wait()
        marks = held[g, rows:, 0:rows].astype(f32)
        wanted = [at_ref[g * n_heads + k].astype(f32) for k in range(n_heads)]
        picked, mark = pick_rows(marks, held[g, 0:rows], wanted, unit, per_block)
        for k in range(n_heads):
            ready[k, g * unit : (g + 1) * unit, :] = picked[k * unit : (k + 1) * unit]
            own_mark = mark[k : k + 1, k * unit : (k + 1) * unit]
            mark_rows[k] = jnp.where(at_mark == g, own_mark, mark_rows[k])
    for k in range(n_heads):
        ready[k, units * unit :, :] = jnp.zeros((16, ready.shape[2]), bf16)
        ready[k, units * unit :, 0:unit] = mark_rows[k].astype(bf16)
        pltpu.make_async_copy(ready.at[k], outs[k], out_sems.at[k]).start()
    for k in range(n_heads):
        pltpu.make_async_copy(ready.at[k], outs[k], out_sems.at[k]).wait()


def pick(unit, per_block, shards, plan, heads_at, flags, cost):
    rows, feature = shards[0].shape
    units = len(plan)
    n_heads = len(heads_at) // units
    size = units * unit + 16
    return pl.pallas_call(
        functools.partial(pick_kernel, unit, per_block, plan, len(shards), n_heads),
        out_shape=[sds((size, feature), bf16)] * n_heads,
        in_specs=[SMEM] + [HBM] * len(shards),
        out_specs=[HBM] * n_heads,
        scratch_shapes=[
            pltpu.VMEM((units, rows, feature), bf16),
            pltpu.VMEM((n_heads, size, feature), bf16),
            pltpu.SemaphoreType.DMA((units,)),
            pltpu.SemaphoreType.DMA((n_heads,)),
        ],
        compiler_params=params(16),
        cost_estimate=spent(cost),
        name="pick",
    )(jnp.stack(heads_at + flags).astype(jnp.int32), *shards)


def pack_kernel(unit, n, *refs):
    parts, out_ref, mark_ref, all_ref, sems = refs[:n], *refs[n:]
    loads = []
    for k in range(n):
        loads.append(
            pltpu.make_async_copy(
                parts[k].at[pl.ds(0, unit)], out_ref.at[pl.ds(k * unit, unit)], sems.at[0, k]
            )
        )
        loads.append(
            pltpu.make_async_copy(
                parts[k].at[pl.ds(unit, 16)], mark_ref.at[k], sems.at[1, k]
            )
        )
    for load in loads:
        load.start()
    for load in loads:
        load.wait()
    at_mark = lax.broadcasted_iota(jnp.int32, (16, unit), 0)
    mark_rows = jnp.zeros((16, unit), f32)
    for k in range(n):
        marks = mark_ref[k, :, 0:unit].astype(f32)
        mark_rows = jnp.where(at_mark == k, marks[0:1], mark_rows)
    all_ref[...] = jnp.zeros(all_ref.shape, bf16)
    all_ref[:, 0:unit] = mark_rows.astype(bf16)
    store = pltpu.make_async_copy(all_ref, out_ref.at[pl.ds(n * unit, 16)], sems.at[0, n])
    store.start()
    store.wait()


def pack(unit, parts):
    feature = parts[0].shape[1]
    n = len(parts)
    return pl.pallas_call(
        functools.partial(pack_kernel, unit, n),
        out_shape=sds((n * unit + 16, feature), bf16),
        in_specs=[HBM] * n,
        out_specs=HBM,
        scratch_shapes=[
            pltpu.VMEM((n, 16, feature), bf16),
            pltpu.VMEM((16, feature), bf16),
            pltpu.SemaphoreType.DMA((2, n + 1)),
        ],
        compiler_params=params(8),
        name="pack",
    )(*parts)


def learn_kernel(unit, spots, n_parts, last, with_total, half_rows, at_ref, *refs):
    parts, refs = refs[:n_parts], refs[n_parts:]
    w_ref, bias_ref, out_ref, refs = refs[0], refs[1], refs[2], refs[3:]
    if with_total:
        total_ref, vec_ref, refs = refs[0], refs[1], refs[2:]
    if last:
        given_ref, new_vec_ref, low_ref, refs = refs[0], refs[1], refs[2], refs[3:]
        rows_ref, wide_ref, mark_ref, target_ref, sems = refs
    else:
        new_total_ref, new_vec_ref, refs = refs[0], refs[1], refs[2:]
        rows_ref, low_ref, mark_ref, target_ref, sems = refs
    low_cut = half_rows // 128 * 128
    rows_all, feature = rows_ref.shape
    loads = []
    for i in range(n_parts):
        loads.append(
            pltpu.make_async_copy(
                parts[i].at[pl.ds(parts[i].shape[0] - 16, 16)], mark_ref.at[i], sems.at[0, i]
            )
        )
    for u, (part, at, _) in enumerate(spots):
        loads.append(
            pltpu.make_async_copy(
                parts[part].at[pl.ds(at, unit)],
                rows_ref.at[pl.ds(u * unit, unit)],
                sems.at[1, u],
            )
        )
    for load in loads:
        load.start()
    for load in loads:
        load.wait()
    eye = lax.broadcasted_iota(jnp.int32, (unit, unit), 0) == lax.broadcasted_iota(
        jnp.int32, (unit, unit), 1
    )
    for u, (part, _, mark_at) in enumerate(spots):
        marks = mark_ref[part, :, 0:unit].astype(f32)[mark_at : mark_at + 1]
        target_ref[u * unit : (u + 1) * unit, :] = jnp.sum(
            jnp.where(eye, marks, 0.0), axis=1, keepdims=True
        ) * at_ref[1].astype(f32)
    bias = bias_ref[...].astype(f32)
    out_weight = out_ref[...].astype(f32)
    step = 2 * unit
    hid = w_ref.shape[1]

    def forward(i, carry):
        span = pl.ds(pl.multiple_of(i * step, step), step)
        pre = jnp.dot(rows_ref[span, :], w_ref[...], preferred_element_type=f32) + bias
        gate = half_sigmoid(pre)
        hidden = pre * gate
        logit = jnp.sum(hidden * out_weight, axis=1, keepdims=True)
        mark = target_ref[span, :]
        residual = jnp.where(mark > 0.5, half_sigmoid(logit) - (mark - 1.0), 0.0)
        grad_pre = residual * out_weight * gate * (1.0 + pre * (1.0 - gate))
        low_ref[span, :] = grad_pre.astype(bf16)
        return (
            carry[0] + jnp.sum(grad_pre, axis=0, keepdims=True),
            carry[1] + jnp.sum(residual * hidden, axis=0, keepdims=True),
        )

    if with_total:
        start = (vec_ref[0:1, :], vec_ref[1:2, :])
    else:
        start = (jnp.zeros((1, hid), f32), jnp.zeros((1, hid), f32))
    grad_bias, grad_out = lax.fori_loop(0, rows_all // step, forward, start)

    def product(first, size):
        piece = lax.dot_general(
            rows_ref[:, first : first + size],
            low_ref[...],
            (((0,), (0,)), ((), ())),
            preferred_element_type=f32,
        )
        if with_total:
            piece = piece + total_ref[first : first + size, :]
        return piece

    tile = 128 * max(n for n in range(1, 5) if feature % (128 * n) == 0)
    if not last:
        for first in range(0, feature, tile):
            new_total_ref[first : first + tile, :] = product(first, tile)
        new_vec_ref[0:1, :] = grad_bias
        new_vec_ref[1:2, :] = grad_out
        return
    first = pl.multiple_of((1 - at_ref[0]) * low_cut, 128)
    skip = pl.multiple_of((1 - at_ref[0]) * (half_rows - low_cut), 8)
    wide_ref[...] = lax.dot_general(
        rows_ref[:, pl.ds(first, feature - low_cut)],
        low_ref[...],
        (((0,), (0,)), ((), ())),
        preferred_element_type=f32,
    )
    other = pl.multiple_of((1 - at_ref[0]) * half_rows, 8)
    given_ref[0:half_rows, :] = (
        wide_ref[pl.ds(skip, half_rows), :] + total_ref[pl.ds(other, half_rows), :]
    )
    given_ref[half_rows : half_rows + 8, :] = jnp.zeros((8, hid), f32)
    given_ref[half_rows : half_rows + 1, :] = grad_bias
    given_ref[half_rows + 1 : half_rows + 2, :] = grad_out
    new_vec_ref[0:1, :] = grad_bias
    new_vec_ref[1:2, :] = grad_out


def keep_kernel(half_rows, low_cut, unit, spots, n_parts, at_ref, *refs):
    parts, (low_ref, total_ref, out_ref, rows_ref, wide_ref, sems) = refs[:n_parts], refs[n_parts:]
    feature = rows_ref.shape[1]
    loads = []
    for u, (part, at, _) in enumerate(spots):
        loads.append(
            pltpu.make_async_copy(
                parts[part].at[pl.ds(at, unit)], rows_ref.at[pl.ds(u * unit, unit)], sems.at[u]
            )
        )
    for load in loads:
        load.start()
    for load in loads:
        load.wait()
    first = pl.multiple_of(at_ref[0] * low_cut, 128)
    skip = pl.multiple_of(at_ref[0] * (half_rows - low_cut), 8)
    wide_ref[...] = lax.dot_general(
        rows_ref[:, pl.ds(first, feature - low_cut)],
        low_ref[...],
        (((0,), (0,)), ((), ())),
        preferred_element_type=f32,
    )
    own = pl.multiple_of(at_ref[0] * half_rows, 8)
    out_ref[...] = wide_ref[pl.ds(skip, half_rows), :] + total_ref[pl.ds(own, half_rows), :]


def keep(unit, spots, parts, at, low, total):
    feature, hid = total.shape
    half = feature // 2
    low_cut = half // 128 * 128
    return pl.pallas_call(
        functools.partial(keep_kernel, half, low_cut, unit, spots, len(parts)),
        out_shape=sds((half, hid), f32),
        in_specs=[SMEM] + [HBM] * len(parts) + [VMEM, VMEM],
        out_specs=VMEM,
        scratch_shapes=[
            pltpu.VMEM((low.shape[0], feature), bf16),
            pltpu.VMEM((feature - low_cut, hid), f32),
            pltpu.SemaphoreType.DMA((len(spots),)),
        ],
        compiler_params=params(16),
        cost_estimate=spent(2),
        name="keep",
    )(at, *parts, low, total)


def learn(unit, spots, parts, at, w, bias, out, total, cost, last):
    feature, hid = w.shape
    rows_all = len(spots) * unit
    half = feature // 2
    if last:
        outs = (sds((half + 8, hid), f32), sds((2, hid), f32), sds((rows_all, hid), bf16))
        work = pltpu.VMEM((feature - half // 128 * 128, hid), f32)
    else:
        outs = (sds((feature, hid), f32), sds((2, hid), f32))
        work = pltpu.VMEM((rows_all, hid), bf16)
    extra = () if total is None else total
    kernel = functools.partial(
        learn_kernel, unit, spots, len(parts), last, total is not None, half
    )
    return pl.pallas_call(
        kernel,
        out_shape=outs,
        in_specs=[SMEM] + [HBM] * len(parts) + [VMEM] * (3 + len(extra)),
        out_specs=(VMEM,) * len(outs),
        scratch_shapes=[
            pltpu.VMEM((rows_all, feature), bf16),
            work,
            pltpu.VMEM((len(parts), 16, feature), bf16),
            pltpu.VMEM((rows_all, 1), f32),
            pltpu.SemaphoreType.DMA((2, max(len(parts), len(spots)))),
        ],
        compiler_params=params(24),
        cost_estimate=spent(cost),
        name="learn",
    )(at, *parts, w, bias, out, *extra)


def adam(old, grad, first, second):
    new_first = beta_one * first + (1.0 - beta_one) * grad
    new_second = beta_two * second + (1.0 - beta_two) * grad * grad
    new = old - learn_rate * new_first / (jnp.sqrt(new_second) + epsilon)
    return new.astype(bf16), new_first, new_second


def step_kernel(
    at_ref, kept, got, kept_vec, got_vec, w, first_w, second_w, vec_old, first_vec, second_vec,
    new_half, new_full, new_vec, new_first_w, new_second_w, new_first_vec, new_second_vec,
):
    new, new_first, new_second = adam(
        w[...].astype(f32), kept[...] + got[...], first_w[0], second_w[0]
    )
    new_half[...] = new
    new_full[0] = new
    new_first_w[0] = new_first
    new_second_w[0] = new_second

    @pl.when(pl.program_id(0) == 0)
    def _():
        grad = kept_vec[...] + got_vec[0:2, :]
        fresh, fresh_first, fresh_second = adam(
            vec_old[...].astype(f32), grad, first_vec[0], second_vec[0]
        )
        new_vec[0] = fresh
        new_first_vec[0] = fresh_first
        new_second_vec[0] = fresh_second


def take_step(rep, kept, kept_vec, got, w_in, vec_old, first_w, second_w, first_vec, second_vec):
    feature, hid = w_in.shape
    half = feature // 2
    tiles = max(n for n in range(1, 5) if half % (16 * n) == 0)
    tile = half // tiles
    here = pl.BlockSpec((tile, hid), lambda i, at: (i, 0))
    there = pl.BlockSpec((tile, hid), lambda i, at: (at[0] * tiles + i, 0))
    tail = pl.BlockSpec((8, hid), lambda i, at: (half // 8, 0))
    moment = pl.BlockSpec((1, tile, hid), lambda i, at: (0, i, 0))
    pair = pl.BlockSpec((2, hid), lambda i, at: (0, 0))
    pairs = pl.BlockSpec((1, 2, hid), lambda i, at: (0, 0, 0))
    full = pl.BlockSpec((1, tile, hid), lambda i, at: (0, at[0] * tiles + i, 0))
    return pl.pallas_call(
        step_kernel,
        grid_spec=pltpu.PrefetchScalarGridSpec(
            num_scalar_prefetch=1,
            grid=(tiles,),
            in_specs=[here, here, pair, tail, there, moment, moment, pair, pairs, pairs],
            out_specs=[here, full, pairs, moment, moment, pairs, pairs],
        ),
        out_shape=(
            sds((half, hid), bf16),
            sds((1, feature, hid), bf16),
            sds((1, 2, hid), bf16),
            sds((1, half, hid), f32),
            sds((1, half, hid), f32),
            sds((1, 2, hid), f32),
            sds((1, 2, hid), f32),
        ),
        compiler_params=params(16),
        name="step",
    )(rep, kept, got, kept_vec, got, w_in, first_w, second_w, vec_old, first_vec, second_vec)


def join_kernel(at_ref, other_ref, full_ref, out_ref, sem):
    half = other_ref.shape[0]
    start = pl.multiple_of((1 - at_ref[0]) * half, half)
    load = pltpu.make_async_copy(other_ref, out_ref.at[0, pl.ds(start, half)], sem)
    load.start()
    load.wait()


def join(rep, other, full):
    return pl.pallas_call(
        join_kernel,
        out_shape=sds(full.shape, full.dtype),
        in_specs=[SMEM, ANY, ANY],
        out_specs=ANY,
        scratch_shapes=[pltpu.SemaphoreType.DMA(())],
        input_output_aliases={2: 0},
        compiler_params=params(8),
        name="join",
    )(rep, other, full)


def gathered(
    embeddings, coverage, labels, w_in, bias_in, w_out, first_w, second_w, first_vec, second_vec
):
    planes = lax.axis_size("dp")
    heads = lax.axis_size("head")
    owners = planes * heads
    z = lax.axis_index("dp")
    q = lax.axis_index("head")
    rep = lax.axis_index("rep").reshape(1)
    blocks, rows_block, feature = embeddings.shape
    per_block = coverage.shape[1]
    slots = 2 * blocks * per_block // owners
    unit = slots * rows_block
    rows = blocks * rows_block
    outer_pairs = [(i, i ^ 1) for i in range(planes)]
    inner_pairs = [(i, i + 1 if i % 2 else i - 1) for i in range(1, planes - 1)]
    out_pairs = [(i, i ^ 1) for i in range(1, planes - 1)]
    end_pairs = [(0, planes - 1), (planes - 1, 0)]

    def exchange(units):
        return [units[0]] + [
            lax.ppermute(units[k], "head", [(i, i ^ k) for i in range(heads)])
            for k in range(1, heads)
        ]

    def plane_heads(plane, real=None):
        found = [plane * heads + (q ^ k) for k in range(heads)]
        return found if real is None else [jnp.where(real, h, -1) for h in found]

    own = make_shard(embeddings.reshape(rows, feature), coverage, labels, owners)
    outer = lax.ppermute(own, "dp", outer_pairs)
    inner = lax.ppermute(own, "dp", inner_pairs)
    always = jnp.ones((), jnp.bool_)
    at_end = (z == 0) | (z == planes - 1)

    def add(total, parts, spots, real, cost, last=False):
        scalars = jnp.stack([rep[0], real]).astype(jnp.int32)
        return learn(unit, spots, parts, scalars, w_in[0], bias_in, w_out, total, cost, last)

    first_heads = plane_heads(jnp.where(at_end, planes - 1 - z, z))
    first_units = exchange(pick(unit, per_block, [own], [(0, 0)], first_heads, [always], 0))
    far_sent = pack(unit, first_units)
    one = jnp.ones((), jnp.int32)
    first_spots = [(k, 0, 0) for k in range(heads)]
    middle = 1 - at_end.astype(jnp.int32)
    outer, inner, far_sent = lax.optimization_barrier((outer, inner, far_sent))
    next_in = lax.ppermute(outer, "dp", inner_pairs)
    next_out = lax.ppermute(inner, "dp", out_pairs)
    messages = pick(
        unit, per_block, [outer, inner, own], [(0, 0), (1, 2)], plane_heads(z) * 2,
        [always, jnp.logical_not(at_end)], PB,
    )
    first_units = lax.optimization_barrier((*first_units, *messages))[:heads]
    total = add(None, first_units, first_spots, middle, LA)
    near = exchange(messages)
    far_sent, next_out, next_in, *total = lax.optimization_barrier(
        (far_sent, next_out, next_in, *total)
    )
    far_got = lax.ppermute(far_sent, "dp", end_pairs)
    messages = pick(
        unit, per_block, [next_in, next_out], [(0, 1)], plane_heads(z),
        [jnp.logical_not(at_end)], PC,
    )
    messages = lax.optimization_barrier((*messages, *near))[:heads]
    rest = [
        (near, [(k, g * unit, g) for k in range(heads) for g in range(2)]),
        (exchange(messages), [(k, 0, 0) for k in range(heads)]),
    ]
    rest.append(([far_got], [(0, k * unit, k) for k in range(heads)]))

    for at, (parts, spots) in enumerate(rest):
        cost = (LB, LC, LF)[min(at, 2)]
        last = at == len(rest) - 1
        done, total = total, add(total, parts, spots, one, cost, last)
    given, kept_vec, low = total
    got = lax.ppermute(given, "rep", swap)
    kept = keep(unit, spots, parts, rep, low, done[0])
    vec_old = jnp.concatenate([bias_in, w_out])
    new_half, new_full, new_vec, nfw, nsw, nfv, nsv = take_step(
        rep, kept, kept_vec, got, w_in[0], vec_old, first_w, second_w, first_vec, second_vec
    )
    new_w_in = join(rep, lax.ppermute(new_half, "rep", swap), new_full)
    return new_w_in, new_vec, nfw, nsw, nfv, nsv


def routed(
    embeddings, coverage, labels, w_in, bias_in, w_out, first_w, second_w, first_vec, second_vec
):
    dp_count = lax.axis_size("dp")
    head_count = lax.axis_size("head")
    owners = dp_count * head_count
    block_count, rows_block, feature = embeddings.shape
    per_block = coverage.shape[1]
    slot_count = 2 * block_count * per_block // owners
    entries = block_count * per_block
    heads_flat = coverage.reshape(entries)
    onehot = (heads_flat[:, None] == jnp.arange(owners, dtype=jnp.int32)[None, :]).astype(jnp.int32)
    slot_rank = jnp.sum((jnp.cumsum(onehot, axis=0) - 1) * onehot, axis=1)
    target_slot = heads_flat * slot_count + slot_rank
    picker = jnp.arange(owners * slot_count, dtype=jnp.int32)[:, None] == target_slot[None, :]
    block_pick = jnp.sum(
        picker.reshape(owners * slot_count, block_count, per_block).astype(jnp.int32), axis=2
    ).astype(jnp.bfloat16)
    send_rows = jnp.dot(
        block_pick,
        embeddings.reshape(block_count, rows_block * feature),
        preferred_element_type=jnp.float32,
    ).astype(jnp.bfloat16)
    label_marks = (labels.reshape(entries, rows_block) + 1).astype(jnp.float32)
    send_marks = jnp.dot(
        picker.astype(jnp.float32), label_marks, precision=lax.Precision.HIGHEST
    ).astype(jnp.bfloat16)
    direct_rows = send_rows.reshape(owners, slot_count, rows_block, feature)
    direct_marks = send_marks.reshape(owners, slot_count, rows_block)
    got_rows, got_marks = (
        lax.all_to_all(direct_rows, ("dp", "head"), split_axis=0, concat_axis=0, tiled=True),
        lax.all_to_all(direct_marks, ("dp", "head"), split_axis=0, concat_axis=0, tiled=True),
    )
    row_data = got_rows.reshape(-1, feature)
    marks_all = got_marks.reshape(-1).astype(jnp.float32)
    usable = marks_all > 0.5
    target = marks_all - 1.0
    out_weight = w_out[0].astype(jnp.float32)
    pre_act = (
        jnp.dot(row_data, w_in[0], preferred_element_type=jnp.float32)
        + bias_in[0].astype(jnp.float32)[None, :]
    )
    sig_pre = jax.nn.sigmoid(pre_act)
    hidden = pre_act * sig_pre
    logits = jnp.sum(hidden * out_weight[None, :], axis=1)
    residual = jnp.where(usable, jax.nn.sigmoid(logits) - target, jnp.zeros_like(logits))
    grad_pre = residual[:, None] * out_weight[None, :] * sig_pre * (1.0 + pre_act * (1.0 - sig_pre))
    grad_low = grad_pre.astype(jnp.bfloat16)
    vec_part = jnp.stack([jnp.sum(grad_pre, axis=0), jnp.sum(residual[:, None] * hidden, axis=0)])
    half_rows = feature // lax.axis_size("rep")
    rep_at = lax.axis_index("rep")
    first_row = rep_at * half_rows
    grad_part = lax.dot_general(
        row_data, grad_low, (((0,), (0,)), ((), ())), preferred_element_type=jnp.float32
    ).reshape(2, half_rows, -1)
    kept = jnp.where(rep_at == 0, grad_part[0], grad_part[1])
    given = jnp.where(rep_at == 0, grad_part[1], grad_part[0])
    grad_w = kept + lax.ppermute(given, "rep", swap)
    grad_vec = vec_part + lax.ppermute(vec_part, "rep", swap)
    new_first_w = beta_one * first_w[0] + (1.0 - beta_one) * grad_w
    new_second_w = beta_two * second_w[0] + (1.0 - beta_two) * grad_w * grad_w
    old_rows = lax.dynamic_slice_in_dim(w_in[0], first_row, half_rows, 0).astype(jnp.float32)
    new_half = (old_rows - learn_rate * new_first_w / (jnp.sqrt(new_second_w) + epsilon)).astype(
        jnp.bfloat16
    )
    other_half = lax.ppermute(new_half, "rep", swap)
    new_w_in = jnp.where(
        rep_at == 0,
        jnp.concatenate([new_half, other_half]),
        jnp.concatenate([other_half, new_half]),
    )
    vector = jnp.stack([bias_in[0], w_out[0]]).astype(jnp.float32)
    new_first_vec = beta_one * first_vec[0] + (1.0 - beta_one) * grad_vec
    new_second_vec = beta_two * second_vec[0] + (1.0 - beta_two) * grad_vec * grad_vec
    new_vec = (vector - learn_rate * new_first_vec / (jnp.sqrt(new_second_vec) + epsilon)).astype(
        jnp.bfloat16
    )
    return (
        new_w_in[None],
        new_vec[None],
        new_first_w[None],
        new_second_w[None],
        new_first_vec[None],
        new_second_vec[None],
    )


def solution(mesh):
    placed = (
        P(("dp", "head", "rep"), None, None),
        P(("dp", "head", "rep"), None),
        P(("dp", "head", "rep"), None, None),
        P(("dp", "head"), None, None),
        P(("dp", "head"), None),
        P(("dp", "head"), None),
        P(("dp", "head"), "rep", None),
        P(("dp", "head"), "rep", None),
        P(("dp", "head"), None, None),
        P(("dp", "head"), None, None),
    )
    planes, heads, reps = mesh.shape["dp"], mesh.shape["head"], mesh.shape["rep"]
    short = planes == 4 and heads & (heads - 1) == 0 and reps == 2
    return jax.shard_map(
        gathered if short else routed,
        mesh=mesh,
        in_specs=placed,
        out_specs=(
            P(("dp", "head"), None, None),
            P(("dp", "head"), None, None),
            P(("dp", "head"), "rep", None),
            P(("dp", "head"), "rep", None),
            P(("dp", "head"), None, None),
            P(("dp", "head"), None, None),
        ),
        check_vma=False,
    )
```

```python
import functools

import jax
import jax.numpy as jnp
from jax import lax
from jax.experimental import pallas as pl
from jax.experimental.pallas import tpu as pltpu
from jax.sharding import PartitionSpec as P

beta_one = 0.9
beta_two = 0.999
learn_rate = 0.001
epsilon = 1e-08
swap = [(0, 1), (1, 0)]
PB, PC, LA, LB, LC, LF = (30, 10, 0, 40, 20, 0)
bf16 = jnp.bfloat16
MIB = 1024 * 1024
ROOM = 60
ANY = pl.BlockSpec(memory_space=pl.ANY)
VMEM = pl.BlockSpec(memory_space=pltpu.VMEM)
HBM = pl.BlockSpec(memory_space=pltpu.HBM)
SMEM = pl.BlockSpec(memory_space=pltpu.SMEM)
f32 = jnp.float32


def spent(us):
    return pl.CostEstimate(flops=int(us * 1150000000) + 1, bytes_accessed=1, transcendentals=0)


def params(mib):
    return pltpu.CompilerParams(vmem_limit_bytes=mib * MIB)


def sds(shape, dtype):
    return jax.ShapeDtypeStruct(shape, dtype)


def half_sigmoid(x):
    return 0.5 * jnp.tanh(0.5 * x) + 0.5


def shard_kernel(owners, cov_hbm, lab_hbm, own_ref, out_ref, cov_ref, lab_ref, held_ref, sems):
    per_block, blocks = cov_ref.shape
    rows_block = lab_ref.shape[1]
    rows = blocks * rows_block
    load_cov = pltpu.make_async_copy(cov_hbm, cov_ref, sems.at[0])
    load_lab = pltpu.make_async_copy(lab_hbm, lab_ref, sems.at[1])
    half = rows // 2
    loads = []
    stores = []
    for i in range(2):
        part = pl.ds(i * half, half)
        loads.append(pltpu.make_async_copy(own_ref.at[part], held_ref.at[part], sems.at[2 + i]))
        stores.append(pltpu.make_async_copy(held_ref.at[part], out_ref.at[part], sems.at[4 + i]))
    load_cov.start()
    load_lab.start()
    for load in loads:
        load.start()
    for load, store in zip(loads, stores):
        load.wait()
        store.start()
    load_cov.wait()
    load_lab.wait()
    cov = cov_ref[...]
    heads_at = lax.broadcasted_iota(jnp.int32, (owners, blocks), 0)
    named = (cov[0:1] == heads_at).astype(f32)
    for t in range(1, per_block):
        named = named + (cov[t : t + 1] == heads_at).astype(f32)
    block_of = lax.broadcasted_iota(jnp.int32, (blocks, rows), 1) // rows_block
    block_at = lax.broadcasted_iota(jnp.int32, (blocks, rows), 0)
    same = (block_of == block_at).astype(bf16)
    before = (block_at < block_of).astype(bf16)
    rank = jnp.dot(named.astype(bf16), before, preferred_element_type=f32)
    cov_rows = jnp.dot(cov.astype(f32).astype(bf16), same, preferred_element_type=f32)
    row_in = lax.broadcasted_iota(jnp.int32, (rows_block, rows), 1) % rows_block
    row_at = lax.broadcasted_iota(jnp.int32, (rows_block, rows), 0)
    head_rows = lax.broadcasted_iota(jnp.int32, (owners, rows), 0).astype(f32)
    at_mark = lax.broadcasted_iota(jnp.int32, (16, rows), 0)
    mark_rows = jnp.zeros((16, rows), f32)
    for t in range(per_block):
        mine = cov_rows[t : t + 1]
        own_rank = jnp.sum(jnp.where(mine == head_rows, rank, 0.0), axis=0, keepdims=True)
        place = own_rank * rows_block + row_in[0:1].astype(f32)
        spread = jnp.dot(lab_ref[t].astype(f32).astype(bf16), same, preferred_element_type=f32)
        label = 1.0 + jnp.sum(jnp.where(row_in == row_at, spread, 0.0), axis=0, keepdims=True)
        mark_rows = jnp.where(at_mark == t, mine, mark_rows)
        mark_rows = jnp.where(at_mark == per_block + t, place, mark_rows)
        mark_rows = jnp.where(at_mark == 2 * per_block + t, label, mark_rows)
    held_ref[rows:, :] = jnp.zeros((16, held_ref.shape[1]), bf16)
    held_ref[rows:, 0:rows] = mark_rows.astype(bf16)
    last = pl.ds(rows, 16)
    stores.append(pltpu.make_async_copy(held_ref.at[last], out_ref.at[last], sems.at[6]))
    stores[-1].start()
    for store in stores:
        store.wait()


def make_shard(own, coverage, labels, owners):
    rows, feature = own.shape
    return pl.pallas_call(
        functools.partial(shard_kernel, owners),
        out_shape=sds((rows + 16, feature), bf16),
        in_specs=[HBM, HBM, HBM],
        out_specs=HBM,
        scratch_shapes=[
            pltpu.VMEM((coverage.shape[1], coverage.shape[0]), jnp.int32),
            pltpu.VMEM((labels.shape[1], labels.shape[2], labels.shape[0]), jnp.int32),
            pltpu.VMEM((rows + 16, feature), bf16),
            pltpu.SemaphoreType.DMA((7,)),
        ],
        compiler_params=params(ROOM),
        name="shard",
    )(coverage.T, labels.transpose(1, 2, 0), own)


def pick_rows(marks, shard, heads, unit, per_block):
    rows = marks.shape[1]
    slot = lax.broadcasted_iota(jnp.int32, (unit, rows), 0).astype(f32)
    at_head = lax.broadcasted_iota(jnp.int32, (8, rows), 0)
    chosen = []
    labels = jnp.zeros((8, rows), f32)
    for k, head in enumerate(heads):
        place = jnp.full((1, rows), -1.0, f32)
        label = jnp.zeros((1, rows), f32)
        for t in range(per_block):
            mine = marks[t : t + 1] == head
            place = jnp.where(mine, marks[per_block + t : per_block + t + 1], place)
            label = jnp.where(mine, marks[2 * per_block + t : 2 * per_block + t + 1], label)
        chosen.append(jnp.where(place == slot, 1.0, 0.0).astype(bf16))
        labels = jnp.where(at_head == k, label, labels)
    chosen = jnp.concatenate(chosen, axis=0)
    picked = jnp.dot(chosen, shard, preferred_element_type=f32).astype(bf16)
    mark = lax.dot_general(
        labels.astype(bf16), chosen, (((1,), (1,)), ((), ())), preferred_element_type=f32
    )
    return picked, mark


def pick_kernel(unit, per_block, plan, n_shards, n_heads, at_ref, *refs):
    shards, refs = refs[:n_shards], refs[n_shards:]
    outs, refs = refs[:n_heads], refs[n_heads:]
    held, ready, in_sems, out_sems = refs
    units = len(plan)
    rows = held.shape[1] - 16

    for g, (yes, no) in enumerate(plan):
        if yes == no:
            pltpu.make_async_copy(shards[yes], held.at[g], in_sems.at[g]).start()
        else:
            flag = at_ref[units * n_heads + g] > 0

            @pl.when(flag)
            def _():
                pltpu.make_async_copy(shards[yes], held.at[g], in_sems.at[g]).start()

            @pl.when(jnp.logical_not(flag))
            def _():
                pltpu.make_async_copy(shards[no], held.at[g], in_sems.at[g]).start()

    at_mark = lax.broadcasted_iota(jnp.int32, (16, unit), 0)
    mark_rows = [jnp.zeros((16, unit), f32)] * n_heads
    for g, (yes, _) in enumerate(plan):
        pltpu.make_async_copy(shards[yes], held.at[g], in_sems.at[g]).wait()
        marks = held[g, rows:, 0:rows].astype(f32)
        wanted = [at_ref[g * n_heads + k].astype(f32) for k in range(n_heads)]
        picked, mark = pick_rows(marks, held[g, 0:rows], wanted, unit, per_block)
        for k in range(n_heads):
            ready[k, g * unit : (g + 1) * unit, :] = picked[k * unit : (k + 1) * unit]
            own_mark = mark[k : k + 1, k * unit : (k + 1) * unit]
            mark_rows[k] = jnp.where(at_mark == g, own_mark, mark_rows[k])
    for k in range(n_heads):
        ready[k, units * unit :, :] = jnp.zeros((16, ready.shape[2]), bf16)
        ready[k, units * unit :, 0:unit] = mark_rows[k].astype(bf16)
        pltpu.make_async_copy(ready.at[k], outs[k], out_sems.at[k]).start()
    for k in range(n_heads):
        pltpu.make_async_copy(ready.at[k], outs[k], out_sems.at[k]).wait()


def pick(unit, per_block, shards, plan, heads_at, flags, cost):
    rows, feature = shards[0].shape
    units = len(plan)
    n_heads = len(heads_at) // units
    size = units * unit + 16
    return pl.pallas_call(
        functools.partial(pick_kernel, unit, per_block, plan, len(shards), n_heads),
        out_shape=[sds((size, feature), bf16)] * n_heads,
        in_specs=[SMEM] + [HBM] * len(shards),
        out_specs=[HBM] * n_heads,
        scratch_shapes=[
            pltpu.VMEM((units, rows, feature), bf16),
            pltpu.VMEM((n_heads, size, feature), bf16),
            pltpu.SemaphoreType.DMA((units,)),
            pltpu.SemaphoreType.DMA((n_heads,)),
        ],
        compiler_params=params(16),
        cost_estimate=spent(cost),
        name="pick",
    )(jnp.stack(heads_at + flags).astype(jnp.int32), *shards)


def pack_kernel(unit, n, *refs):
    parts, out_ref, mark_ref, all_ref, sems = refs[:n], *refs[n:]
    loads = []
    for k in range(n):
        loads.append(
            pltpu.make_async_copy(
                parts[k].at[pl.ds(0, unit)], out_ref.at[pl.ds(k * unit, unit)], sems.at[0, k]
            )
        )
        loads.append(
            pltpu.make_async_copy(
                parts[k].at[pl.ds(unit, 16)], mark_ref.at[k], sems.at[1, k]
            )
        )
    for load in loads:
        load.start()
    for load in loads:
        load.wait()
    at_mark = lax.broadcasted_iota(jnp.int32, (16, unit), 0)
    mark_rows = jnp.zeros((16, unit), f32)
    for k in range(n):
        marks = mark_ref[k, :, 0:unit].astype(f32)
        mark_rows = jnp.where(at_mark == k, marks[0:1], mark_rows)
    all_ref[...] = jnp.zeros(all_ref.shape, bf16)
    all_ref[:, 0:unit] = mark_rows.astype(bf16)
    store = pltpu.make_async_copy(all_ref, out_ref.at[pl.ds(n * unit, 16)], sems.at[0, n])
    store.start()
    store.wait()


def pack(unit, parts):
    feature = parts[0].shape[1]
    n = len(parts)
    return pl.pallas_call(
        functools.partial(pack_kernel, unit, n),
        out_shape=sds((n * unit + 16, feature), bf16),
        in_specs=[HBM] * n,
        out_specs=HBM,
        scratch_shapes=[
            pltpu.VMEM((n, 16, feature), bf16),
            pltpu.VMEM((16, feature), bf16),
            pltpu.SemaphoreType.DMA((2, n + 1)),
        ],
        compiler_params=params(8),
        name="pack",
    )(*parts)


def learn_kernel(unit, spots, n_parts, last, with_total, half_rows, at_ref, *refs):
    parts, refs = refs[:n_parts], refs[n_parts:]
    w_ref, bias_ref, out_ref, refs = refs[0], refs[1], refs[2], refs[3:]
    if with_total:
        total_ref, vec_ref, refs = refs[0], refs[1], refs[2:]
    if last:
        given_ref, new_vec_ref, low_ref, refs = refs[0], refs[1], refs[2], refs[3:]
        rows_ref, wide_ref, mark_ref, target_ref, sems = refs
    else:
        new_total_ref, new_vec_ref, refs = refs[0], refs[1], refs[2:]
        rows_ref, low_ref, mark_ref, target_ref, sems = refs
    low_cut = half_rows // 128 * 128
    rows_all, feature = rows_ref.shape
    loads = []
    for i in range(n_parts):
        loads.append(
            pltpu.make_async_copy(
                parts[i].at[pl.ds(parts[i].shape[0] - 16, 16)], mark_ref.at[i], sems.at[0, i]
            )
        )
    for u, (part, at, _) in enumerate(spots):
        loads.append(
            pltpu.make_async_copy(
                parts[part].at[pl.ds(at, unit)],
                rows_ref.at[pl.ds(u * unit, unit)],
                sems.at[1, u],
            )
        )
    for load in loads:
        load.start()
    for load in loads:
        load.wait()
    eye = lax.broadcasted_iota(jnp.int32, (unit, unit), 0) == lax.broadcasted_iota(
        jnp.int32, (unit, unit), 1
    )
    for u, (part, _, mark_at) in enumerate(spots):
        marks = mark_ref[part, :, 0:unit].astype(f32)[mark_at : mark_at + 1]
        target_ref[u * unit : (u + 1) * unit, :] = jnp.sum(
            jnp.where(eye, marks, 0.0), axis=1, keepdims=True
        ) * at_ref[1].astype(f32)
    bias = bias_ref[...].astype(f32)
    out_weight = out_ref[...].astype(f32)
    step = 2 * unit
    hid = w_ref.shape[1]

    def forward(i, carry):
        span = pl.ds(pl.multiple_of(i * step, step), step)
        pre = jnp.dot(rows_ref[span, :], w_ref[...], preferred_element_type=f32) + bias
        gate = half_sigmoid(pre)
        hidden = pre * gate
        logit = jnp.sum(hidden * out_weight, axis=1, keepdims=True)
        mark = target_ref[span, :]
        residual = jnp.where(mark > 0.5, half_sigmoid(logit) - (mark - 1.0), 0.0)
        grad_pre = residual * out_weight * gate * (1.0 + pre * (1.0 - gate))
        low_ref[span, :] = grad_pre.astype(bf16)
        return (
            carry[0] + jnp.sum(grad_pre, axis=0, keepdims=True),
            carry[1] + jnp.sum(residual * hidden, axis=0, keepdims=True),
        )

    if with_total:
        start = (vec_ref[0:1, :], vec_ref[1:2, :])
    else:
        start = (jnp.zeros((1, hid), f32), jnp.zeros((1, hid), f32))
    grad_bias, grad_out = lax.fori_loop(0, rows_all // step, forward, start, unroll=True)

    def product(first, size):
        piece = lax.dot_general(
            rows_ref[:, first : first + size],
            low_ref[...],
            (((0,), (0,)), ((), ())),
            preferred_element_type=f32,
        )
        if with_total:
            piece = piece + total_ref[first : first + size, :]
        return piece

    tile = 128 * max(n for n in range(1, 5) if feature % (128 * n) == 0)
    if not last:
        for first in range(0, feature, tile):
            new_total_ref[first : first + tile, :] = product(first, tile)
        new_vec_ref[0:1, :] = grad_bias
        new_vec_ref[1:2, :] = grad_out
        return
    first = pl.multiple_of((1 - at_ref[0]) * low_cut, 128)
    skip = pl.multiple_of((1 - at_ref[0]) * (half_rows - low_cut), 8)
    wide_ref[...] = lax.dot_general(
        rows_ref[:, pl.ds(first, feature - low_cut)],
        low_ref[...],
        (((0,), (0,)), ((), ())),
        preferred_element_type=f32,
    )
    other = pl.multiple_of((1 - at_ref[0]) * half_rows, 8)
    given_ref[0:half_rows, :] = (
        wide_ref[pl.ds(skip, half_rows), :] + total_ref[pl.ds(other, half_rows), :]
    )
    given_ref[half_rows : half_rows + 8, :] = jnp.zeros((8, hid), f32)
    given_ref[half_rows : half_rows + 1, :] = grad_bias
    given_ref[half_rows + 1 : half_rows + 2, :] = grad_out
    new_vec_ref[0:1, :] = grad_bias
    new_vec_ref[1:2, :] = grad_out


def keep_kernel(half_rows, low_cut, unit, spots, n_parts, at_ref, *refs):
    parts, (low_ref, total_ref, out_ref, rows_ref, wide_ref, sems) = refs[:n_parts], refs[n_parts:]
    feature = rows_ref.shape[1]
    loads = []
    for u, (part, at, _) in enumerate(spots):
        loads.append(
            pltpu.make_async_copy(
                parts[part].at[pl.ds(at, unit)], rows_ref.at[pl.ds(u * unit, unit)], sems.at[u]
            )
        )
    for load in loads:
        load.start()
    for load in loads:
        load.wait()
    first = pl.multiple_of(at_ref[0] * low_cut, 128)
    skip = pl.multiple_of(at_ref[0] * (half_rows - low_cut), 8)
    wide_ref[...] = lax.dot_general(
        rows_ref[:, pl.ds(first, feature - low_cut)],
        low_ref[...],
        (((0,), (0,)), ((), ())),
        preferred_element_type=f32,
    )
    own = pl.multiple_of(at_ref[0] * half_rows, 8)
    out_ref[...] = wide_ref[pl.ds(skip, half_rows), :] + total_ref[pl.ds(own, half_rows), :]


def keep(unit, spots, parts, at, low, total):
    feature, hid = total.shape
    half = feature // 2
    low_cut = half // 128 * 128
    return pl.pallas_call(
        functools.partial(keep_kernel, half, low_cut, unit, spots, len(parts)),
        out_shape=sds((half, hid), f32),
        in_specs=[SMEM] + [HBM] * len(parts) + [VMEM, VMEM],
        out_specs=VMEM,
        scratch_shapes=[
            pltpu.VMEM((low.shape[0], feature), bf16),
            pltpu.VMEM((feature - low_cut, hid), f32),
            pltpu.SemaphoreType.DMA((len(spots),)),
        ],
        compiler_params=params(16),
        cost_estimate=spent(2),
        name="keep",
    )(at, *parts, low, total)


def learn(unit, spots, parts, at, w, bias, out, total, cost, last):
    feature, hid = w.shape
    rows_all = len(spots) * unit
    half = feature // 2
    if last:
        outs = (sds((half + 8, hid), f32), sds((2, hid), f32), sds((rows_all, hid), bf16))
        work = pltpu.VMEM((feature - half // 128 * 128, hid), f32)
    else:
        outs = (sds((feature, hid), f32), sds((2, hid), f32))
        work = pltpu.VMEM((rows_all, hid), bf16)
    extra = () if total is None else total
    kernel = functools.partial(
        learn_kernel, unit, spots, len(parts), last, total is not None, half
    )
    return pl.pallas_call(
        kernel,
        out_shape=outs,
        in_specs=[SMEM] + [HBM] * len(parts) + [VMEM] * (3 + len(extra)),
        out_specs=(VMEM,) * len(outs),
        scratch_shapes=[
            pltpu.VMEM((rows_all, feature), bf16),
            work,
            pltpu.VMEM((len(parts), 16, feature), bf16),
            pltpu.VMEM((rows_all, 1), f32),
            pltpu.SemaphoreType.DMA((2, max(len(parts), len(spots)))),
        ],
        compiler_params=params(24),
        cost_estimate=spent(cost),
        name="learn",
    )(at, *parts, w, bias, out, *extra)


def adam(old, grad, first, second):
    new_first = beta_one * first + (1.0 - beta_one) * grad
    new_second = beta_two * second + (1.0 - beta_two) * grad * grad
    new = old - learn_rate * new_first / (jnp.sqrt(new_second) + epsilon)
    return new.astype(bf16), new_first, new_second


def weights_kernel(at_ref, kept, got, w, first_w, second_w, new_half):
    new, _, _ = adam(w[...].astype(f32), kept[...] + got[...], first_w[0], second_w[0])
    new_half[...] = new


def moments_kernel(
    at_ref, kept, got, kept_vec, got_vec, half_rows, first_w, second_w, bias, out, first_vec, second_vec,
    new_full, new_vec, new_first_w, new_second_w, new_first_vec, new_second_vec,
):
    grad = kept[...] + got[...]
    new_full[0] = half_rows[...]
    new_first_w[0] = beta_one * first_w[0] + (1.0 - beta_one) * grad
    new_second_w[0] = beta_two * second_w[0] + (1.0 - beta_two) * grad * grad

    @pl.when(pl.program_id(0) == 0)
    def _():
        vec = kept_vec[...] + got_vec[0:2, :]
        for row, old in enumerate((bias, out)):
            fresh, fresh_first, fresh_second = adam(
                old[...].astype(f32),
                vec[row : row + 1],
                first_vec[0, row : row + 1],
                second_vec[0, row : row + 1],
            )
            new_vec[0, row : row + 1] = fresh
            new_first_vec[0, row : row + 1] = fresh_first
            new_second_vec[0, row : row + 1] = fresh_second


def take_step(rep, kept, kept_vec, got, w_in, bias, out, first_w, second_w, first_vec, second_vec):
    feature, hid = w_in.shape
    half = feature // 2
    tiles = max(n for n in range(1, 3) if half % (16 * n) == 0)
    tile = half // tiles
    here = pl.BlockSpec((tile, hid), lambda i, at: (i, 0))
    there = pl.BlockSpec((tile, hid), lambda i, at: (at[0] * tiles + i, 0))
    tail = pl.BlockSpec((8, hid), lambda i, at: (half // 8, 0))
    moment = pl.BlockSpec((1, tile, hid), lambda i, at: (0, i, 0))
    row = pl.BlockSpec((1, hid), lambda i, at: (0, 0))
    pair = pl.BlockSpec((2, hid), lambda i, at: (0, 0))
    pairs = pl.BlockSpec((1, 2, hid), lambda i, at: (0, 0, 0))
    full = pl.BlockSpec((1, tile, hid), lambda i, at: (0, at[0] * tiles + i, 0))
    new_half = pl.pallas_call(
        weights_kernel,
        grid_spec=pltpu.PrefetchScalarGridSpec(
            num_scalar_prefetch=1,
            grid=(tiles,),
            in_specs=[here, here, there, moment, moment],
            out_specs=here,
        ),
        out_shape=sds((half, hid), bf16),
        compiler_params=params(16),
        cost_estimate=spent(2),
        name="weights",
    )(rep, kept, got, w_in, first_w, second_w)
    other = lax.ppermute(new_half, "rep", swap)
    new_full, *rest = pl.pallas_call(
        moments_kernel,
        grid_spec=pltpu.PrefetchScalarGridSpec(
            num_scalar_prefetch=1,
            grid=(tiles,),
            in_specs=[here, here, pair, tail, here, moment, moment, row, row, pairs, pairs],
            out_specs=[full, pairs, moment, moment, pairs, pairs],
        ),
        out_shape=(
            sds((1, feature, hid), bf16),
            sds((1, 2, hid), bf16),
            sds((1, half, hid), f32),
            sds((1, half, hid), f32),
            sds((1, 2, hid), f32),
            sds((1, 2, hid), f32),
        ),
        compiler_params=params(16),
        cost_estimate=spent(3),
        name="moments",
    )(rep, kept, got, kept_vec, got, new_half, first_w, second_w, bias, out, first_vec, second_vec)
    return join(rep, other, new_full), *rest


def join_kernel(at_ref, other_ref, full_ref, out_ref, sem):
    half = other_ref.shape[0]
    start = pl.multiple_of((1 - at_ref[0]) * half, half)
    load = pltpu.make_async_copy(other_ref, out_ref.at[0, pl.ds(start, half)], sem)
    load.start()
    load.wait()


def join(rep, other, full):
    return pl.pallas_call(
        join_kernel,
        out_shape=sds(full.shape, full.dtype),
        in_specs=[SMEM, ANY, ANY],
        out_specs=ANY,
        scratch_shapes=[pltpu.SemaphoreType.DMA(())],
        input_output_aliases={2: 0},
        compiler_params=params(8),
        name="join",
    )(rep, other, full)


def gathered(
    embeddings, coverage, labels, w_in, bias_in, w_out, first_w, second_w, first_vec, second_vec
):
    planes = lax.axis_size("dp")
    heads = lax.axis_size("head")
    owners = planes * heads
    z = lax.axis_index("dp")
    q = lax.axis_index("head")
    rep = lax.axis_index("rep").reshape(1)
    blocks, rows_block, feature = embeddings.shape
    per_block = coverage.shape[1]
    slots = 2 * blocks * per_block // owners
    unit = slots * rows_block
    rows = blocks * rows_block
    outer_pairs = [(i, i ^ 1) for i in range(planes)]
    inner_pairs = [(i, i + 1 if i % 2 else i - 1) for i in range(1, planes - 1)]
    out_pairs = [(i, i ^ 1) for i in range(1, planes - 1)]
    end_pairs = [(0, planes - 1), (planes - 1, 0)]

    def exchange(units):
        return [units[0]] + [
            lax.ppermute(units[k], "head", [(i, i ^ k) for i in range(heads)])
            for k in range(1, heads)
        ]

    def plane_heads(plane, real=None):
        found = [plane * heads + (q ^ k) for k in range(heads)]
        return found if real is None else [jnp.where(real, h, -1) for h in found]

    own = make_shard(embeddings.reshape(rows, feature), coverage, labels, owners)
    inner = lax.ppermute(own, "dp", inner_pairs)
    outer = lax.ppermute(own, "dp", outer_pairs)
    always = jnp.ones((), jnp.bool_)
    at_end = (z == 0) | (z == planes - 1)

    def add(total, parts, spots, real, cost, last=False):
        scalars = jnp.stack([rep[0], real]).astype(jnp.int32)
        return learn(unit, spots, parts, scalars, w_in[0], bias_in, w_out, total, cost, last)

    first_heads = plane_heads(jnp.where(at_end, planes - 1 - z, z))
    first_units = exchange(pick(unit, per_block, [own], [(0, 0)], first_heads, [always], 0))
    far_sent = pack(unit, first_units)
    one = jnp.ones((), jnp.int32)
    first_spots = [(k, 0, 0) for k in range(heads)]
    middle = 1 - at_end.astype(jnp.int32)
    inner, far_sent = lax.optimization_barrier((inner, far_sent))
    next_out = lax.ppermute(inner, "dp", out_pairs)
    next_in = lax.ppermute(outer, "dp", inner_pairs)
    messages = pick(
        unit, per_block, [outer, inner, own], [(0, 0), (1, 2)], plane_heads(z) * 2,
        [always, jnp.logical_not(at_end)], PB,
    )
    first_units = lax.optimization_barrier((*first_units, *messages))[:heads]
    total = add(None, first_units, first_spots, middle, LA)
    near = exchange(messages)
    far_sent, next_out, next_in, *total = lax.optimization_barrier(
        (far_sent, next_out, next_in, *total)
    )
    far_got = lax.ppermute(far_sent, "dp", end_pairs)
    messages = pick(
        unit, per_block, [next_in, next_out], [(0, 1)], plane_heads(z),
        [jnp.logical_not(at_end)], PC,
    )
    messages = lax.optimization_barrier((*messages, *near))[:heads]
    rest = [
        (near, [(k, g * unit, g) for k in range(heads) for g in range(2)]),
        (exchange(messages), [(k, 0, 0) for k in range(heads)]),
    ]
    rest.append(([far_got], [(0, k * unit, k) for k in range(heads)]))

    for at, (parts, spots) in enumerate(rest):
        cost = (LB, LC, LF)[min(at, 2)]
        last = at == len(rest) - 1
        done, total = total, add(total, parts, spots, one, cost, last)
    given, kept_vec, low = total
    got = lax.ppermute(given, "rep", swap)
    kept = keep(unit, spots, parts, rep, low, done[0])
    return take_step(
        rep, kept, kept_vec, got, w_in[0], bias_in, w_out, first_w, second_w, first_vec, second_vec
    )


def routed(
    embeddings, coverage, labels, w_in, bias_in, w_out, first_w, second_w, first_vec, second_vec
):
    dp_count = lax.axis_size("dp")
    head_count = lax.axis_size("head")
    owners = dp_count * head_count
    block_count, rows_block, feature = embeddings.shape
    per_block = coverage.shape[1]
    slot_count = 2 * block_count * per_block // owners
    entries = block_count * per_block
    heads_flat = coverage.reshape(entries)
    onehot = (heads_flat[:, None] == jnp.arange(owners, dtype=jnp.int32)[None, :]).astype(jnp.int32)
    slot_rank = jnp.sum((jnp.cumsum(onehot, axis=0) - 1) * onehot, axis=1)
    target_slot = heads_flat * slot_count + slot_rank
    picker = jnp.arange(owners * slot_count, dtype=jnp.int32)[:, None] == target_slot[None, :]
    block_pick = jnp.sum(
        picker.reshape(owners * slot_count, block_count, per_block).astype(jnp.int32), axis=2
    ).astype(jnp.bfloat16)
    send_rows = jnp.dot(
        block_pick,
        embeddings.reshape(block_count, rows_block * feature),
        preferred_element_type=jnp.float32,
    ).astype(jnp.bfloat16)
    label_marks = (labels.reshape(entries, rows_block) + 1).astype(jnp.float32)
    send_marks = jnp.dot(
        picker.astype(jnp.float32), label_marks, precision=lax.Precision.HIGHEST
    ).astype(jnp.bfloat16)
    direct_rows = send_rows.reshape(owners, slot_count, rows_block, feature)
    direct_marks = send_marks.reshape(owners, slot_count, rows_block)
    got_rows, got_marks = (
        lax.all_to_all(direct_rows, ("dp", "head"), split_axis=0, concat_axis=0, tiled=True),
        lax.all_to_all(direct_marks, ("dp", "head"), split_axis=0, concat_axis=0, tiled=True),
    )
    row_data = got_rows.reshape(-1, feature)
    marks_all = got_marks.reshape(-1).astype(jnp.float32)
    usable = marks_all > 0.5
    target = marks_all - 1.0
    out_weight = w_out[0].astype(jnp.float32)
    pre_act = (
        jnp.dot(row_data, w_in[0], preferred_element_type=jnp.float32)
        + bias_in[0].astype(jnp.float32)[None, :]
    )
    sig_pre = jax.nn.sigmoid(pre_act)
    hidden = pre_act * sig_pre
    logits = jnp.sum(hidden * out_weight[None, :], axis=1)
    residual = jnp.where(usable, jax.nn.sigmoid(logits) - target, jnp.zeros_like(logits))
    grad_pre = residual[:, None] * out_weight[None, :] * sig_pre * (1.0 + pre_act * (1.0 - sig_pre))
    grad_low = grad_pre.astype(jnp.bfloat16)
    vec_part = jnp.stack([jnp.sum(grad_pre, axis=0), jnp.sum(residual[:, None] * hidden, axis=0)])
    half_rows = feature // lax.axis_size("rep")
    rep_at = lax.axis_index("rep")
    first_row = rep_at * half_rows
    grad_part = lax.dot_general(
        row_data, grad_low, (((0,), (0,)), ((), ())), preferred_element_type=jnp.float32
    ).reshape(2, half_rows, -1)
    kept = jnp.where(rep_at == 0, grad_part[0], grad_part[1])
    given = jnp.where(rep_at == 0, grad_part[1], grad_part[0])
    grad_w = kept + lax.ppermute(given, "rep", swap)
    grad_vec = vec_part + lax.ppermute(vec_part, "rep", swap)
    new_first_w = beta_one * first_w[0] + (1.0 - beta_one) * grad_w
    new_second_w = beta_two * second_w[0] + (1.0 - beta_two) * grad_w * grad_w
    old_rows = lax.dynamic_slice_in_dim(w_in[0], first_row, half_rows, 0).astype(jnp.float32)
    new_half = (old_rows - learn_rate * new_first_w / (jnp.sqrt(new_second_w) + epsilon)).astype(
        jnp.bfloat16
    )
    other_half = lax.ppermute(new_half, "rep", swap)
    new_w_in = jnp.where(
        rep_at == 0,
        jnp.concatenate([new_half, other_half]),
        jnp.concatenate([other_half, new_half]),
    )
    vector = jnp.stack([bias_in[0], w_out[0]]).astype(jnp.float32)
    new_first_vec = beta_one * first_vec[0] + (1.0 - beta_one) * grad_vec
    new_second_vec = beta_two * second_vec[0] + (1.0 - beta_two) * grad_vec * grad_vec
    new_vec = (vector - learn_rate * new_first_vec / (jnp.sqrt(new_second_vec) + epsilon)).astype(
        jnp.bfloat16
    )
    return (
        new_w_in[None],
        new_vec[None],
        new_first_w[None],
        new_second_w[None],
        new_first_vec[None],
        new_second_vec[None],
    )


def solution(mesh):
    placed = (
        P(("dp", "head", "rep"), None, None),
        P(("dp", "head", "rep"), None),
        P(("dp", "head", "rep"), None, None),
        P(("dp", "head"), None, None),
        P(("dp", "head"), None),
        P(("dp", "head"), None),
        P(("dp", "head"), "rep", None),
        P(("dp", "head"), "rep", None),
        P(("dp", "head"), None, None),
        P(("dp", "head"), None, None),
    )
    planes, heads, reps = mesh.shape["dp"], mesh.shape["head"], mesh.shape["rep"]
    short = planes == 4 and heads & (heads - 1) == 0 and reps == 2
    return jax.shard_map(
        gathered if short else routed,
        mesh=mesh,
        in_specs=placed,
        out_specs=(
            P(("dp", "head"), None, None),
            P(("dp", "head"), None, None),
            P(("dp", "head"), "rep", None),
            P(("dp", "head"), "rep", None),
            P(("dp", "head"), None, None),
            P(("dp", "head"), None, None),
        ),
        check_vma=False,
    )
```

```python
import functools

import jax
import jax.numpy as jnp
from jax import lax
from jax.experimental import pallas as pl
from jax.experimental.pallas import tpu as pltpu
from jax.sharding import PartitionSpec as P

beta_one = 0.9
beta_two = 0.999
learn_rate = 0.001
epsilon = 1e-08
swap = [(0, 1), (1, 0)]
PB, PC, LA, LB, LC, LF = (30, 5, 0, 5, 0, 0)
bf16 = jnp.bfloat16
MIB = 1024 * 1024
ROOM = 60
ANY = pl.BlockSpec(memory_space=pl.ANY)
VMEM = pl.BlockSpec(memory_space=pltpu.VMEM)
HBM = pl.BlockSpec(memory_space=pltpu.HBM)
SMEM = pl.BlockSpec(memory_space=pltpu.SMEM)
f32 = jnp.float32


def spent(us):
    return pl.CostEstimate(flops=int(us * 1150000000) + 1, bytes_accessed=1, transcendentals=0)


def params(mib):
    return pltpu.CompilerParams(vmem_limit_bytes=mib * MIB)


def sds(shape, dtype):
    return jax.ShapeDtypeStruct(shape, dtype)


def half_sigmoid(x):
    return 0.5 * jnp.tanh(0.5 * x) + 0.5


def shard_kernel(owners, cov_hbm, lab_hbm, own_ref, out_ref, cov_ref, lab_ref, held_ref, sems):
    per_block, blocks = cov_ref.shape
    rows_block = lab_ref.shape[1]
    rows = blocks * rows_block
    load_cov = pltpu.make_async_copy(cov_hbm, cov_ref, sems.at[0])
    load_lab = pltpu.make_async_copy(lab_hbm, lab_ref, sems.at[1])
    half = rows // 2
    loads = []
    stores = []
    for i in range(2):
        part = pl.ds(i * half, half)
        loads.append(pltpu.make_async_copy(own_ref.at[part], held_ref.at[part], sems.at[2 + i]))
        stores.append(pltpu.make_async_copy(held_ref.at[part], out_ref.at[part], sems.at[4 + i]))
    load_cov.start()
    load_lab.start()
    for load in loads:
        load.start()
    for load, store in zip(loads, stores):
        load.wait()
        store.start()
    load_cov.wait()
    load_lab.wait()
    cov = cov_ref[...]
    heads_at = lax.broadcasted_iota(jnp.int32, (owners, blocks), 0)
    named = (cov[0:1] == heads_at).astype(f32)
    for t in range(1, per_block):
        named = named + (cov[t : t + 1] == heads_at).astype(f32)
    block_of = lax.broadcasted_iota(jnp.int32, (blocks, rows), 1) // rows_block
    block_at = lax.broadcasted_iota(jnp.int32, (blocks, rows), 0)
    same = (block_of == block_at).astype(bf16)
    before = (block_at < block_of).astype(bf16)
    rank = jnp.dot(named.astype(bf16), before, preferred_element_type=f32)
    cov_rows = jnp.dot(cov.astype(f32).astype(bf16), same, preferred_element_type=f32)
    row_in = lax.broadcasted_iota(jnp.int32, (rows_block, rows), 1) % rows_block
    row_at = lax.broadcasted_iota(jnp.int32, (rows_block, rows), 0)
    head_rows = lax.broadcasted_iota(jnp.int32, (owners, rows), 0).astype(f32)
    at_mark = lax.broadcasted_iota(jnp.int32, (16, rows), 0)
    mark_rows = jnp.zeros((16, rows), f32)
    for t in range(per_block):
        mine = cov_rows[t : t + 1]
        own_rank = jnp.sum(jnp.where(mine == head_rows, rank, 0.0), axis=0, keepdims=True)
        place = own_rank * rows_block + row_in[0:1].astype(f32)
        spread = jnp.dot(lab_ref[t].astype(f32).astype(bf16), same, preferred_element_type=f32)
        label = 1.0 + jnp.sum(jnp.where(row_in == row_at, spread, 0.0), axis=0, keepdims=True)
        mark_rows = jnp.where(at_mark == t, mine, mark_rows)
        mark_rows = jnp.where(at_mark == per_block + t, place, mark_rows)
        mark_rows = jnp.where(at_mark == 2 * per_block + t, label, mark_rows)
    held_ref[rows:, :] = jnp.zeros((16, held_ref.shape[1]), bf16)
    held_ref[rows:, 0:rows] = mark_rows.astype(bf16)
    last = pl.ds(rows, 16)
    stores.append(pltpu.make_async_copy(held_ref.at[last], out_ref.at[last], sems.at[6]))
    stores[-1].start()
    for store in stores:
        store.wait()


def make_shard(own, coverage, labels, owners):
    rows, feature = own.shape
    return pl.pallas_call(
        functools.partial(shard_kernel, owners),
        out_shape=sds((rows + 16, feature), bf16),
        in_specs=[HBM, HBM, HBM],
        out_specs=HBM,
        scratch_shapes=[
            pltpu.VMEM((coverage.shape[1], coverage.shape[0]), jnp.int32),
            pltpu.VMEM((labels.shape[1], labels.shape[2], labels.shape[0]), jnp.int32),
            pltpu.VMEM((rows + 16, feature), bf16),
            pltpu.SemaphoreType.DMA((7,)),
        ],
        compiler_params=params(ROOM),
        name="shard",
    )(coverage.T, labels.transpose(1, 2, 0), own)


def pick_rows(marks, shard, heads, unit, per_block):
    rows = marks.shape[1]
    slot = lax.broadcasted_iota(jnp.int32, (unit, rows), 0).astype(f32)
    at_head = lax.broadcasted_iota(jnp.int32, (8, rows), 0)
    chosen = []
    labels = jnp.zeros((8, rows), f32)
    for k, head in enumerate(heads):
        place = jnp.full((1, rows), -1.0, f32)
        label = jnp.zeros((1, rows), f32)
        for t in range(per_block):
            mine = marks[t : t + 1] == head
            place = jnp.where(mine, marks[per_block + t : per_block + t + 1], place)
            label = jnp.where(mine, marks[2 * per_block + t : 2 * per_block + t + 1], label)
        chosen.append(jnp.where(place == slot, 1.0, 0.0).astype(bf16))
        labels = jnp.where(at_head == k, label, labels)
    chosen = jnp.concatenate(chosen, axis=0)
    picked = jnp.dot(chosen, shard, preferred_element_type=f32).astype(bf16)
    mark = lax.dot_general(
        labels.astype(bf16), chosen, (((1,), (1,)), ((), ())), preferred_element_type=f32
    )
    return picked, mark


def pick_kernel(unit, per_block, plan, n_shards, n_heads, at_ref, *refs):
    shards, refs = refs[:n_shards], refs[n_shards:]
    outs, refs = refs[:n_heads], refs[n_heads:]
    held, ready, in_sems, out_sems = refs
    units = len(plan)
    rows = held.shape[1] - 16

    for g, (yes, no) in enumerate(plan):
        if yes == no:
            pltpu.make_async_copy(shards[yes], held.at[g], in_sems.at[g]).start()
        else:
            flag = at_ref[units * n_heads + g] > 0

            @pl.when(flag)
            def _():
                pltpu.make_async_copy(shards[yes], held.at[g], in_sems.at[g]).start()

            @pl.when(jnp.logical_not(flag))
            def _():
                pltpu.make_async_copy(shards[no], held.at[g], in_sems.at[g]).start()

    at_mark = lax.broadcasted_iota(jnp.int32, (16, unit), 0)
    mark_rows = [jnp.zeros((16, unit), f32)] * n_heads
    for g, (yes, _) in enumerate(plan):
        pltpu.make_async_copy(shards[yes], held.at[g], in_sems.at[g]).wait()
        marks = held[g, rows:, 0:rows].astype(f32)
        wanted = [at_ref[g * n_heads + k].astype(f32) for k in range(n_heads)]
        picked, mark = pick_rows(marks, held[g, 0:rows], wanted, unit, per_block)
        for k in range(n_heads):
            ready[k, g * unit : (g + 1) * unit, :] = picked[k * unit : (k + 1) * unit]
            own_mark = mark[k : k + 1, k * unit : (k + 1) * unit]
            mark_rows[k] = jnp.where(at_mark == g, own_mark, mark_rows[k])
    for k in range(n_heads):
        ready[k, units * unit :, :] = jnp.zeros((16, ready.shape[2]), bf16)
        ready[k, units * unit :, 0:unit] = mark_rows[k].astype(bf16)
        pltpu.make_async_copy(ready.at[k], outs[k], out_sems.at[k]).start()
    for k in range(n_heads):
        pltpu.make_async_copy(ready.at[k], outs[k], out_sems.at[k]).wait()


def pick(unit, per_block, shards, plan, heads_at, flags, cost):
    rows, feature = shards[0].shape
    units = len(plan)
    n_heads = len(heads_at) // units
    size = units * unit + 16
    return pl.pallas_call(
        functools.partial(pick_kernel, unit, per_block, plan, len(shards), n_heads),
        out_shape=[sds((size, feature), bf16)] * n_heads,
        in_specs=[SMEM] + [HBM] * len(shards),
        out_specs=[HBM] * n_heads,
        scratch_shapes=[
            pltpu.VMEM((units, rows, feature), bf16),
            pltpu.VMEM((n_heads, size, feature), bf16),
            pltpu.SemaphoreType.DMA((units,)),
            pltpu.SemaphoreType.DMA((n_heads,)),
        ],
        compiler_params=params(16),
        cost_estimate=spent(cost),
        name="pick",
    )(jnp.stack(heads_at + flags).astype(jnp.int32), *shards)


def pack_kernel(unit, n, *refs):
    parts, out_ref, mark_ref, all_ref, sems = refs[:n], *refs[n:]
    loads = []
    for k in range(n):
        loads.append(
            pltpu.make_async_copy(
                parts[k].at[pl.ds(0, unit)], out_ref.at[pl.ds(k * unit, unit)], sems.at[0, k]
            )
        )
        loads.append(
            pltpu.make_async_copy(
                parts[k].at[pl.ds(unit, 16)], mark_ref.at[k], sems.at[1, k]
            )
        )
    for load in loads:
        load.start()
    for load in loads:
        load.wait()
    at_mark = lax.broadcasted_iota(jnp.int32, (16, unit), 0)
    mark_rows = jnp.zeros((16, unit), f32)
    for k in range(n):
        marks = mark_ref[k, :, 0:unit].astype(f32)
        mark_rows = jnp.where(at_mark == k, marks[0:1], mark_rows)
    all_ref[...] = jnp.zeros(all_ref.shape, bf16)
    all_ref[:, 0:unit] = mark_rows.astype(bf16)
    store = pltpu.make_async_copy(all_ref, out_ref.at[pl.ds(n * unit, 16)], sems.at[0, n])
    store.start()
    store.wait()


def pack(unit, parts):
    feature = parts[0].shape[1]
    n = len(parts)
    return pl.pallas_call(
        functools.partial(pack_kernel, unit, n),
        out_shape=sds((n * unit + 16, feature), bf16),
        in_specs=[HBM] * n,
        out_specs=HBM,
        scratch_shapes=[
            pltpu.VMEM((n, 16, feature), bf16),
            pltpu.VMEM((16, feature), bf16),
            pltpu.SemaphoreType.DMA((2, n + 1)),
        ],
        compiler_params=params(8),
        name="pack",
    )(*parts)


def learn_kernel(unit, spots, n_parts, mode, with_total, half_rows, at_ref, *refs):
    parts, refs = refs[:n_parts], refs[n_parts:]
    w_ref, bias_ref, out_ref, refs = refs[0], refs[1], refs[2], refs[3:]
    if with_total:
        total_ref, vec_ref, refs = refs[0], refs[1], refs[2:]
    if mode == "rows":
        low_ref, new_vec_ref, refs = refs[0], refs[1], refs[2:]
        rows_ref, mark_ref, target_ref, sems = refs
    elif mode == "halves":
        kept_ref, given_ref, new_vec_ref, refs = refs[0], refs[1], refs[2], refs[3:]
        rows_ref, low_ref, mark_ref, target_ref, sems = refs
    else:
        new_total_ref, new_vec_ref, refs = refs[0], refs[1], refs[2:]
        rows_ref, low_ref, mark_ref, target_ref, sems = refs
    rows_all, feature = rows_ref.shape
    loads = []
    for i in range(n_parts):
        loads.append(
            pltpu.make_async_copy(
                parts[i].at[pl.ds(parts[i].shape[0] - 16, 16)], mark_ref.at[i], sems.at[0, i]
            )
        )
    for u, (part, at, _) in enumerate(spots):
        loads.append(
            pltpu.make_async_copy(
                parts[part].at[pl.ds(at, unit)],
                rows_ref.at[pl.ds(u * unit, unit)],
                sems.at[1, u],
            )
        )
    for load in loads:
        load.start()
    for load in loads:
        load.wait()
    eye = lax.broadcasted_iota(jnp.int32, (unit, unit), 0) == lax.broadcasted_iota(
        jnp.int32, (unit, unit), 1
    )
    for u, (part, _, mark_at) in enumerate(spots):
        marks = mark_ref[part, :, 0:unit].astype(f32)[mark_at : mark_at + 1]
        target_ref[u * unit : (u + 1) * unit, :] = jnp.sum(
            jnp.where(eye, marks, 0.0), axis=1, keepdims=True
        ) * at_ref[1].astype(f32)
    bias = bias_ref[...].astype(f32)
    out_weight = out_ref[...].astype(f32)
    step = 2 * unit
    hid = w_ref.shape[1]

    def forward(i, carry):
        span = pl.ds(pl.multiple_of(i * step, step), step)
        pre = jnp.dot(rows_ref[span, :], w_ref[...], preferred_element_type=f32) + bias
        gate = half_sigmoid(pre)
        hidden = pre * gate
        logit = jnp.sum(hidden * out_weight, axis=1, keepdims=True)
        mark = target_ref[span, :]
        residual = jnp.where(mark > 0.5, half_sigmoid(logit) - (mark - 1.0), 0.0)
        grad_pre = residual * out_weight * gate * (1.0 + pre * (1.0 - gate))
        low_ref[span, :] = grad_pre.astype(bf16)
        return (
            carry[0] + jnp.sum(grad_pre, axis=0, keepdims=True),
            carry[1] + jnp.sum(residual * hidden, axis=0, keepdims=True),
        )

    if with_total:
        start = (vec_ref[0:1, :], vec_ref[1:2, :])
    else:
        start = (jnp.zeros((1, hid), f32), jnp.zeros((1, hid), f32))
    grad_bias, grad_out = lax.fori_loop(0, rows_all // step, forward, start, unroll=True)

    def product(first, size):
        piece = lax.dot_general(
            rows_ref[:, first : first + size],
            low_ref[...],
            (((0,), (0,)), ((), ())),
            preferred_element_type=f32,
        )
        if with_total:
            piece = piece + total_ref[first : first + size, :]
        return piece

    new_vec_ref[...] = jnp.zeros(new_vec_ref.shape, f32)
    new_vec_ref[0:1, :] = grad_bias
    new_vec_ref[1:2, :] = grad_out
    if mode == "rows":
        return
    tile = 128 * max(n for n in range(1, 5) if feature % (128 * n) == 0)
    if mode == "total":
        for first in range(0, feature, tile):
            new_total_ref[first : first + tile, :] = product(first, tile)
        return
    given_ref[half_rows:, :] = new_vec_ref[...]
    for first in range(0, feature, tile):
        piece = product(first, tile)
        cut = min(max(half_rows - first, 0), tile)
        for core in range(2):
            low_half, high_half = (kept_ref, given_ref) if core == 0 else (given_ref, kept_ref)

            @pl.when(at_ref[0] == core)
            def _():
                if cut > 0:
                    low_half[first : first + cut, :] = piece[:cut]
                if cut < tile:
                    high_half[first + cut - half_rows : first + tile - half_rows, :] = piece[cut:]


def keep_kernel(half_rows, low_cut, unit, spots, n_parts, at_ref, *refs):
    parts, (low_ref, kept_ref, out_ref, rows_ref, wide_ref, sems) = refs[:n_parts], refs[n_parts:]
    feature = rows_ref.shape[1]
    loads = []
    for u, (part, at, _) in enumerate(spots):
        loads.append(
            pltpu.make_async_copy(
                parts[part].at[pl.ds(at, unit)], rows_ref.at[pl.ds(u * unit, unit)], sems.at[u]
            )
        )
    for load in loads:
        load.start()
    for load in loads:
        load.wait()
    first = pl.multiple_of(at_ref[0] * low_cut, 128)
    skip = pl.multiple_of(at_ref[0] * (half_rows - low_cut), 8)
    wide_ref[...] = lax.dot_general(
        rows_ref[:, pl.ds(first, feature - low_cut)],
        low_ref[...],
        (((0,), (0,)), ((), ())),
        preferred_element_type=f32,
    )
    out_ref[...] = wide_ref[pl.ds(skip, half_rows), :] + kept_ref[...]


def keep(unit, spots, parts, at, low, kept):
    feature = parts[0].shape[1]
    half, hid = kept.shape
    low_cut = half // 128 * 128
    return pl.pallas_call(
        functools.partial(keep_kernel, half, low_cut, unit, spots, len(parts)),
        out_shape=sds((half, hid), f32),
        in_specs=[SMEM] + [HBM] * len(parts) + [VMEM, VMEM],
        out_specs=VMEM,
        scratch_shapes=[
            pltpu.VMEM((low.shape[0], feature), bf16),
            pltpu.VMEM((feature - low_cut, hid), f32),
            pltpu.SemaphoreType.DMA((len(spots),)),
        ],
        compiler_params=params(16),
        cost_estimate=spent(2),
        name="keep",
    )(at, *parts, low, kept)


def learn(unit, spots, parts, at, w, bias, out, total, cost, mode):
    feature, hid = w.shape
    rows_all = len(spots) * unit
    half = feature // 2
    work = (pltpu.VMEM((rows_all, hid), bf16),)
    if mode == "rows":
        outs, work = (sds((rows_all, hid), bf16), sds((8, hid), f32)), ()
    elif mode == "halves":
        outs = (sds((half, hid), f32), sds((half + 8, hid), f32), sds((8, hid), f32))
    else:
        outs = (sds((feature, hid), f32), sds((8, hid), f32))
    extra = () if total is None else total
    kernel = functools.partial(
        learn_kernel, unit, spots, len(parts), mode, total is not None, half
    )
    return pl.pallas_call(
        kernel,
        out_shape=outs,
        in_specs=[SMEM] + [HBM] * len(parts) + [VMEM] * (3 + len(extra)),
        out_specs=(VMEM,) * len(outs),
        scratch_shapes=[
            pltpu.VMEM((rows_all, feature), bf16),
            *work,
            pltpu.VMEM((len(parts), 16, feature), bf16),
            pltpu.VMEM((rows_all, 1), f32),
            pltpu.SemaphoreType.DMA((2, max(len(parts), len(spots)))),
        ],
        compiler_params=params(24),
        cost_estimate=spent(cost),
        name="learn",
    )(at, *parts, w, bias, out, *extra)


def adam(old, grad, first, second):
    new_first = beta_one * first + (1.0 - beta_one) * grad
    new_second = beta_two * second + (1.0 - beta_two) * grad * grad
    new = old - learn_rate * new_first / (jnp.sqrt(new_second) + epsilon)
    return new.astype(bf16), new_first, new_second


def weights_kernel(
    low_cut, n_tiles, at_ref, rows_ref, low_ref, kept, got, w, first_w, second_w, new_half, grad_ref, wide_ref
):
    half = kept.shape[0]
    first = pl.multiple_of(at_ref[0] * low_cut, 128)
    skip = pl.multiple_of(at_ref[0] * (half - low_cut), 8)
    own = pl.multiple_of(at_ref[0] * half, 16)
    wide_ref[...] = lax.dot_general(
        rows_ref[0 : low_ref.shape[0], pl.ds(first, rows_ref.shape[1] - low_cut)],
        low_ref[...],
        (((0,), (0,)), ((), ())),
        preferred_element_type=f32,
    )
    tile = half // n_tiles
    for i in range(n_tiles):
        span = pl.ds(i * tile, tile)
        there = pl.ds(pl.multiple_of(own + i * tile, 16), tile)
        there_wide = pl.ds(pl.multiple_of(skip + i * tile, 8), tile)
        grad = kept[span, :] + got[span, :] + wide_ref[there_wide, :]
        new, _, _ = adam(w[there, :].astype(f32), grad, first_w[0, span, :], second_w[0, span, :])
        new_half[span, :] = new
        grad_ref[span, :] = grad


def moments_kernel(
    at_ref, grad_ref, vec_near, vec_far, vec_other, got_vec, half_rows, first_w, second_w, bias, out,
    first_vec, second_vec,
    new_full, new_vec, new_first_w, new_second_w, new_first_vec, new_second_vec,
):
    grad = grad_ref[...]
    new_full[0] = half_rows[...]
    new_first_w[0] = beta_one * first_w[0] + (1.0 - beta_one) * grad
    new_second_w[0] = beta_two * second_w[0] + (1.0 - beta_two) * grad * grad

    @pl.when(pl.program_id(0) == 0)
    def _():
        vec = (vec_near[0:2, :] + vec_far[0:2, :]) + (got_vec[0:2, :] + vec_other[0:2, :])
        for row, old in enumerate((bias, out)):
            fresh, fresh_first, fresh_second = adam(
                old[...].astype(f32),
                vec[row : row + 1],
                first_vec[0, row : row + 1],
                second_vec[0, row : row + 1],
            )
            new_vec[0, row : row + 1] = fresh
            new_first_vec[0, row : row + 1] = fresh_first
            new_second_vec[0, row : row + 1] = fresh_second


def take_step(
    rep, rows, low, kept, got, vecs, w_in, bias, out, first_w, second_w, first_vec, second_vec
):
    feature, hid = w_in.shape
    half = feature // 2
    low_cut = half // 128 * 128
    tiles = max(n for n in range(1, 3) if half % (16 * n) == 0)
    tile = half // tiles
    here = pl.BlockSpec((tile, hid), lambda i, at: (i, 0))
    tail = pl.BlockSpec((8, hid), lambda i, at: (half // 8, 0))
    top = pl.BlockSpec((8, hid), lambda i, at: (0, 0))
    moment = pl.BlockSpec((1, tile, hid), lambda i, at: (0, i, 0))
    row = pl.BlockSpec((1, hid), lambda i, at: (0, 0))
    pairs = pl.BlockSpec((1, 2, hid), lambda i, at: (0, 0, 0))
    full = pl.BlockSpec((1, tile, hid), lambda i, at: (0, at[0] * tiles + i, 0))
    new_half, grad = pl.pallas_call(
        functools.partial(weights_kernel, low_cut, 2 * tiles),
        in_specs=[SMEM] + [VMEM] * 7,
        out_specs=[VMEM, VMEM],
        out_shape=(sds((half, hid), bf16), sds((half, hid), f32)),
        scratch_shapes=[pltpu.VMEM((feature - low_cut, hid), f32)],
        compiler_params=params(16),
        cost_estimate=spent(2),
        name="weights",
    )(rep, rows, low, kept, got, w_in, first_w, second_w)
    other = lax.ppermute(new_half, "rep", swap)
    new_full, *rest = pl.pallas_call(
        moments_kernel,
        grid_spec=pltpu.PrefetchScalarGridSpec(
            num_scalar_prefetch=1,
            grid=(tiles,),
            in_specs=[here, top, top, top, tail, here, moment, moment, row, row, pairs, pairs],
            out_specs=[full, pairs, moment, moment, pairs, pairs],
        ),
        out_shape=(
            sds((1, feature, hid), bf16),
            sds((1, 2, hid), bf16),
            sds((1, half, hid), f32),
            sds((1, half, hid), f32),
            sds((1, 2, hid), f32),
            sds((1, 2, hid), f32),
        ),
        compiler_params=params(16),
        cost_estimate=spent(3),
        name="moments",
    )(rep, grad, *vecs, got, new_half, first_w, second_w, bias, out, first_vec, second_vec)
    return join(rep, other, new_full), *rest


def join_kernel(at_ref, other_ref, full_ref, out_ref, sem):
    half = other_ref.shape[0]
    start = pl.multiple_of((1 - at_ref[0]) * half, half)
    load = pltpu.make_async_copy(other_ref, out_ref.at[0, pl.ds(start, half)], sem)
    load.start()
    load.wait()


def join(rep, other, full):
    return pl.pallas_call(
        join_kernel,
        out_shape=sds(full.shape, full.dtype),
        in_specs=[SMEM, ANY, ANY],
        out_specs=ANY,
        scratch_shapes=[pltpu.SemaphoreType.DMA(())],
        input_output_aliases={2: 0},
        compiler_params=params(8),
        name="join",
    )(rep, other, full)


def gathered(
    embeddings, coverage, labels, w_in, bias_in, w_out, first_w, second_w, first_vec, second_vec
):
    planes = lax.axis_size("dp")
    heads = lax.axis_size("head")
    owners = planes * heads
    z = lax.axis_index("dp")
    q = lax.axis_index("head")
    rep = lax.axis_index("rep").reshape(1)
    blocks, rows_block, feature = embeddings.shape
    per_block = coverage.shape[1]
    slots = 2 * blocks * per_block // owners
    unit = slots * rows_block
    rows = blocks * rows_block
    outer_pairs = [(i, i ^ 1) for i in range(planes)]
    inner_pairs = [(i, i + 1 if i % 2 else i - 1) for i in range(1, planes - 1)]
    out_pairs = [(i, i ^ 1) for i in range(1, planes - 1)]
    end_pairs = [(0, planes - 1), (planes - 1, 0)]

    def exchange(units):
        return [units[0]] + [
            lax.ppermute(units[k], "head", [(i, i ^ k) for i in range(heads)])
            for k in range(1, heads)
        ]

    def plane_heads(plane, real=None):
        found = [plane * heads + (q ^ k) for k in range(heads)]
        return found if real is None else [jnp.where(real, h, -1) for h in found]

    own = make_shard(embeddings.reshape(rows, feature), coverage, labels, owners)
    inner = lax.ppermute(own, "dp", inner_pairs)
    outer = lax.ppermute(own, "dp", outer_pairs)
    always = jnp.ones((), jnp.bool_)
    at_end = (z == 0) | (z == planes - 1)

    def add(total, parts, spots, real, cost, mode="total"):
        scalars = jnp.stack([rep[0], real]).astype(jnp.int32)
        return learn(unit, spots, parts, scalars, w_in[0], bias_in, w_out, total, cost, mode)

    first_heads = plane_heads(jnp.where(at_end, planes - 1 - z, z))
    first_units = exchange(pick(unit, per_block, [own], [(0, 0)], first_heads, [always], 0))
    far_sent = pack(unit, first_units)
    one = jnp.ones((), jnp.int32)
    first_spots = [(k, 0, 0) for k in range(heads)]
    middle = 1 - at_end.astype(jnp.int32)
    inner, far_sent = lax.optimization_barrier((inner, far_sent))
    next_out = lax.ppermute(inner, "dp", out_pairs)
    next_in = lax.ppermute(outer, "dp", inner_pairs)
    messages = pick(
        unit, per_block, [outer, inner, own], [(0, 0), (1, 2)], plane_heads(z) * 2,
        [always, jnp.logical_not(at_end)], PB,
    )
    first_units = lax.optimization_barrier((*first_units, *messages))[:heads]
    total = add(None, first_units, first_spots, middle, LA)
    near = exchange(messages)
    far_sent, next_out, next_in, *total = lax.optimization_barrier(
        (far_sent, next_out, next_in, *total)
    )
    far_got = lax.ppermute(far_sent, "dp", end_pairs)
    messages = pick(
        unit, per_block, [next_in, next_out], [(0, 1)], plane_heads(z),
        [jnp.logical_not(at_end)], PC,
    )
    messages = lax.optimization_barrier((*messages, *near))[:heads]
    rest = [
        (near, [(k, g * unit, g) for k in range(heads) for g in range(2)]),
        (exchange(messages), [(k, 0, 0) for k in range(heads)]),
    ]
    for at, (parts, spots) in enumerate(rest):
        last = at == len(rest) - 1
        total = add(total, parts, spots, one, (LB, LC)[min(at, 1)], "halves" if last else "total")
    kept, given, vec_near = total
    got = lax.ppermute(given, "rep", swap)
    far_other = lax.ppermute(far_got, "rep", swap)
    spots = [(0, k * unit, k) for k in range(heads)]
    low, vec_far = add(None, [far_got], spots, one, LF, "rows")
    low_other = lax.ppermute(low, "rep", swap)
    vec_other = lax.ppermute(vec_far, "rep", swap)
    low_other, vec_other = lax.optimization_barrier((low_other, vec_other))
    kept = keep(unit, spots, [far_got], rep, low, kept)
    return take_step(
        rep, far_other, low_other, kept, got, [vec_near, vec_far, vec_other], w_in[0], bias_in, w_out,
        first_w, second_w, first_vec, second_vec,
    )


def routed(
    embeddings, coverage, labels, w_in, bias_in, w_out, first_w, second_w, first_vec, second_vec
):
    dp_count = lax.axis_size("dp")
    head_count = lax.axis_size("head")
    owners = dp_count * head_count
    block_count, rows_block, feature = embeddings.shape
    per_block = coverage.shape[1]
    slot_count = 2 * block_count * per_block // owners
    entries = block_count * per_block
    heads_flat = coverage.reshape(entries)
    onehot = (heads_flat[:, None] == jnp.arange(owners, dtype=jnp.int32)[None, :]).astype(jnp.int32)
    slot_rank = jnp.sum((jnp.cumsum(onehot, axis=0) - 1) * onehot, axis=1)
    target_slot = heads_flat * slot_count + slot_rank
    picker = jnp.arange(owners * slot_count, dtype=jnp.int32)[:, None] == target_slot[None, :]
    block_pick = jnp.sum(
        picker.reshape(owners * slot_count, block_count, per_block).astype(jnp.int32), axis=2
    ).astype(jnp.bfloat16)
    send_rows = jnp.dot(
        block_pick,
        embeddings.reshape(block_count, rows_block * feature),
        preferred_element_type=jnp.float32,
    ).astype(jnp.bfloat16)
    label_marks = (labels.reshape(entries, rows_block) + 1).astype(jnp.float32)
    send_marks = jnp.dot(
        picker.astype(jnp.float32), label_marks, precision=lax.Precision.HIGHEST
    ).astype(jnp.bfloat16)
    direct_rows = send_rows.reshape(owners, slot_count, rows_block, feature)
    direct_marks = send_marks.reshape(owners, slot_count, rows_block)
    got_rows, got_marks = (
        lax.all_to_all(direct_rows, ("dp", "head"), split_axis=0, concat_axis=0, tiled=True),
        lax.all_to_all(direct_marks, ("dp", "head"), split_axis=0, concat_axis=0, tiled=True),
    )
    row_data = got_rows.reshape(-1, feature)
    marks_all = got_marks.reshape(-1).astype(jnp.float32)
    usable = marks_all > 0.5
    target = marks_all - 1.0
    out_weight = w_out[0].astype(jnp.float32)
    pre_act = (
        jnp.dot(row_data, w_in[0], preferred_element_type=jnp.float32)
        + bias_in[0].astype(jnp.float32)[None, :]
    )
    sig_pre = jax.nn.sigmoid(pre_act)
    hidden = pre_act * sig_pre
    logits = jnp.sum(hidden * out_weight[None, :], axis=1)
    residual = jnp.where(usable, jax.nn.sigmoid(logits) - target, jnp.zeros_like(logits))
    grad_pre = residual[:, None] * out_weight[None, :] * sig_pre * (1.0 + pre_act * (1.0 - sig_pre))
    grad_low = grad_pre.astype(jnp.bfloat16)
    vec_part = jnp.stack([jnp.sum(grad_pre, axis=0), jnp.sum(residual[:, None] * hidden, axis=0)])
    half_rows = feature // lax.axis_size("rep")
    rep_at = lax.axis_index("rep")
    first_row = rep_at * half_rows
    grad_part = lax.dot_general(
        row_data, grad_low, (((0,), (0,)), ((), ())), preferred_element_type=jnp.float32
    ).reshape(2, half_rows, -1)
    kept = jnp.where(rep_at == 0, grad_part[0], grad_part[1])
    given = jnp.where(rep_at == 0, grad_part[1], grad_part[0])
    grad_w = kept + lax.ppermute(given, "rep", swap)
    grad_vec = vec_part + lax.ppermute(vec_part, "rep", swap)
    new_first_w = beta_one * first_w[0] + (1.0 - beta_one) * grad_w
    new_second_w = beta_two * second_w[0] + (1.0 - beta_two) * grad_w * grad_w
    old_rows = lax.dynamic_slice_in_dim(w_in[0], first_row, half_rows, 0).astype(jnp.float32)
    new_half = (old_rows - learn_rate * new_first_w / (jnp.sqrt(new_second_w) + epsilon)).astype(
        jnp.bfloat16
    )
    other_half = lax.ppermute(new_half, "rep", swap)
    new_w_in = jnp.where(
        rep_at == 0,
        jnp.concatenate([new_half, other_half]),
        jnp.concatenate([other_half, new_half]),
    )
    vector = jnp.stack([bias_in[0], w_out[0]]).astype(jnp.float32)
    new_first_vec = beta_one * first_vec[0] + (1.0 - beta_one) * grad_vec
    new_second_vec = beta_two * second_vec[0] + (1.0 - beta_two) * grad_vec * grad_vec
    new_vec = (vector - learn_rate * new_first_vec / (jnp.sqrt(new_second_vec) + epsilon)).astype(
        jnp.bfloat16
    )
    return (
        new_w_in[None],
        new_vec[None],
        new_first_w[None],
        new_second_w[None],
        new_first_vec[None],
        new_second_vec[None],
    )


def solution(mesh):
    placed = (
        P(("dp", "head", "rep"), None, None),
        P(("dp", "head", "rep"), None),
        P(("dp", "head", "rep"), None, None),
        P(("dp", "head"), None, None),
        P(("dp", "head"), None),
        P(("dp", "head"), None),
        P(("dp", "head"), "rep", None),
        P(("dp", "head"), "rep", None),
        P(("dp", "head"), None, None),
        P(("dp", "head"), None, None),
    )
    planes, heads, reps = mesh.shape["dp"], mesh.shape["head"], mesh.shape["rep"]
    short = planes == 4 and heads & (heads - 1) == 0 and reps == 2
    return jax.shard_map(
        gathered if short else routed,
        mesh=mesh,
        in_specs=placed,
        out_specs=(
            P(("dp", "head"), None, None),
            P(("dp", "head"), None, None),
            P(("dp", "head"), "rep", None),
            P(("dp", "head"), "rep", None),
            P(("dp", "head"), None, None),
            P(("dp", "head"), None, None),
        ),
        check_vma=False,
    )
```

```python
import functools

import jax
import jax.numpy as jnp
from jax import lax
from jax.experimental import pallas as pl
from jax.experimental.pallas import tpu as pltpu
from jax.sharding import PartitionSpec as P

beta_one = 0.9
beta_two = 0.999
learn_rate = 0.001
epsilon = 1e-08
swap = [(0, 1), (1, 0)]
PB, PC, LA, LB, LC, LF = (30, 5, 0, 5, 0, 0)
bf16 = jnp.bfloat16
MIB = 1024 * 1024
ROOM = 60
ANY = pl.BlockSpec(memory_space=pl.ANY)
VMEM = pl.BlockSpec(memory_space=pltpu.VMEM)
HBM = pl.BlockSpec(memory_space=pltpu.HBM)
SMEM = pl.BlockSpec(memory_space=pltpu.SMEM)
f32 = jnp.float32


def spent(us):
    return pl.CostEstimate(flops=int(us * 1150000000) + 1, bytes_accessed=1, transcendentals=0)


def params(mib):
    return pltpu.CompilerParams(vmem_limit_bytes=mib * MIB)


def sds(shape, dtype):
    return jax.ShapeDtypeStruct(shape, dtype)


def half_sigmoid(x):
    return 0.5 * jnp.tanh(0.5 * x) + 0.5


def shard_kernel(owners, cov_hbm, lab_hbm, own_ref, out_ref, cov_ref, lab_ref, held_ref, sems):
    per_block, blocks = cov_ref.shape
    rows_block = lab_ref.shape[1]
    rows = blocks * rows_block
    load_cov = pltpu.make_async_copy(cov_hbm, cov_ref, sems.at[0])
    load_lab = pltpu.make_async_copy(lab_hbm, lab_ref, sems.at[1])
    half = rows // 2
    loads = []
    stores = []
    for i in range(2):
        part = pl.ds(i * half, half)
        loads.append(pltpu.make_async_copy(own_ref.at[part], held_ref.at[part], sems.at[2 + i]))
        stores.append(pltpu.make_async_copy(held_ref.at[part], out_ref.at[part], sems.at[4 + i]))
    load_cov.start()
    load_lab.start()
    for load in loads:
        load.start()
    for load, store in zip(loads, stores):
        load.wait()
        store.start()
    load_cov.wait()
    load_lab.wait()
    cov = cov_ref[...]
    heads_at = lax.broadcasted_iota(jnp.int32, (owners, blocks), 0)
    named = (cov[0:1] == heads_at).astype(f32)
    for t in range(1, per_block):
        named = named + (cov[t : t + 1] == heads_at).astype(f32)
    block_of = lax.broadcasted_iota(jnp.int32, (blocks, rows), 1) // rows_block
    block_at = lax.broadcasted_iota(jnp.int32, (blocks, rows), 0)
    same = (block_of == block_at).astype(bf16)
    before = (block_at < block_of).astype(bf16)
    rank = jnp.dot(named.astype(bf16), before, preferred_element_type=f32)
    cov_rows = jnp.dot(cov.astype(f32).astype(bf16), same, preferred_element_type=f32)
    row_in = lax.broadcasted_iota(jnp.int32, (rows_block, rows), 1) % rows_block
    row_at = lax.broadcasted_iota(jnp.int32, (rows_block, rows), 0)
    head_rows = lax.broadcasted_iota(jnp.int32, (owners, rows), 0).astype(f32)
    at_mark = lax.broadcasted_iota(jnp.int32, (16, rows), 0)
    mark_rows = jnp.zeros((16, rows), f32)
    for t in range(per_block):
        mine = cov_rows[t : t + 1]
        own_rank = jnp.sum(jnp.where(mine == head_rows, rank, 0.0), axis=0, keepdims=True)
        place = own_rank * rows_block + row_in[0:1].astype(f32)
        spread = jnp.dot(lab_ref[t].astype(f32).astype(bf16), same, preferred_element_type=f32)
        label = 1.0 + jnp.sum(jnp.where(row_in == row_at, spread, 0.0), axis=0, keepdims=True)
        mark_rows = jnp.where(at_mark == t, mine, mark_rows)
        mark_rows = jnp.where(at_mark == per_block + t, place, mark_rows)
        mark_rows = jnp.where(at_mark == 2 * per_block + t, label, mark_rows)
    held_ref[rows:, :] = jnp.zeros((16, held_ref.shape[1]), bf16)
    held_ref[rows:, 0:rows] = mark_rows.astype(bf16)
    last = pl.ds(rows, 16)
    stores.append(pltpu.make_async_copy(held_ref.at[last], out_ref.at[last], sems.at[6]))
    stores[-1].start()
    for store in stores:
        store.wait()


def make_shard(own, coverage, labels, owners):
    rows, feature = own.shape
    return pl.pallas_call(
        functools.partial(shard_kernel, owners),
        out_shape=sds((rows + 16, feature), bf16),
        in_specs=[HBM, HBM, HBM],
        out_specs=HBM,
        scratch_shapes=[
            pltpu.VMEM((coverage.shape[1], coverage.shape[0]), jnp.int32),
            pltpu.VMEM((labels.shape[1], labels.shape[2], labels.shape[0]), jnp.int32),
            pltpu.VMEM((rows + 16, feature), bf16),
            pltpu.SemaphoreType.DMA((7,)),
        ],
        compiler_params=params(ROOM),
        name="shard",
    )(coverage.T, labels.transpose(1, 2, 0), own)


def pick_rows(marks, shard, heads, unit, per_block):
    rows = marks.shape[1]
    slot = lax.broadcasted_iota(jnp.int32, (unit, rows), 0).astype(f32)
    at_head = lax.broadcasted_iota(jnp.int32, (8, rows), 0)
    chosen = []
    labels = jnp.zeros((8, rows), f32)
    for k, head in enumerate(heads):
        place = jnp.full((1, rows), -1.0, f32)
        label = jnp.zeros((1, rows), f32)
        for t in range(per_block):
            mine = marks[t : t + 1] == head
            place = jnp.where(mine, marks[per_block + t : per_block + t + 1], place)
            label = jnp.where(mine, marks[2 * per_block + t : 2 * per_block + t + 1], label)
        chosen.append(jnp.where(place == slot, 1.0, 0.0).astype(bf16))
        labels = jnp.where(at_head == k, label, labels)
    chosen = jnp.concatenate(chosen, axis=0)
    picked = jnp.dot(chosen, shard, preferred_element_type=f32).astype(bf16)
    mark = lax.dot_general(
        labels.astype(bf16), chosen, (((1,), (1,)), ((), ())), preferred_element_type=f32
    )
    return picked, mark


def pick_kernel(unit, per_block, plan, n_shards, n_heads, at_ref, *refs):
    shards, refs = refs[:n_shards], refs[n_shards:]
    outs, refs = refs[:n_heads], refs[n_heads:]
    held, ready, in_sems, out_sems = refs
    units = len(plan)
    rows = held.shape[1] - 16

    for g, (yes, no) in enumerate(plan):
        if yes == no:
            pltpu.make_async_copy(shards[yes], held.at[g], in_sems.at[g]).start()
        else:
            flag = at_ref[units * n_heads + g] > 0

            @pl.when(flag)
            def _():
                pltpu.make_async_copy(shards[yes], held.at[g], in_sems.at[g]).start()

            @pl.when(jnp.logical_not(flag))
            def _():
                pltpu.make_async_copy(shards[no], held.at[g], in_sems.at[g]).start()

    at_mark = lax.broadcasted_iota(jnp.int32, (16, unit), 0)
    mark_rows = [jnp.zeros((16, unit), f32)] * n_heads
    for g, (yes, _) in enumerate(plan):
        pltpu.make_async_copy(shards[yes], held.at[g], in_sems.at[g]).wait()
        marks = held[g, rows:, 0:rows].astype(f32)
        wanted = [at_ref[g * n_heads + k].astype(f32) for k in range(n_heads)]
        picked, mark = pick_rows(marks, held[g, 0:rows], wanted, unit, per_block)
        for k in range(n_heads):
            ready[k, g * unit : (g + 1) * unit, :] = picked[k * unit : (k + 1) * unit]
            own_mark = mark[k : k + 1, k * unit : (k + 1) * unit]
            mark_rows[k] = jnp.where(at_mark == g, own_mark, mark_rows[k])
    for k in range(n_heads):
        ready[k, units * unit :, :] = jnp.zeros((16, ready.shape[2]), bf16)
        ready[k, units * unit :, 0:unit] = mark_rows[k].astype(bf16)
        pltpu.make_async_copy(ready.at[k], outs[k], out_sems.at[k]).start()
    for k in range(n_heads):
        pltpu.make_async_copy(ready.at[k], outs[k], out_sems.at[k]).wait()


def pick(unit, per_block, shards, plan, heads_at, flags, cost):
    rows, feature = shards[0].shape
    units = len(plan)
    n_heads = len(heads_at) // units
    size = units * unit + 16
    return pl.pallas_call(
        functools.partial(pick_kernel, unit, per_block, plan, len(shards), n_heads),
        out_shape=[sds((size, feature), bf16)] * n_heads,
        in_specs=[SMEM] + [HBM] * len(shards),
        out_specs=[HBM] * n_heads,
        scratch_shapes=[
            pltpu.VMEM((units, rows, feature), bf16),
            pltpu.VMEM((n_heads, size, feature), bf16),
            pltpu.SemaphoreType.DMA((units,)),
            pltpu.SemaphoreType.DMA((n_heads,)),
        ],
        compiler_params=params(16),
        cost_estimate=spent(cost),
        name="pick",
    )(jnp.stack(heads_at + flags).astype(jnp.int32), *shards)


def pack_kernel(unit, n, *refs):
    parts, out_ref, mark_ref, all_ref, sems = refs[:n], *refs[n:]
    loads = []
    for k in range(n):
        loads.append(
            pltpu.make_async_copy(
                parts[k].at[pl.ds(0, unit)], out_ref.at[pl.ds(k * unit, unit)], sems.at[0, k]
            )
        )
        loads.append(
            pltpu.make_async_copy(
                parts[k].at[pl.ds(unit, 16)], mark_ref.at[k], sems.at[1, k]
            )
        )
    for load in loads:
        load.start()
    for load in loads:
        load.wait()
    at_mark = lax.broadcasted_iota(jnp.int32, (16, unit), 0)
    mark_rows = jnp.zeros((16, unit), f32)
    for k in range(n):
        marks = mark_ref[k, :, 0:unit].astype(f32)
        mark_rows = jnp.where(at_mark == k, marks[0:1], mark_rows)
    all_ref[...] = jnp.zeros(all_ref.shape, bf16)
    all_ref[:, 0:unit] = mark_rows.astype(bf16)
    store = pltpu.make_async_copy(all_ref, out_ref.at[pl.ds(n * unit, 16)], sems.at[0, n])
    store.start()
    store.wait()


def pack(unit, parts):
    feature = parts[0].shape[1]
    n = len(parts)
    return pl.pallas_call(
        functools.partial(pack_kernel, unit, n),
        out_shape=sds((n * unit + 16, feature), bf16),
        in_specs=[HBM] * n,
        out_specs=HBM,
        scratch_shapes=[
            pltpu.VMEM((n, 16, feature), bf16),
            pltpu.VMEM((16, feature), bf16),
            pltpu.SemaphoreType.DMA((2, n + 1)),
        ],
        compiler_params=params(8),
        name="pack",
    )(*parts)


def learn_kernel(unit, spots, n_parts, mode, with_total, half_rows, at_ref, *refs):
    parts, refs = refs[:n_parts], refs[n_parts:]
    w_ref, bias_ref, out_ref, refs = refs[0], refs[1], refs[2], refs[3:]
    if with_total:
        total_ref, vec_ref, refs = refs[0], refs[1], refs[2:]
    if mode == "rows":
        low_ref, new_vec_ref, refs = refs[0], refs[1], refs[2:]
        rows_ref, mark_ref, target_ref, sems = refs
    elif mode == "halves":
        kept_ref, given_ref, new_vec_ref, refs = refs[0], refs[1], refs[2], refs[3:]
        rows_ref, low_ref, mark_ref, target_ref, sems = refs
    else:
        new_total_ref, new_vec_ref, refs = refs[0], refs[1], refs[2:]
        rows_ref, low_ref, mark_ref, target_ref, sems = refs
    rows_all, feature = rows_ref.shape
    loads = []
    for i in range(n_parts):
        loads.append(
            pltpu.make_async_copy(
                parts[i].at[pl.ds(parts[i].shape[0] - 16, 16)], mark_ref.at[i], sems.at[0, i]
            )
        )
    for u, (part, at, _) in enumerate(spots):
        loads.append(
            pltpu.make_async_copy(
                parts[part].at[pl.ds(at, unit)],
                rows_ref.at[pl.ds(u * unit, unit)],
                sems.at[1, u],
            )
        )
    for load in loads:
        load.start()
    for load in loads:
        load.wait()
    eye = lax.broadcasted_iota(jnp.int32, (unit, unit), 0) == lax.broadcasted_iota(
        jnp.int32, (unit, unit), 1
    )
    for u, (part, _, mark_at) in enumerate(spots):
        marks = mark_ref[part, :, 0:unit].astype(f32)[mark_at : mark_at + 1]
        target_ref[u * unit : (u + 1) * unit, :] = jnp.sum(
            jnp.where(eye, marks, 0.0), axis=1, keepdims=True
        ) * at_ref[1].astype(f32)
    bias = bias_ref[...].astype(f32)
    out_weight = out_ref[...].astype(f32)
    step = 2 * unit
    hid = w_ref.shape[1]

    def forward(i, carry):
        span = pl.ds(pl.multiple_of(i * step, step), step)
        pre = jnp.dot(rows_ref[span, :], w_ref[...], preferred_element_type=f32) + bias
        gate = half_sigmoid(pre)
        hidden = pre * gate
        logit = jnp.sum(hidden * out_weight, axis=1, keepdims=True)
        mark = target_ref[span, :]
        residual = jnp.where(mark > 0.5, half_sigmoid(logit) - (mark - 1.0), 0.0)
        grad_pre = residual * out_weight * gate * (1.0 + pre * (1.0 - gate))
        low_ref[span, :] = grad_pre.astype(bf16)
        return (
            carry[0] + jnp.sum(grad_pre, axis=0, keepdims=True),
            carry[1] + jnp.sum(residual * hidden, axis=0, keepdims=True),
        )

    if with_total:
        start = (vec_ref[0:1, :], vec_ref[1:2, :])
    else:
        start = (jnp.zeros((1, hid), f32), jnp.zeros((1, hid), f32))
    grad_bias, grad_out = lax.fori_loop(0, rows_all // step, forward, start, unroll=True)

    def product(first, size):
        piece = lax.dot_general(
            rows_ref[:, first : first + size],
            low_ref[...],
            (((0,), (0,)), ((), ())),
            preferred_element_type=f32,
        )
        if with_total:
            piece = piece + total_ref[first : first + size, :]
        return piece

    new_vec_ref[...] = jnp.zeros(new_vec_ref.shape, f32)
    new_vec_ref[0:1, :] = grad_bias
    new_vec_ref[1:2, :] = grad_out
    if mode == "rows":
        return
    tile = 128 * max(n for n in range(1, 5) if feature % (128 * n) == 0)
    if mode == "total":
        for first in range(0, feature, tile):
            new_total_ref[first : first + tile, :] = product(first, tile)
        return
    given_ref[half_rows:, :] = new_vec_ref[...]
    for first in range(0, feature, tile):
        piece = product(first, tile)
        cut = min(max(half_rows - first, 0), tile)
        for core in range(2):
            low_half, high_half = (kept_ref, given_ref) if core == 0 else (given_ref, kept_ref)

            @pl.when(at_ref[0] == core)
            def _():
                if cut > 0:
                    low_half[first : first + cut, :] = piece[:cut]
                if cut < tile:
                    high_half[first + cut - half_rows : first + tile - half_rows, :] = piece[cut:]


def keep_kernel(half_rows, low_cut, unit, spots, n_parts, at_ref, *refs):
    parts, (low_ref, kept_ref, out_ref, rows_ref, wide_ref, sems) = refs[:n_parts], refs[n_parts:]
    feature = rows_ref.shape[1]
    loads = []
    for u, (part, at, _) in enumerate(spots):
        loads.append(
            pltpu.make_async_copy(
                parts[part].at[pl.ds(at, unit)], rows_ref.at[pl.ds(u * unit, unit)], sems.at[u]
            )
        )
    for load in loads:
        load.start()
    for load in loads:
        load.wait()
    first = pl.multiple_of(at_ref[0] * low_cut, 128)
    skip = pl.multiple_of(at_ref[0] * (half_rows - low_cut), 8)
    wide_ref[...] = lax.dot_general(
        rows_ref[:, pl.ds(first, feature - low_cut)],
        low_ref[...],
        (((0,), (0,)), ((), ())),
        preferred_element_type=f32,
    )
    out_ref[...] = wide_ref[pl.ds(skip, half_rows), :] + kept_ref[...]


def keep(unit, spots, parts, at, low, kept):
    feature = parts[0].shape[1]
    half, hid = kept.shape
    low_cut = half // 128 * 128
    return pl.pallas_call(
        functools.partial(keep_kernel, half, low_cut, unit, spots, len(parts)),
        out_shape=sds((half, hid), f32),
        in_specs=[SMEM] + [HBM] * len(parts) + [VMEM, VMEM],
        out_specs=VMEM,
        scratch_shapes=[
            pltpu.VMEM((low.shape[0], feature), bf16),
            pltpu.VMEM((feature - low_cut, hid), f32),
            pltpu.SemaphoreType.DMA((len(spots),)),
        ],
        compiler_params=params(16),
        cost_estimate=spent(2),
        name="keep",
    )(at, *parts, low, kept)


def learn(unit, spots, parts, at, w, bias, out, total, cost, mode):
    feature, hid = w.shape
    rows_all = len(spots) * unit
    half = feature // 2
    work = (pltpu.VMEM((rows_all, hid), bf16),)
    if mode == "rows":
        outs, work = (sds((rows_all, hid), bf16), sds((8, hid), f32)), ()
    elif mode == "halves":
        outs = (sds((half, hid), f32), sds((half + 8, hid), f32), sds((8, hid), f32))
    else:
        outs = (sds((feature, hid), f32), sds((8, hid), f32))
    extra = () if total is None else total
    kernel = functools.partial(
        learn_kernel, unit, spots, len(parts), mode, total is not None, half
    )
    return pl.pallas_call(
        kernel,
        out_shape=outs,
        in_specs=[SMEM] + [HBM] * len(parts) + [VMEM] * (3 + len(extra)),
        out_specs=(VMEM,) * len(outs),
        scratch_shapes=[
            pltpu.VMEM((rows_all, feature), bf16),
            *work,
            pltpu.VMEM((len(parts), 16, feature), bf16),
            pltpu.VMEM((rows_all, 1), f32),
            pltpu.SemaphoreType.DMA((2, max(len(parts), len(spots)))),
        ],
        compiler_params=params(24),
        cost_estimate=spent(cost),
        name="learn",
    )(at, *parts, w, bias, out, *extra)


def adam(old, grad, first, second):
    new_first = beta_one * first + (1.0 - beta_one) * grad
    new_second = beta_two * second + (1.0 - beta_two) * grad * grad
    new = old - learn_rate * new_first / (jnp.sqrt(new_second) + epsilon)
    return new.astype(bf16), new_first, new_second


def weights_kernel(
    low_cut, n_tiles, at_ref, rows_ref, low_ref, kept, got, w, first_w, second_w, new_half, grad_ref, wide_ref
):
    half = kept.shape[0]
    first = pl.multiple_of(at_ref[0] * low_cut, 128)
    skip = pl.multiple_of(at_ref[0] * (half - low_cut), 8)
    own = pl.multiple_of(at_ref[0] * half, 16)
    wide_ref[...] = lax.dot_general(
        rows_ref[0 : low_ref.shape[0], pl.ds(first, rows_ref.shape[1] - low_cut)],
        low_ref[...],
        (((0,), (0,)), ((), ())),
        preferred_element_type=f32,
    )
    tile = half // n_tiles
    for i in range(n_tiles):
        span = pl.ds(i * tile, tile)
        there = pl.ds(pl.multiple_of(own + i * tile, 16), tile)
        there_wide = pl.ds(pl.multiple_of(skip + i * tile, 8), tile)
        grad = kept[span, :] + got[span, :] + wide_ref[there_wide, :]
        new, _, _ = adam(w[there, :].astype(f32), grad, first_w[0, span, :], second_w[0, span, :])
        new_half[span, :] = new
        grad_ref[span, :] = grad


def moments_kernel(
    at_ref, grad_ref, vec_near, vec_far, vec_other, got_vec, half_rows, first_w, second_w, bias, out,
    first_vec, second_vec,
    new_full, new_vec, new_first_w, new_second_w, new_first_vec, new_second_vec,
):
    grad = grad_ref[...]
    new_full[0] = half_rows[...]
    new_first_w[0] = beta_one * first_w[0] + (1.0 - beta_one) * grad
    new_second_w[0] = beta_two * second_w[0] + (1.0 - beta_two) * grad * grad

    @pl.when(pl.program_id(0) == 0)
    def _():
        vec = (vec_near[0:2, :] + vec_far[0:2, :]) + (got_vec[0:2, :] + vec_other[0:2, :])
        for row, old in enumerate((bias, out)):
            fresh, fresh_first, fresh_second = adam(
                old[...].astype(f32),
                vec[row : row + 1],
                first_vec[0, row : row + 1],
                second_vec[0, row : row + 1],
            )
            new_vec[0, row : row + 1] = fresh
            new_first_vec[0, row : row + 1] = fresh_first
            new_second_vec[0, row : row + 1] = fresh_second


def take_step(
    rep, rows, low, kept, got, vecs, w_in, bias, out, first_w, second_w, first_vec, second_vec
):
    feature, hid = w_in.shape
    half = feature // 2
    low_cut = half // 128 * 128
    tiles = max(n for n in range(1, 3) if half % (16 * n) == 0)
    tile = half // tiles
    here = pl.BlockSpec((tile, hid), lambda i, at: (i, 0))
    tail = pl.BlockSpec((8, hid), lambda i, at: (half // 8, 0))
    top = pl.BlockSpec((8, hid), lambda i, at: (0, 0))
    moment = pl.BlockSpec((1, tile, hid), lambda i, at: (0, i, 0))
    row = pl.BlockSpec((1, hid), lambda i, at: (0, 0))
    pairs = pl.BlockSpec((1, 2, hid), lambda i, at: (0, 0, 0))
    full = pl.BlockSpec((1, tile, hid), lambda i, at: (0, at[0] * tiles + i, 0))
    new_half, grad = pl.pallas_call(
        functools.partial(weights_kernel, low_cut, 1),
        in_specs=[SMEM] + [VMEM] * 7,
        out_specs=[VMEM, VMEM],
        out_shape=(sds((half, hid), bf16), sds((half, hid), f32)),
        scratch_shapes=[pltpu.VMEM((feature - low_cut, hid), f32)],
        compiler_params=params(16),
        cost_estimate=spent(2),
        name="weights",
    )(rep, rows, low, kept, got, w_in, first_w, second_w)
    other = lax.ppermute(new_half, "rep", swap)
    new_full, *rest = pl.pallas_call(
        moments_kernel,
        grid_spec=pltpu.PrefetchScalarGridSpec(
            num_scalar_prefetch=1,
            grid=(tiles,),
            in_specs=[here, top, top, top, tail, here, moment, moment, row, row, pairs, pairs],
            out_specs=[full, pairs, moment, moment, pairs, pairs],
        ),
        out_shape=(
            sds((1, feature, hid), bf16),
            sds((1, 2, hid), bf16),
            sds((1, half, hid), f32),
            sds((1, half, hid), f32),
            sds((1, 2, hid), f32),
            sds((1, 2, hid), f32),
        ),
        compiler_params=params(16),
        cost_estimate=spent(3),
        name="moments",
    )(rep, grad, *vecs, got, new_half, first_w, second_w, bias, out, first_vec, second_vec)
    return join(rep, other, new_full), *rest


def join_kernel(at_ref, other_ref, full_ref, out_ref, sem):
    half = other_ref.shape[0]
    start = pl.multiple_of((1 - at_ref[0]) * half, half)
    load = pltpu.make_async_copy(other_ref, out_ref.at[0, pl.ds(start, half)], sem)
    load.start()
    load.wait()


def join(rep, other, full):
    return pl.pallas_call(
        join_kernel,
        out_shape=sds(full.shape, full.dtype),
        in_specs=[SMEM, ANY, ANY],
        out_specs=ANY,
        scratch_shapes=[pltpu.SemaphoreType.DMA(())],
        input_output_aliases={2: 0},
        compiler_params=params(8),
        name="join",
    )(rep, other, full)


def gathered(
    embeddings, coverage, labels, w_in, bias_in, w_out, first_w, second_w, first_vec, second_vec
):
    planes = lax.axis_size("dp")
    heads = lax.axis_size("head")
    owners = planes * heads
    z = lax.axis_index("dp")
    q = lax.axis_index("head")
    rep = lax.axis_index("rep").reshape(1)
    blocks, rows_block, feature = embeddings.shape
    per_block = coverage.shape[1]
    slots = 2 * blocks * per_block // owners
    unit = slots * rows_block
    rows = blocks * rows_block
    outer_pairs = [(i, i ^ 1) for i in range(planes)]
    inner_pairs = [(i, i + 1 if i % 2 else i - 1) for i in range(1, planes - 1)]
    out_pairs = [(i, i ^ 1) for i in range(1, planes - 1)]
    end_pairs = [(0, planes - 1), (planes - 1, 0)]

    def exchange(units):
        return [units[0]] + [
            lax.ppermute(units[k], "head", [(i, i ^ k) for i in range(heads)])
            for k in range(1, heads)
        ]

    def plane_heads(plane, real=None):
        found = [plane * heads + (q ^ k) for k in range(heads)]
        return found if real is None else [jnp.where(real, h, -1) for h in found]

    own = make_shard(embeddings.reshape(rows, feature), coverage, labels, owners)
    inner = lax.ppermute(own, "dp", inner_pairs)
    outer = lax.ppermute(own, "dp", outer_pairs)
    always = jnp.ones((), jnp.bool_)
    at_end = (z == 0) | (z == planes - 1)

    def add(total, parts, spots, real, cost, mode="total"):
        scalars = jnp.stack([rep[0], real]).astype(jnp.int32)
        return learn(unit, spots, parts, scalars, w_in[0], bias_in, w_out, total, cost, mode)

    first_heads = plane_heads(jnp.where(at_end, planes - 1 - z, z))
    first_units = exchange(pick(unit, per_block, [own], [(0, 0)], first_heads, [always], 0))
    far_sent = pack(unit, first_units)
    one = jnp.ones((), jnp.int32)
    first_spots = [(k, 0, 0) for k in range(heads)]
    middle = 1 - at_end.astype(jnp.int32)
    inner, far_sent = lax.optimization_barrier((inner, far_sent))
    next_out = lax.ppermute(inner, "dp", out_pairs)
    next_in = lax.ppermute(outer, "dp", inner_pairs)
    messages = pick(
        unit, per_block, [outer, inner, own], [(0, 0), (1, 2)], plane_heads(z) * 2,
        [always, jnp.logical_not(at_end)], PB,
    )
    first_units = lax.optimization_barrier((*first_units, *messages))[:heads]
    total = add(None, first_units, first_spots, middle, LA)
    near = exchange(messages)
    far_sent, next_out, next_in, *total = lax.optimization_barrier(
        (far_sent, next_out, next_in, *total)
    )
    far_got = lax.ppermute(far_sent, "dp", end_pairs)
    messages = pick(
        unit, per_block, [next_in, next_out], [(0, 1)], plane_heads(z),
        [jnp.logical_not(at_end)], PC,
    )
    messages = lax.optimization_barrier((*messages, *near))[:heads]
    rest = [
        (near, [(k, g * unit, g) for k in range(heads) for g in range(2)]),
        (exchange(messages), [(k, 0, 0) for k in range(heads)]),
    ]
    for at, (parts, spots) in enumerate(rest):
        last = at == len(rest) - 1
        total = add(total, parts, spots, one, (LB, LC)[min(at, 1)], "halves" if last else "total")
    kept, given, vec_near = total
    got = lax.ppermute(given, "rep", swap)
    far_other = lax.ppermute(far_got, "rep", swap)
    spots = [(0, k * unit, k) for k in range(heads)]
    low, vec_far = add(None, [far_got], spots, one, LF, "rows")
    low_other = lax.ppermute(low, "rep", swap)
    vec_other = lax.ppermute(vec_far, "rep", swap)
    low_other, vec_other = lax.optimization_barrier((low_other, vec_other))
    kept = keep(unit, spots, [far_got], rep, low, kept)
    return take_step(
        rep, far_other, low_other, kept, got, [vec_near, vec_far, vec_other], w_in[0], bias_in, w_out,
        first_w, second_w, first_vec, second_vec,
    )


def routed(
    embeddings, coverage, labels, w_in, bias_in, w_out, first_w, second_w, first_vec, second_vec
):
    dp_count = lax.axis_size("dp")
    head_count = lax.axis_size("head")
    owners = dp_count * head_count
    block_count, rows_block, feature = embeddings.shape
    per_block = coverage.shape[1]
    slot_count = 2 * block_count * per_block // owners
    entries = block_count * per_block
    heads_flat = coverage.reshape(entries)
    onehot = (heads_flat[:, None] == jnp.arange(owners, dtype=jnp.int32)[None, :]).astype(jnp.int32)
    slot_rank = jnp.sum((jnp.cumsum(onehot, axis=0) - 1) * onehot, axis=1)
    target_slot = heads_flat * slot_count + slot_rank
    picker = jnp.arange(owners * slot_count, dtype=jnp.int32)[:, None] == target_slot[None, :]
    block_pick = jnp.sum(
        picker.reshape(owners * slot_count, block_count, per_block).astype(jnp.int32), axis=2
    ).astype(jnp.bfloat16)
    send_rows = jnp.dot(
        block_pick,
        embeddings.reshape(block_count, rows_block * feature),
        preferred_element_type=jnp.float32,
    ).astype(jnp.bfloat16)
    label_marks = (labels.reshape(entries, rows_block) + 1).astype(jnp.float32)
    send_marks = jnp.dot(
        picker.astype(jnp.float32), label_marks, precision=lax.Precision.HIGHEST
    ).astype(jnp.bfloat16)
    direct_rows = send_rows.reshape(owners, slot_count, rows_block, feature)
    direct_marks = send_marks.reshape(owners, slot_count, rows_block)
    got_rows, got_marks = (
        lax.all_to_all(direct_rows, ("dp", "head"), split_axis=0, concat_axis=0, tiled=True),
        lax.all_to_all(direct_marks, ("dp", "head"), split_axis=0, concat_axis=0, tiled=True),
    )
    row_data = got_rows.reshape(-1, feature)
    marks_all = got_marks.reshape(-1).astype(jnp.float32)
    usable = marks_all > 0.5
    target = marks_all - 1.0
    out_weight = w_out[0].astype(jnp.float32)
    pre_act = (
        jnp.dot(row_data, w_in[0], preferred_element_type=jnp.float32)
        + bias_in[0].astype(jnp.float32)[None, :]
    )
    sig_pre = jax.nn.sigmoid(pre_act)
    hidden = pre_act * sig_pre
    logits = jnp.sum(hidden * out_weight[None, :], axis=1)
    residual = jnp.where(usable, jax.nn.sigmoid(logits) - target, jnp.zeros_like(logits))
    grad_pre = residual[:, None] * out_weight[None, :] * sig_pre * (1.0 + pre_act * (1.0 - sig_pre))
    grad_low = grad_pre.astype(jnp.bfloat16)
    vec_part = jnp.stack([jnp.sum(grad_pre, axis=0), jnp.sum(residual[:, None] * hidden, axis=0)])
    half_rows = feature // lax.axis_size("rep")
    rep_at = lax.axis_index("rep")
    first_row = rep_at * half_rows
    grad_part = lax.dot_general(
        row_data, grad_low, (((0,), (0,)), ((), ())), preferred_element_type=jnp.float32
    ).reshape(2, half_rows, -1)
    kept = jnp.where(rep_at == 0, grad_part[0], grad_part[1])
    given = jnp.where(rep_at == 0, grad_part[1], grad_part[0])
    grad_w = kept + lax.ppermute(given, "rep", swap)
    grad_vec = vec_part + lax.ppermute(vec_part, "rep", swap)
    new_first_w = beta_one * first_w[0] + (1.0 - beta_one) * grad_w
    new_second_w = beta_two * second_w[0] + (1.0 - beta_two) * grad_w * grad_w
    old_rows = lax.dynamic_slice_in_dim(w_in[0], first_row, half_rows, 0).astype(jnp.float32)
    new_half = (old_rows - learn_rate * new_first_w / (jnp.sqrt(new_second_w) + epsilon)).astype(
        jnp.bfloat16
    )
    other_half = lax.ppermute(new_half, "rep", swap)
    new_w_in = jnp.where(
        rep_at == 0,
        jnp.concatenate([new_half, other_half]),
        jnp.concatenate([other_half, new_half]),
    )
    vector = jnp.stack([bias_in[0], w_out[0]]).astype(jnp.float32)
    new_first_vec = beta_one * first_vec[0] + (1.0 - beta_one) * grad_vec
    new_second_vec = beta_two * second_vec[0] + (1.0 - beta_two) * grad_vec * grad_vec
    new_vec = (vector - learn_rate * new_first_vec / (jnp.sqrt(new_second_vec) + epsilon)).astype(
        jnp.bfloat16
    )
    return (
        new_w_in[None],
        new_vec[None],
        new_first_w[None],
        new_second_w[None],
        new_first_vec[None],
        new_second_vec[None],
    )


def solution(mesh):
    placed = (
        P(("dp", "head", "rep"), None, None),
        P(("dp", "head", "rep"), None),
        P(("dp", "head", "rep"), None, None),
        P(("dp", "head"), None, None),
        P(("dp", "head"), None),
        P(("dp", "head"), None),
        P(("dp", "head"), "rep", None),
        P(("dp", "head"), "rep", None),
        P(("dp", "head"), None, None),
        P(("dp", "head"), None, None),
    )
    planes, heads, reps = mesh.shape["dp"], mesh.shape["head"], mesh.shape["rep"]
    short = planes == 4 and heads & (heads - 1) == 0 and reps == 2
    return jax.shard_map(
        gathered if short else routed,
        mesh=mesh,
        in_specs=placed,
        out_specs=(
            P(("dp", "head"), None, None),
            P(("dp", "head"), None, None),
            P(("dp", "head"), "rep", None),
            P(("dp", "head"), "rep", None),
            P(("dp", "head"), None, None),
            P(("dp", "head"), None, None),
        ),
        check_vma=False,
    )
```
